512 devices in a mesh: space: 8 (over z), vel: 64 (over x, y, core).
Axes of the slice: x: 4, y: 8, z: 8, core: 2. Of those that a mesh axis runs over, the one named last changes fastest.
Arguments:
- distribution: float32 [32768, 2048], P('vel', 'space'), may hold values from 0.1 to 32, as said below
- normals: float32 [4, 3, 2048], P(None, None, 'space'), may hold values from -0.3 to 0.3
- adjacency: int32 [4, 2048], P(None, 'space'), may hold values from 0 to 2047, as said below
- send_list: int32 [8, 8, 256], P('space'), may hold values from 0 to 255
- block_counts: int32 [8, 8], P(None, 'space'), may hold values from 0 to 2, as said below
Outputs:
- relaxed: float32 [32768, 2048], P('vel', 'space')
- fields: float32 [13, 2048], P(None, 'space')
The draws below stay inside these ranges and needn't reach their ends.
Inputs may be any that keep to these rules, and one draw needn't show every extreme that they name: `adjacency`: every entry of 256 or more names a position below 128 times the sum of block_counts over the senders to its group. `block_counts`: no group sends to itself; every other pair has at least one block; one receiving group gets 2 blocks from every other group. `distribution`: Positive.
All inputs are finite; a program needn't handle non-finite values.
Results may differ from the reference program's by a relative error of at most 0.00011.
Values sent between devices are 32-bit elements; how exact they have to be, the bound alone decides.
No kernel may reach another device: no remote copies, remote signals or barrier semaphores. Data moves between devices by JAX's collectives and lax.ppermute only.
A program may use at most 64 MiB of HBM per device.

```python
import math
import jax
import jax.numpy as jnp
from jax import lax

VXY = 32
C_DEV = 256
FACES = 4
TILE = 128
MAXB = 2
BND = 256
ITERS = 2
V = 32768
VZN = 32
CELLS = 2048
SLOTS = 256
N_SPACE = 8


def counts_core(key):
    key_one, key_three = jax.random.split(jax.random.fold_in(key, 11), 2)
    counts = jax.random.randint(key_one, (N_SPACE, N_SPACE), 1, MAXB + 1)
    full_group = jax.random.randint(key_three, (), 0, N_SPACE)
    row_ids = jnp.arange(N_SPACE)[:, None]
    col_ids = jnp.arange(N_SPACE)[None, :]
    counts = jnp.where(col_ids == full_group, MAXB, counts)
    return (jnp.where(row_ids == col_ids, 0, counts).astype(jnp.int32), full_group)


def draw_block_counts(key, part):
    counts, full_group = counts_core(key)
    return counts


def draw_adjacency(key, part):
    counts, full_group = counts_core(key)
    packed_total = jnp.sum(counts, axis=0) * TILE
    key_a, key_b, key_c = jax.random.split(jax.random.fold_in(key, 23), 3)
    group_of = jnp.arange(C_DEV * N_SPACE) // C_DEV
    limit = packed_total[group_of]
    local_pick = jax.random.randint(key_a, (FACES, C_DEV * N_SPACE), 0, C_DEV)
    ghost_pick = jax.random.randint(key_b, (FACES, C_DEV * N_SPACE), 0, 1 << 20) % limit[None, :]
    remote = jax.random.randint(key_c, (FACES, C_DEV * N_SPACE), 0, 8) == 0
    result = jnp.where(remote, C_DEV + ghost_pick, local_pick)
    first_cell = full_group * C_DEV
    face_ids = jnp.arange(FACES)[:, None]
    cell_ids = jnp.arange(C_DEV * N_SPACE)[None, :]
    top_value = C_DEV + (N_SPACE - 1) * SLOTS - 1
    result = jnp.where((face_ids == 0) & (cell_ids == first_cell), top_value, result)
    result = jnp.where((face_ids == 1) & (cell_ids == first_cell), 0, result)
    return result.astype(jnp.int32)


def draw_distribution(key, part):
    level = (jnp.arange(V) // (VXY * VXY)).astype(jnp.float32)
    comp_z = (level - (VZN - 1) / 2.0) * 0.3
    z_span = max(VZN - 1, 1) * 0.3
    key_one = jax.random.fold_in(key, 0)
    rough = jnp.exp(jax.random.uniform(key_one, (V, C_DEV * N_SPACE), jnp.float32, math.log(0.3), math.log(3.0)))
    tilt = math.log(5.0) / z_span
    return (rough * jnp.exp(tilt * comp_z)[:, None]).astype(jnp.float32)


def plant(values, own_key, smallest, largest):
    longest = values.shape.index(max(values.shape))
    spots = []
    for shift in (0, 1):
        where = [jax.random.randint(jax.random.fold_in(own_key, axis), (), 0, length) for axis, length in enumerate(values.shape)]
        where[longest] = (where[longest] + shift) % values.shape[longest]
        spots.append(tuple(where))
    return values.at[spots[0]].set(smallest).at[spots[1]].set(largest)


def block_levels(own_key, shape, cuts, least, largest):
    def one(dim, shards_of):
        heights = jax.random.uniform(jax.random.fold_in(jax.random.fold_in(own_key, 6), dim), (shards_of,), jnp.float32, least / len(cuts), largest / len(cuts))
        return jnp.repeat(jnp.exp(heights), shape[dim] // shards_of).reshape((-1,) + (1,) * (len(shape) - dim - 1))

    factor_of = one(*cuts[0])
    for cut in cuts[1:]:
        factor_of = factor_of * one(*cut)
    return factor_of


def setup_inputs(seed: int = 0) -> dict:
    key_list = jax.random.split(jax.random.key(seed), 6)
    distribution = draw_distribution(jax.random.fold_in(key_list[5], 71), 0)
    normals = jnp.clip(jax.random.uniform(key_list[1], (FACES, 3, CELLS), jnp.float32, -0.3, 0.3) * block_levels(key_list[1], (FACES, 3, CELLS), ((2, 8),), -0.4, 0.0), -0.3, 0.3)
    adjacency = draw_adjacency(jax.random.fold_in(key_list[5], 71), 0)
    send_list = plant(jax.random.randint(key_list[3], (N_SPACE, N_SPACE, SLOTS), 0, BND), jax.random.fold_in(key_list[3], 1), 0, BND - 1).astype(jnp.int32)
    block_counts = draw_block_counts(jax.random.fold_in(key_list[5], 71), 0)
    return {"distribution": distribution, "normals": normals, "adjacency": adjacency, "send_list": send_list, "block_counts": block_counts}


spacing = 0.3
ellipsoid_mix = -0.25
prandtl = 0.8
visc_power = 0.26
time_step = 0.025


def velocity_nodes(vel_index, z_count):
    comp_x = (vel_index % VXY).astype(jnp.float32)
    comp_y = ((vel_index // VXY) % VXY).astype(jnp.float32)
    comp_z = (vel_index // (VXY * VXY)).astype(jnp.float32)
    centre = (VXY - 1) / 2.0
    return jnp.stack([(comp_x - centre) * spacing, (comp_y - centre) * spacing, (comp_z - (z_count - 1) / 2.0) * spacing])


def moment_rows(velocity):
    comp_x, comp_y, comp_z = velocity[0], velocity[1], velocity[2]
    squared = comp_x * comp_x + comp_y * comp_y + comp_z * comp_z
    return jnp.stack([jnp.ones_like(comp_x), comp_x, comp_y, comp_z, comp_x * comp_x, comp_y * comp_y, comp_z * comp_z, comp_x * comp_y, comp_x * comp_z, comp_y * comp_z, comp_x * squared, comp_y * squared, comp_z * squared])


def quad_rows(velocity):
    comp_x, comp_y, comp_z = velocity[0], velocity[1], velocity[2]
    return jnp.stack([comp_x * comp_x, comp_y * comp_y, comp_z * comp_z, comp_x * comp_y, comp_x * comp_z, comp_y * comp_z, comp_x, comp_y, comp_z, jnp.ones_like(comp_x)])


def macroscopic(moments):
    density = moments[0]
    mean_x = moments[1] / density
    mean_y = moments[2] / density
    mean_z = moments[3] / density
    second = moments[4:10] / density[None, :]
    third = moments[10:13] / density[None, :]
    theta_xx = second[0] - mean_x * mean_x
    theta_yy = second[1] - mean_y * mean_y
    theta_zz = second[2] - mean_z * mean_z
    theta_xy = second[3] - mean_x * mean_y
    theta_xz = second[4] - mean_x * mean_z
    theta_yz = second[5] - mean_y * mean_z
    temper = (theta_xx + theta_yy + theta_zz) / 3.0
    trace_b = second[0] + second[1] + second[2]
    bu_x = second[0] * mean_x + second[3] * mean_y + second[4] * mean_z
    bu_y = second[3] * mean_x + second[1] * mean_y + second[5] * mean_z
    bu_z = second[4] * mean_x + second[5] * mean_y + second[2] * mean_z
    mean_sq = mean_x * mean_x + mean_y * mean_y + mean_z * mean_z
    flux_x = 0.5 * (third[0] - 2.0 * bu_x - mean_x * trace_b + 2.0 * mean_x * mean_sq)
    flux_y = 0.5 * (third[1] - 2.0 * bu_y - mean_y * trace_b + 2.0 * mean_y * mean_sq)
    flux_z = 0.5 * (third[2] - 2.0 * bu_z - mean_z * trace_b + 2.0 * mean_z * mean_sq)
    iso_part = (1.0 - ellipsoid_mix) * temper
    lam_xx = iso_part + ellipsoid_mix * theta_xx
    lam_yy = iso_part + ellipsoid_mix * theta_yy
    lam_zz = iso_part + ellipsoid_mix * theta_zz
    lam_xy = ellipsoid_mix * theta_xy
    lam_xz = ellipsoid_mix * theta_xz
    lam_yz = ellipsoid_mix * theta_yz
    cof_xx = lam_yy * lam_zz - lam_yz * lam_yz
    cof_xy = lam_yz * lam_xz - lam_xy * lam_zz
    cof_xz = lam_xy * lam_yz - lam_yy * lam_xz
    cof_yy = lam_xx * lam_zz - lam_xz * lam_xz
    cof_yz = lam_xy * lam_xz - lam_xx * lam_yz
    cof_zz = lam_xx * lam_yy - lam_xy * lam_xy
    determinant = lam_xx * cof_xx + lam_xy * cof_xy + lam_xz * cof_xz
    inv_xx = cof_xx / determinant
    inv_yy = cof_yy / determinant
    inv_zz = cof_zz / determinant
    inv_xy = cof_xy / determinant
    inv_xz = cof_xz / determinant
    inv_yz = cof_yz / determinant
    lin_x = inv_xx * mean_x + inv_xy * mean_y + inv_xz * mean_z
    lin_y = inv_xy * mean_x + inv_yy * mean_y + inv_yz * mean_z
    lin_z = inv_xz * mean_x + inv_yz * mean_y + inv_zz * mean_z
    offset = mean_x * lin_x + mean_y * lin_y + mean_z * lin_z
    collide = prandtl * density * jnp.exp(visc_power * jnp.log(temper))
    return jnp.stack([density, mean_x, mean_y, mean_z, theta_xx, theta_yy, theta_zz, theta_xy, theta_xz, theta_yz, flux_x, flux_y, flux_z,
                      inv_xx, inv_yy, inv_zz, 2.0 * inv_xy, 2.0 * inv_xz, 2.0 * inv_yz, -2.0 * lin_x, -2.0 * lin_y, -2.0 * lin_z, offset, collide])


def ghost_slots(adjacency, counts, cells, groups, slot_count):
    ends = (jnp.cumsum(counts) * TILE).astype(jnp.int32)
    starts = (ends - counts * TILE).astype(jnp.int32)
    is_local = adjacency < cells
    position = jnp.maximum(adjacency - cells, 0)
    source = jnp.sum((ends[:, None, None] <= position[None]).astype(jnp.int32), axis=0).astype(jnp.int32)
    source = jnp.minimum(source, groups - 1)
    group_ids = jnp.arange(groups, dtype=jnp.int32)[:, None, None]
    chosen = jnp.sum(jnp.where(group_ids == source[None], starts[:, None, None], 0), axis=0).astype(jnp.int32)
    slot_pos = jnp.clip(position - chosen, 0, slot_count - 1).astype(jnp.int32)
    return is_local, source, slot_pos


def relax(current, neighbours, velocity, normals, params, norm_z, equilibrium):
    gauss = params[0][None, :] * equilibrium / norm_z[None, :]
    outflow = jnp.zeros(current.shape, jnp.float32)
    inflow = jnp.zeros(current.shape, jnp.float32)
    for side in range(normals.shape[0]):
        normal_speed = (velocity[0][:, None] * normals[side, 0][None, :] + velocity[1][:, None] * normals[side, 1][None, :]
                        + velocity[2][:, None] * normals[side, 2][None, :])
        outflow = outflow + jnp.maximum(normal_speed, 0.0)
        inflow = inflow + jnp.minimum(normal_speed, 0.0) * neighbours[side]
    return current + time_step * (params[23][None, :] * (gauss - current) - outflow * current - inflow)


def reference(distribution, normals, adjacency, send_list, block_counts):
    pieces = []
    for group in range(N_SPACE):
        local_adj = adjacency[:, group * C_DEV:(group + 1) * C_DEV]
        is_local, source, slot_pos = ghost_slots(local_adj, block_counts[:, group], C_DEV, N_SPACE, SLOTS)
        listed = send_list[:, group, :]
        remote = source * C_DEV + listed[source, slot_pos]
        pieces.append(jnp.where(is_local, group * C_DEV + local_adj, remote).astype(jnp.int32))
    neighbour_index = jnp.concatenate(pieces, axis=1)
    level_count = V // (VXY * VXY)
    block_rows = VXY * VXY
    velocity = velocity_nodes(jnp.arange(V, dtype=jnp.int32), level_count)
    moment_table = moment_rows(velocity)
    quad_table = quad_rows(velocity).T
    vel_blocks = velocity.reshape(3, level_count, block_rows).transpose(1, 0, 2)
    quad_blocks = quad_table.reshape(level_count, block_rows, 10)

    def reduce_moments(current):
        partial_value = jnp.dot(moment_table, current, precision=lax.Precision.HIGHEST, preferred_element_type=jnp.float32)
        return macroscopic(partial_value / V)

    current = distribution
    for iteration in range(ITERS):
        params = reduce_moments(current)

        def block_equilibrium(quad_block):
            exponent = jnp.dot(quad_block, params[13:23], precision=lax.Precision.HIGHEST, preferred_element_type=jnp.float32)
            return jnp.exp(-0.5 * exponent)

        norm_z = jnp.sum(lax.map(lambda quad_block: jnp.sum(block_equilibrium(quad_block), axis=0), quad_blocks), axis=0) / V
        state_blocks = current.reshape(level_count, block_rows, CELLS)

        def update(inputs):
            state_block, vel_block, quad_block = inputs
            neighbours = [jnp.take(state_block, neighbour_index[side], axis=1) for side in range(FACES)]
            return relax(state_block, neighbours, vel_block, normals, params, norm_z, block_equilibrium(quad_block))

        current = lax.map(update, (state_blocks, vel_blocks, quad_blocks)).reshape(V, CELLS)
    final = reduce_moments(current)
    return current, final[:13]
```

```python
import functools

import jax
import jax.numpy as jnp
from jax import lax
from jax.experimental import pallas as pl
from jax.experimental.pallas import tpu as pltpu
from jax.sharding import Mesh, PartitionSpec as P

VXY = 32
TILE = 128
CELLS = 256
GROUPS = 8
NODES = 64
LANES = 128
TILES = 16
LEVELS = 32
FACES = 4
TOTAL = 32768

spacing = 0.3
ellipsoid_mix = -0.25
prandtl = 0.8
visc_power = 0.26
time_step = 0.025

ROW_ADJ = NODES
ROW_NORMAL = ROW_ADJ + FACES
ROW_SEND = ROW_NORMAL + 3 * FACES
ROW_COUNT = ROW_SEND + GROUPS
ROWS = ROW_COUNT + GROUPS

HIGHEST = lax.Precision.HIGHEST
PARAMS = pltpu.CompilerParams(vmem_limit_bytes=48 * 1024 * 1024)


def level(i):
    return (i - (VXY - 1) / 2.0) * spacing


def take_lanes(values, lanes):
    return jnp.take_along_axis(values, lanes, axis=1, mode="promise_in_bounds")


def node_x(rows, lanes):
    row = lax.broadcasted_iota(jnp.int32, (rows, lanes), 0)
    return ((row & (VXY - 1)).astype(jnp.float32) - (VXY - 1) / 2.0) * spacing


def neighbour_tiles(block_ref, g):
    adj = block_ref[g, ROW_ADJ : ROW_ADJ + FACES, :]
    adj = jnp.concatenate([adj[:, :LANES], adj[:, LANES:]], axis=0)
    place = adj - CELLS
    end = jnp.zeros((1, LANES), jnp.float32)
    source = jnp.zeros(adj.shape, jnp.float32)
    start = jnp.zeros(adj.shape, jnp.float32)
    for s in range(GROUPS):
        end = end + TILE * block_ref[g, ROW_COUNT + s : ROW_COUNT + s + 1, :LANES]
        past = end <= place
        source = source + jnp.where(past, 1.0, 0.0)
        if s < GROUPS - 1:
            start = jnp.where(past, jnp.broadcast_to(end, adj.shape), start)
    source = jnp.minimum(source, GROUPS - 1.0)
    slot = jnp.clip(place - start, 0.0, CELLS - 1.0).astype(jnp.int32)
    table = source.astype(jnp.int32) * 2 + (slot >> 7)
    lane = slot & (LANES - 1)
    mine = lax.broadcasted_iota(jnp.int32, adj.shape, 0) == g
    listed = jnp.zeros(adj.shape, jnp.float32)
    for s in range(GROUPS):
        for half in range(2):
            rows = block_ref[s, ROW_SEND : ROW_SEND + GROUPS, half * LANES : (half + 1) * LANES]
            row = column_sum(jnp.where(mine, rows, 0.0))
            found = take_lanes(jnp.broadcast_to(row, adj.shape), lane)
            listed = jnp.where(table == s * 2 + half, found, listed)
    far = source * CELLS + listed
    own = adj + jnp.float32(CELLS) * lax.convert_element_type(g, jnp.float32)
    return jnp.where(adj < CELLS, own, far).astype(jnp.int32)


def transport(value_ref, normal_ref, near, node_ref, g, half):
    at = slice(half * LANES, (half + 1) * LANES)
    lanes, tiles = [], []
    for face in range(FACES):
        row = jnp.broadcast_to(near[half * FACES + face : half * FACES + face + 1, :], (8, LANES))
        lanes.append(row & (LANES - 1))
        tiles.append(row >> 7)
    blocks = NODES // 8
    found = [[None] * blocks for _ in range(FACES)]
    for t in range(TILES):
        hit = [tiles[face] == t for face in range(FACES)]
        for b in range(blocks):
            source = value_ref[t // 2, b * 8 : b * 8 + 8, (t % 2) * LANES : (t % 2 + 1) * LANES]
            for face in range(FACES):
                got = take_lanes(source, lanes[face])
                found[face][b] = got if t == 0 else jnp.where(hit[face], got, found[face][b])
    out = []
    speeds = []
    for face in range(FACES):
        normal = [
            normal_ref[g, ROW_NORMAL + 3 * face + d : ROW_NORMAL + 3 * face + d + 1, at] for d in range(3)
        ]
        fixed = [normal[1] * node_ref[0, y] + normal[2] * node_ref[0, 2] for y in range(2)]
        speeds.append((jnp.broadcast_to(normal[0], (8, LANES)), [jnp.broadcast_to(f, (8, LANES)) for f in fixed]))
    comp_x = node_x(VXY, LANES)
    for b in range(blocks):
        own = value_ref[g, b * 8 : b * 8 + 8, at]
        vx = comp_x[(b % 4) * 8 : (b % 4) * 8 + 8, :]
        total = jnp.zeros((8, LANES), jnp.float32)
        for face in range(FACES):
            speed = speeds[face][0] * vx + speeds[face][1][b // 4]
            total = total + speed * jnp.where(speed > 0.0, own, found[face][b])
        out.append(total)
    return jnp.concatenate(out, axis=0)


def moment_table(node_ref, third):
    row = lax.broadcasted_iota(jnp.int32, (8, NODES), 0)
    col = lax.broadcasted_iota(jnp.int32, (8, NODES), 1)
    x = ((col & (VXY - 1)).astype(jnp.float32) - (VXY - 1) / 2.0) * spacing
    y = jnp.where(col >= VXY, node_ref[0, 1], node_ref[0, 0])
    flat = x * x + y * y
    table = jnp.zeros((8, NODES), jnp.float32)
    picks = [jnp.ones_like(x), x, y, x * x, y * y, x * y]
    if third:
        picks += [x * flat, y * flat]
    for i, pick in enumerate(picks):
        table = jnp.where(row == i, pick, table)
    return table


def first_kernel(node_ref, block_ref, near_ref, flux_ref, sums_ref):
    table = moment_table(node_ref, False)

    def group(g, carry):
        near = neighbour_tiles(block_ref, g)
        near_ref[g] = near
        for half in range(2):
            at = slice(half * LANES, (half + 1) * LANES)
            flux = transport(block_ref, block_ref, near, node_ref, g, half)
            flux_ref[g, :, at] = flux
            own = block_ref[g, :NODES, at]
            sums_ref[g * 2 + half, :8, :] = jnp.dot(
                table, own, precision=HIGHEST, preferred_element_type=jnp.float32
            )
            sums_ref[g * 2 + half, 8:, :] = jnp.dot(
                table, flux, precision=HIGHEST, preferred_element_type=jnp.float32
            )
        return carry

    lax.fori_loop(0, GROUPS, group, 0)


def macroscopic(m):
    density = m[0]
    scale = 1.0 / density
    ux, uy, uz = m[1] * scale, m[2] * scale, m[3] * scale
    second = [m[4 + i] * scale for i in range(6)]
    txx = second[0] - ux * ux
    tyy = second[1] - uy * uy
    tzz = second[2] - uz * uz
    txy = second[3] - ux * uy
    txz = second[4] - ux * uz
    tyz = second[5] - uy * uz
    temper = (txx + tyy + tzz) / 3.0
    return density, (ux, uy, uz), second, (txx, tyy, tzz, txy, txz, tyz), temper


def coefficients(m):
    density, (ux, uy, uz), _, (txx, tyy, tzz, txy, txz, tyz), temper = macroscopic(m)
    iso = (1.0 - ellipsoid_mix) * temper
    lxx = iso + ellipsoid_mix * txx
    lyy = iso + ellipsoid_mix * tyy
    lzz = iso + ellipsoid_mix * tzz
    lxy = ellipsoid_mix * txy
    lxz = ellipsoid_mix * txz
    lyz = ellipsoid_mix * tyz
    cxx = lyy * lzz - lyz * lyz
    cxy = lyz * lxz - lxy * lzz
    cxz = lxy * lyz - lyy * lxz
    cyy = lxx * lzz - lxz * lxz
    cyz = lxy * lxz - lxx * lyz
    czz = lxx * lyy - lxy * lxy
    det = 1.0 / (lxx * cxx + lxy * cxy + lxz * cxz)
    inverse = (cxx * det, cyy * det, czz * det, cxy * det, cxz * det, cyz * det)
    collide = prandtl * density * jnp.exp(visc_power * jnp.log(temper))
    return density, (ux, uy, uz), inverse, collide


def factor_tables(mean, inverse, pair_ref, row_ref, col_ref):
    grid = level(lax.broadcasted_iota(jnp.int32, (VXY, LANES), 0).astype(jnp.float32))
    ixx, iyy, izz, ixy, ixz, iyz = inverse
    cx, cy, cz = grid - mean[0], grid - mean[1], grid - mean[2]
    own_x, own_y, own_z = -0.25 * ixx * cx * cx, -0.25 * iyy * cy * cy, -0.25 * izz * cz * cz
    cross_y = -ixy * cy
    cross_z = -ixz * cz
    cross_yz = -iyz * cy
    for i in range(VXY):
        x_own, x_c = own_x[i : i + 1, :], cx[i : i + 1, :]
        z_own, z_c = own_z[i : i + 1, :], cz[i : i + 1, :]
        pair_ref[i] = jnp.exp(x_own + own_y + x_c * cross_y)
        row_ref[i] = jnp.exp(x_own + own_z + x_c * cross_z)
        col_ref[i] = jnp.exp(z_own + own_y + z_c * cross_yz)


def column_sum(a):
    return jnp.sum(a, axis=0, keepdims=True)


def equilibrium_moments(mean, inverse, pair_ref, row_ref, col_ref):
    factor_tables(mean, inverse, pair_ref, row_ref, col_ref)
    zero = jnp.zeros((VXY, LANES), jnp.float32)

    def step(i, carry):
        s0, sx, sxx, s1, s1x, s2 = carry
        u0, u1, u2 = zero, zero, zero
        for k in range(VXY // 2):
            z = -level(k)
            low = row_ref[i, k : k + 1, :] * col_ref[k]
            high = row_ref[i, VXY - 1 - k : VXY - k, :] * col_ref[VXY - 1 - k]
            both = low + high
            u0 = u0 + both
            u1 = u1 + z * (high - low)
            u2 = u2 + (z * z) * both
        pair = pair_ref[i]
        x = level(lax.convert_element_type(i, jnp.float32))
        w0, w1 = pair * u0, pair * u1
        s0 = s0 + w0
        sx = sx + x * w0
        sxx = sxx + (x * x) * w0
        s1 = s1 + w1
        s1x = s1x + x * w1
        s2 = s2 + pair * u2
        return s0, sx, sxx, s1, s1x, s2

    s0, sx, sxx, s1, s1x, s2 = lax.fori_loop(0, VXY, step, (zero,) * 6)
    y = level(lax.broadcasted_iota(jnp.int32, (VXY, LANES), 0).astype(jnp.float32))
    return [
        column_sum(a)
        for a in (s0, sx, y * s0, s1, sxx, y * y * s0, s2, y * sx, s1x, y * s1)
    ]


def equilibrium_total(mean, inverse, pair_ref, row_ref, col_ref):
    factor_tables(mean, inverse, pair_ref, row_ref, col_ref)
    zero = jnp.zeros((VXY, LANES), jnp.float32)

    def step(i, total):
        u = zero
        for k in range(VXY):
            u = u + row_ref[i, k : k + 1, :] * col_ref[k]
        return total + pair_ref[i] * u

    return column_sum(lax.fori_loop(0, VXY, step, zero))


def put_rows(out_ref, base, mean, inverse, alpha, beta):
    ixx, iyy, izz, ixy, ixz, iyz = inverse
    lx = ixx * mean[0] + ixy * mean[1] + ixz * mean[2]
    ly = ixy * mean[0] + iyy * mean[1] + iyz * mean[2]
    lz = ixz * mean[0] + iyz * mean[1] + izz * mean[2]
    offset = mean[0] * lx + mean[1] * ly + mean[2] * lz
    rows = [ixx, iyy, izz, 2.0 * ixy, 2.0 * ixz, 2.0 * iyz, -2.0 * lx, -2.0 * ly, -2.0 * lz, offset, alpha, beta]
    for i, row in enumerate(rows):
        out_ref[base + i : base + i + 1, :] = row


def level_sums(parts_ref, rows):
    zero = jnp.zeros((rows, LANES), jnp.float32)
    s0, s1, s2, s3 = zero, zero, zero, zero
    for i in range(LEVELS):
        part = parts_ref[i]
        z = level(i)
        s0 = s0 + part
        s1 = s1 + z * part
        s2 = s2 + (z * z) * part
        if rows == 8:
            s3 = s3 + (z * z * z) * part
    return s0, s1, s2, s3


def ten(s0, s1, s2, base):
    def row(a, i):
        return a[base + i : base + i + 1, :] / TOTAL

    return [
        row(s0, 0), row(s0, 1), row(s0, 2), row(s1, 0), row(s0, 3), row(s0, 4), row(s2, 0),
        row(s0, 5), row(s1, 1), row(s1, 2),
    ]


def fields_kernel(parts_ref, out_ref, pair_ref, row_ref, col_ref):
    s0, s1, s2, _ = level_sums(parts_ref, 16)
    now = ten(s0, s1, s2, 0)
    moved = ten(s0, s1, s2, 8)
    density, mean, inverse, collide = coefficients(now)
    gauss = equilibrium_moments(mean, inverse, pair_ref, row_ref, col_ref)
    beta = time_step * collide * density * TOTAL / gauss[0]
    alpha = 1.0 - time_step * collide
    put_rows(out_ref, 0, mean, inverse, alpha, beta)
    later = [alpha * a + beta * (e / TOTAL) - time_step * b for a, e, b in zip(now, gauss, moved)]
    density, mean, inverse, collide = coefficients(later)
    total = equilibrium_total(mean, inverse, pair_ref, row_ref, col_ref)
    beta = time_step * collide * density * TOTAL / total
    put_rows(out_ref, 12, mean, inverse, 1.0 - time_step * collide, beta)


def relaxed_tile(value, flux, params_ref, base, tile, node_ref):
    rows = [params_ref[tile, base + i : base + i + 1, :] for i in range(12)]
    ixx, iyy, izz, ixy, ixz, iyz, lx, ly, lz, offset, alpha, beta = rows
    vz = node_ref[0, 2]
    x = node_x(VXY, LANES)
    parts = []
    for y in range(2):
        vy = node_ref[0, y]
        slope = ixy * vy + ixz * vz + lx
        rest = (iyy * vy + iyz * vz + ly) * vy + (izz * vz + lz) * vz + offset
        energy = jnp.exp(-0.5 * ((ixx * x + slope) * x + rest))
        at = slice(y * VXY, (y + 1) * VXY)
        parts.append(alpha * value[at, :] + beta * energy - time_step * flux[at, :])
    return jnp.concatenate(parts, axis=0)


def second_kernel(node_ref, block_ref, near_ref, flux_ref, params_ref, out_ref, sums_ref, value_ref):
    table = moment_table(node_ref, True)

    def first_step(g, carry):
        for half in range(2):
            at = slice(half * LANES, (half + 1) * LANES)
            value_ref[g, :, at] = relaxed_tile(
                block_ref[g, :NODES, at], flux_ref[g, :, at], params_ref, 0, g * 2 + half, node_ref
            )
        return carry

    lax.fori_loop(0, GROUPS, first_step, 0)

    def second_step(g, carry):
        near = near_ref[g]
        for half in range(2):
            at = slice(half * LANES, (half + 1) * LANES)
            flux = transport(value_ref, block_ref, near, node_ref, g, half)
            value = relaxed_tile(value_ref[g, :, at], flux, params_ref, 12, g * 2 + half, node_ref)
            out_ref[g, :, at] = value
            sums_ref[g * 2 + half] = jnp.dot(
                table, value, precision=HIGHEST, preferred_element_type=jnp.float32
            )
        return carry

    lax.fori_loop(0, GROUPS, second_step, 0)


def final_kernel(parts_ref, out_ref):
    s0, s1, s2, s3 = level_sums(parts_ref, 8)

    def row(a, i):
        return a[i : i + 1, :] / TOTAL

    density, (ux, uy, uz), b, theta, _ = macroscopic(ten(s0, s1, s2, 0))
    third = [
        row(s0, 6) + row(s2, 1),
        row(s0, 7) + row(s2, 2),
        row(s1, 3) + row(s1, 4) + row(s3, 0),
    ]
    trace = b[0] + b[1] + b[2]
    square = ux * ux + uy * uy + uz * uz
    stress = (
        b[0] * ux + b[3] * uy + b[4] * uz,
        b[3] * ux + b[1] * uy + b[5] * uz,
        b[4] * ux + b[5] * uy + b[2] * uz,
    )
    flux = [
        0.5 * (t / density - 2.0 * s - u * trace + 2.0 * u * square)
        for t, s, u in zip(third, stress, (ux, uy, uz))
    ]
    for i, value in enumerate((density, ux, uy, uz, *theta, *flux)):
        out_ref[i : i + 1, :] = value
    out_ref[13:16, :] = jnp.zeros((3, LANES), jnp.float32)


def shape(*dims, dtype=jnp.float32):
    return jax.ShapeDtypeStruct(dims, dtype)


VMEM = pl.BlockSpec(memory_space=pltpu.VMEM)
SMEM = pl.BlockSpec(memory_space=pltpu.SMEM)
TABLES = [pltpu.VMEM((VXY, VXY, LANES), jnp.float32)] * 3


def spread(x, axes, count):
    copies = jnp.broadcast_to(x, (count, *x.shape))
    return lax.all_to_all(copies, axes, 0, 0, tiled=True)


def per_device(distribution, normals, adjacency, send_list, block_counts):
    z, x, y, c = (lax.axis_index(a) for a in ("z", "x", "y", "c"))
    vel = (x * 8 + y) * 2 + c
    row = (vel * 16 + z * 2) & (VXY - 1)
    node = jnp.stack([row, row + 1, vel // 2, vel // 2]).astype(jnp.float32)
    node = ((node - (VXY - 1) / 2.0) * spacing).reshape(1, 4)

    extra = jnp.concatenate(
        [
            adjacency.astype(jnp.float32),
            normals.reshape(3 * FACES, CELLS),
            send_list[0].astype(jnp.float32),
            jnp.broadcast_to(block_counts.astype(jnp.float32), (GROUPS, CELLS)),
        ],
        axis=0,
    )
    block = jnp.concatenate(
        [distribution.reshape(GROUPS, NODES, CELLS), jnp.broadcast_to(extra, (GROUPS, *extra.shape))], axis=1
    )
    block = lax.all_to_all(block, "z", 0, 0, tiled=True)

    near, flux, sums = pl.pallas_call(
        first_kernel,
        out_shape=(
            shape(GROUPS, 8, LANES, dtype=jnp.int32),
            shape(GROUPS, NODES, CELLS),
            shape(TILES, 16, LANES),
        ),
        in_specs=[SMEM, VMEM],
        out_specs=(VMEM, VMEM, VMEM),
        compiler_params=PARAMS,
    )(node, block)

    mine = jnp.sum(lax.all_to_all(sums, ("z", "c"), 0, 0, tiled=True), axis=0)
    params = pl.pallas_call(
        fields_kernel,
        out_shape=shape(24, LANES),
        in_specs=[VMEM],
        out_specs=VMEM,
        scratch_shapes=TABLES,
        compiler_params=PARAMS,
    )(spread(mine, ("x", "y"), LEVELS))
    params = spread(params, ("z", "c"), TILES)

    value, sums = pl.pallas_call(
        second_kernel,
        out_shape=(shape(GROUPS, NODES, CELLS), shape(TILES, 8, LANES)),
        in_specs=[SMEM, VMEM, VMEM, VMEM, VMEM],
        out_specs=(VMEM, VMEM),
        scratch_shapes=[pltpu.VMEM((GROUPS, NODES, CELLS), jnp.float32)],
        compiler_params=PARAMS,
    )(node, block, near, flux, params)

    relaxed = lax.all_to_all(value, "z", 0, 0, tiled=True).reshape(GROUPS * NODES, CELLS)
    mine = jnp.sum(lax.all_to_all(sums, ("z", "c"), 0, 0, tiled=True), axis=0)
    fields = pl.pallas_call(
        final_kernel,
        out_shape=shape(16, LANES),
        in_specs=[VMEM],
        out_specs=VMEM,
        compiler_params=PARAMS,
    )(spread(mine, ("x", "y"), LEVELS))
    both = spread(fields, "c", 2)
    return relaxed, jnp.concatenate([both[0], both[1]], axis=1)[:13]


def solution(mesh):
    split = Mesh(mesh.devices.reshape(8, 4, 8, 2), ("z", "x", "y", "c"))
    vel = ("x", "y", "c")
    placed = (P(vel, "z"), P(None, None, "z"), P(None, "z"), P("z", None, None), P(None, "z"))
    return jax.shard_map(
        per_device,
        mesh=split,
        in_specs=placed,
        out_specs=(P(vel, "z"), P(None, "z")),
        check_vma=False,
    )
```

```python
import jax
import jax.numpy as jnp
from jax import lax
from jax.experimental import pallas as pl
from jax.experimental.pallas import tpu as pltpu
from jax.sharding import Mesh, PartitionSpec as P

VXY = 32
TILE = 128
CELLS = 256
GROUPS = 8
NODES = 64
LANES = 128
TILES = 16
LEVELS = 32
FACES = 4
TOTAL = 32768

spacing = 0.3
ellipsoid_mix = -0.25
prandtl = 0.8
visc_power = 0.26
time_step = 0.025

ROW_ADJ = NODES
ROW_NORMAL = ROW_ADJ + FACES
ROW_SEND = ROW_NORMAL + 3 * FACES
ROW_COUNT = ROW_SEND + GROUPS
ROWS = ROW_COUNT + GROUPS

HIGHEST = lax.Precision.HIGHEST
PARAMS = pltpu.CompilerParams(vmem_limit_bytes=48 * 1024 * 1024)


def level(i):
    return (i - (VXY - 1) / 2.0) * spacing


def take_lanes(values, lanes):
    return jnp.take_along_axis(values, lanes, axis=1, mode="promise_in_bounds")


def node_x(rows, lanes):
    row = lax.broadcasted_iota(jnp.int32, (rows, lanes), 0)
    return ((row & (VXY - 1)).astype(jnp.float32) - (VXY - 1) / 2.0) * spacing


def neighbour_tiles(block_ref, g):
    adj = block_ref[g, ROW_ADJ : ROW_ADJ + FACES, :]
    adj = jnp.concatenate([adj[:, :LANES], adj[:, LANES:]], axis=0)
    place = adj - CELLS
    end = jnp.zeros((1, LANES), jnp.float32)
    source = jnp.zeros(adj.shape, jnp.float32)
    start = jnp.zeros(adj.shape, jnp.float32)
    for s in range(GROUPS):
        end = end + TILE * block_ref[g, ROW_COUNT + s : ROW_COUNT + s + 1, :LANES]
        past = end <= place
        source = source + jnp.where(past, 1.0, 0.0)
        if s < GROUPS - 1:
            start = jnp.where(past, jnp.broadcast_to(end, adj.shape), start)
    source = jnp.minimum(source, GROUPS - 1.0)
    slot = jnp.clip(place - start, 0.0, CELLS - 1.0).astype(jnp.int32)
    table = source.astype(jnp.int32) * 2 + (slot >> 7)
    lane = slot & (LANES - 1)
    mine = lax.broadcasted_iota(jnp.int32, adj.shape, 0) == g
    listed = jnp.zeros(adj.shape, jnp.float32)
    for s in range(GROUPS):
        for half in range(2):
            rows = block_ref[s, ROW_SEND : ROW_SEND + GROUPS, half * LANES : (half + 1) * LANES]
            row = column_sum(jnp.where(mine, rows, 0.0))
            found = take_lanes(jnp.broadcast_to(row, adj.shape), lane)
            listed = jnp.where(table == s * 2 + half, found, listed)
    far = source * CELLS + listed
    own = adj + jnp.float32(CELLS) * lax.convert_element_type(g, jnp.float32)
    return jnp.where(adj < CELLS, own, far).astype(jnp.int32)


def split_terms(value_ref, terms_ref, g):
    value = value_ref[g, :NODES, :]
    high = value.astype(jnp.bfloat16)
    terms_ref[g, :NODES, :] = high
    terms_ref[g, NODES:, :] = (value - high.astype(jnp.float32)).astype(jnp.bfloat16)


def transport(value_ref, terms_ref, normal_ref, near, node_ref, g):
    own = value_ref[g, :NODES, :]
    x = node_x(NODES, CELLS)
    second = lax.broadcasted_iota(jnp.int32, (NODES, CELLS), 0) >= VXY
    place = lax.broadcasted_iota(jnp.int32, (CELLS, CELLS), 0)
    total = jnp.zeros((NODES, CELLS), jnp.float32)
    for face in range(FACES):
        row = jnp.concatenate([near[face : face + 1, :], near[FACES + face : FACES + face + 1, :]], axis=1)
        chosen = jnp.where(place == (row & (CELLS - 1)), 1.0, 0.0).astype(jnp.bfloat16)
        group = row >> 8
        found = None
        for s in range(GROUPS):
            both = jnp.dot(terms_ref[s], chosen, preferred_element_type=jnp.float32)
            got = both[:NODES] + both[NODES:]
            found = got if s == 0 else jnp.where(group == s, got, found)
        normal = [normal_ref[g, ROW_NORMAL + 3 * face + d : ROW_NORMAL + 3 * face + d + 1, :] for d in range(3)]
        fixed = [normal[1] * node_ref[0, y] + normal[2] * node_ref[0, 2] for y in range(2)]
        speed = normal[0] * x + jnp.where(second, fixed[1], fixed[0])
        total = total + speed * jnp.where(speed > 0.0, own, found)
    return total


def moment_table(node_ref, third):
    row = lax.broadcasted_iota(jnp.int32, (8, NODES), 0)
    col = lax.broadcasted_iota(jnp.int32, (8, NODES), 1)
    x = ((col & (VXY - 1)).astype(jnp.float32) - (VXY - 1) / 2.0) * spacing
    y = jnp.where(col >= VXY, node_ref[0, 1], node_ref[0, 0])
    flat = x * x + y * y
    table = jnp.zeros((8, NODES), jnp.float32)
    picks = [jnp.ones_like(x), x, y, x * x, y * y, x * y]
    if third:
        picks += [x * flat, y * flat]
    for i, pick in enumerate(picks):
        table = jnp.where(row == i, pick, table)
    return table


def first_kernel(node_ref, block_ref, near_ref, flux_ref, sums_ref, terms_ref):
    table = moment_table(node_ref, False)
    for g in range(GROUPS):
        split_terms(block_ref, terms_ref, g)

    def group(g, carry):
        near = neighbour_tiles(block_ref, g)
        near_ref[g] = near
        flux = transport(block_ref, terms_ref, block_ref, near, node_ref, g)
        flux_ref[g] = flux
        own = block_ref[g, :NODES, :]
        for base, value in ((0, own), (8, flux)):
            sums = jnp.dot(table, value, precision=HIGHEST, preferred_element_type=jnp.float32)
            for half in range(2):
                sums_ref[g * 2 + half, base : base + 8, :] = sums[:, half * LANES : (half + 1) * LANES]
        return carry

    lax.fori_loop(0, GROUPS, group, 0)


def macroscopic(m):
    density = m[0]
    scale = 1.0 / density
    ux, uy, uz = m[1] * scale, m[2] * scale, m[3] * scale
    second = [m[4 + i] * scale for i in range(6)]
    txx = second[0] - ux * ux
    tyy = second[1] - uy * uy
    tzz = second[2] - uz * uz
    txy = second[3] - ux * uy
    txz = second[4] - ux * uz
    tyz = second[5] - uy * uz
    temper = (txx + tyy + tzz) / 3.0
    return density, (ux, uy, uz), second, (txx, tyy, tzz, txy, txz, tyz), temper


def coefficients(m):
    density, (ux, uy, uz), _, (txx, tyy, tzz, txy, txz, tyz), temper = macroscopic(m)
    iso = (1.0 - ellipsoid_mix) * temper
    lxx = iso + ellipsoid_mix * txx
    lyy = iso + ellipsoid_mix * tyy
    lzz = iso + ellipsoid_mix * tzz
    lxy = ellipsoid_mix * txy
    lxz = ellipsoid_mix * txz
    lyz = ellipsoid_mix * tyz
    cxx = lyy * lzz - lyz * lyz
    cxy = lyz * lxz - lxy * lzz
    cxz = lxy * lyz - lyy * lxz
    cyy = lxx * lzz - lxz * lxz
    cyz = lxy * lxz - lxx * lyz
    czz = lxx * lyy - lxy * lxy
    det = 1.0 / (lxx * cxx + lxy * cxy + lxz * cxz)
    inverse = (cxx * det, cyy * det, czz * det, cxy * det, cxz * det, cyz * det)
    collide = prandtl * density * jnp.exp(visc_power * jnp.log(temper))
    return density, (ux, uy, uz), inverse, collide


def factor_tables(mean, inverse, pair_ref, row_ref, col_ref):
    grid = level(lax.broadcasted_iota(jnp.int32, (VXY, LANES), 0).astype(jnp.float32))
    ixx, iyy, izz, ixy, ixz, iyz = inverse
    cx, cy, cz = grid - mean[0], grid - mean[1], grid - mean[2]
    own_x, own_y, own_z = -0.25 * ixx * cx * cx, -0.25 * iyy * cy * cy, -0.25 * izz * cz * cz
    cross_y = -ixy * cy
    cross_z = -ixz * cz
    cross_yz = -iyz * cy
    for i in range(VXY):
        x_own, x_c = own_x[i : i + 1, :], cx[i : i + 1, :]
        z_own, z_c = own_z[i : i + 1, :], cz[i : i + 1, :]
        pair_ref[i] = jnp.exp(x_own + own_y + x_c * cross_y)
        row_ref[i] = jnp.exp(x_own + own_z + x_c * cross_z)
        col_ref[i] = jnp.exp(z_own + own_y + z_c * cross_yz)


def column_sum(a):
    return jnp.sum(a, axis=0, keepdims=True)


def equilibrium_moments(mean, inverse, pair_ref, row_ref, col_ref):
    factor_tables(mean, inverse, pair_ref, row_ref, col_ref)
    zero = jnp.zeros((VXY, LANES), jnp.float32)

    def step(i, carry):
        s0, sx, sxx, s1, s1x, s2 = carry
        u0, u1, u2 = zero, zero, zero
        for k in range(VXY // 2):
            z = -level(k)
            low = row_ref[i, k : k + 1, :] * col_ref[k]
            high = row_ref[i, VXY - 1 - k : VXY - k, :] * col_ref[VXY - 1 - k]
            both = low + high
            u0 = u0 + both
            u1 = u1 + z * (high - low)
            u2 = u2 + (z * z) * both
        pair = pair_ref[i]
        x = level(lax.convert_element_type(i, jnp.float32))
        w0, w1 = pair * u0, pair * u1
        s0 = s0 + w0
        sx = sx + x * w0
        sxx = sxx + (x * x) * w0
        s1 = s1 + w1
        s1x = s1x + x * w1
        s2 = s2 + pair * u2
        return s0, sx, sxx, s1, s1x, s2

    s0, sx, sxx, s1, s1x, s2 = lax.fori_loop(0, VXY, step, (zero,) * 6)
    y = level(lax.broadcasted_iota(jnp.int32, (VXY, LANES), 0).astype(jnp.float32))
    return [
        column_sum(a)
        for a in (s0, sx, y * s0, s1, sxx, y * y * s0, s2, y * sx, s1x, y * s1)
    ]


def equilibrium_total(mean, inverse, pair_ref, row_ref, col_ref):
    factor_tables(mean, inverse, pair_ref, row_ref, col_ref)
    zero = jnp.zeros((VXY, LANES), jnp.float32)

    def step(i, total):
        u = zero
        for k in range(VXY):
            u = u + row_ref[i, k : k + 1, :] * col_ref[k]
        return total + pair_ref[i] * u

    return column_sum(lax.fori_loop(0, VXY, step, zero))


def put_rows(out_ref, base, mean, inverse, alpha, beta):
    ixx, iyy, izz, ixy, ixz, iyz = inverse
    lx = ixx * mean[0] + ixy * mean[1] + ixz * mean[2]
    ly = ixy * mean[0] + iyy * mean[1] + iyz * mean[2]
    lz = ixz * mean[0] + iyz * mean[1] + izz * mean[2]
    offset = mean[0] * lx + mean[1] * ly + mean[2] * lz
    rows = [ixx, iyy, izz, 2.0 * ixy, 2.0 * ixz, 2.0 * iyz, -2.0 * lx, -2.0 * ly, -2.0 * lz, offset, alpha, beta]
    for i, row in enumerate(rows):
        out_ref[base + i : base + i + 1, :] = row


def level_sums(parts_ref, rows):
    zero = jnp.zeros((rows, LANES), jnp.float32)
    s0, s1, s2, s3 = zero, zero, zero, zero
    for i in range(LEVELS):
        part = parts_ref[i]
        z = level(i)
        s0 = s0 + part
        s1 = s1 + z * part
        s2 = s2 + (z * z) * part
        if rows == 8:
            s3 = s3 + (z * z * z) * part
    return s0, s1, s2, s3


def ten(s0, s1, s2, base):
    def row(a, i):
        return a[base + i : base + i + 1, :] / TOTAL

    return [
        row(s0, 0), row(s0, 1), row(s0, 2), row(s1, 0), row(s0, 3), row(s0, 4), row(s2, 0),
        row(s0, 5), row(s1, 1), row(s1, 2),
    ]


def fields_kernel(parts_ref, out_ref, pair_ref, row_ref, col_ref):
    s0, s1, s2, _ = level_sums(parts_ref, 16)
    now = ten(s0, s1, s2, 0)
    moved = ten(s0, s1, s2, 8)
    density, mean, inverse, collide = coefficients(now)
    gauss = equilibrium_moments(mean, inverse, pair_ref, row_ref, col_ref)
    beta = time_step * collide * density * TOTAL / gauss[0]
    alpha = 1.0 - time_step * collide
    put_rows(out_ref, 0, mean, inverse, alpha, beta)
    later = [alpha * a + beta * (e / TOTAL) - time_step * b for a, e, b in zip(now, gauss, moved)]
    density, mean, inverse, collide = coefficients(later)
    total = equilibrium_total(mean, inverse, pair_ref, row_ref, col_ref)
    beta = time_step * collide * density * TOTAL / total
    put_rows(out_ref, 12, mean, inverse, 1.0 - time_step * collide, beta)


def relaxed_tile(value, flux, params_ref, base, tile, node_ref):
    rows = [params_ref[tile, base + i : base + i + 1, :] for i in range(12)]
    ixx, iyy, izz, ixy, ixz, iyz, lx, ly, lz, offset, alpha, beta = rows
    vz = node_ref[0, 2]
    x = node_x(VXY, LANES)
    parts = []
    for y in range(2):
        vy = node_ref[0, y]
        slope = ixy * vy + ixz * vz + lx
        rest = (iyy * vy + iyz * vz + ly) * vy + (izz * vz + lz) * vz + offset
        energy = jnp.exp(-0.5 * ((ixx * x + slope) * x + rest))
        at = slice(y * VXY, (y + 1) * VXY)
        parts.append(alpha * value[at, :] + beta * energy - time_step * flux[at, :])
    return jnp.concatenate(parts, axis=0)


def second_kernel(node_ref, block_ref, near_ref, flux_ref, params_ref, out_ref, sums_ref, value_ref, terms_ref):
    table = moment_table(node_ref, True)

    def first_step(g, carry):
        for half in range(2):
            at = slice(half * LANES, (half + 1) * LANES)
            value_ref[g, :, at] = relaxed_tile(
                block_ref[g, :NODES, at], flux_ref[g, :, at], params_ref, 0, g * 2 + half, node_ref
            )
        split_terms(value_ref, terms_ref, g)
        return carry

    lax.fori_loop(0, GROUPS, first_step, 0)

    def second_step(g, carry):
        flux = transport(value_ref, terms_ref, block_ref, near_ref[g], node_ref, g)
        for half in range(2):
            at = slice(half * LANES, (half + 1) * LANES)
            value = relaxed_tile(value_ref[g, :, at], flux[:, at], params_ref, 12, g * 2 + half, node_ref)
            out_ref[g, :, at] = value
            sums_ref[g * 2 + half] = jnp.dot(
                table, value, precision=HIGHEST, preferred_element_type=jnp.float32
            )
        return carry

    lax.fori_loop(0, GROUPS, second_step, 0)


def final_kernel(parts_ref, out_ref):
    s0, s1, s2, s3 = level_sums(parts_ref, 8)

    def row(a, i):
        return a[i : i + 1, :] / TOTAL

    density, (ux, uy, uz), b, theta, _ = macroscopic(ten(s0, s1, s2, 0))
    third = [
        row(s0, 6) + row(s2, 1),
        row(s0, 7) + row(s2, 2),
        row(s1, 3) + row(s1, 4) + row(s3, 0),
    ]
    trace = b[0] + b[1] + b[2]
    square = ux * ux + uy * uy + uz * uz
    stress = (
        b[0] * ux + b[3] * uy + b[4] * uz,
        b[3] * ux + b[1] * uy + b[5] * uz,
        b[4] * ux + b[5] * uy + b[2] * uz,
    )
    flux = [
        0.5 * (t / density - 2.0 * s - u * trace + 2.0 * u * square)
        for t, s, u in zip(third, stress, (ux, uy, uz))
    ]
    for i, value in enumerate((density, ux, uy, uz, *theta, *flux)):
        out_ref[i : i + 1, :] = value
    out_ref[13:16, :] = jnp.zeros((3, LANES), jnp.float32)


def shape(*dims, dtype=jnp.float32):
    return jax.ShapeDtypeStruct(dims, dtype)


VMEM = pl.BlockSpec(memory_space=pltpu.VMEM)
SMEM = pl.BlockSpec(memory_space=pltpu.SMEM)
TERMS = pltpu.VMEM((GROUPS, 2 * NODES, CELLS), jnp.bfloat16)
TABLES = [pltpu.VMEM((VXY, VXY, LANES), jnp.float32)] * 3


def spread(x, axes, count):
    copies = jnp.broadcast_to(x, (count, *x.shape))
    return lax.all_to_all(copies, axes, 0, 0, tiled=True)


def per_device(distribution, normals, adjacency, send_list, block_counts):
    z, x, y, c = (lax.axis_index(a) for a in ("z", "x", "y", "c"))
    vel = (x * 8 + y) * 2 + c
    row = (vel * 16 + z * 2) & (VXY - 1)
    node = jnp.stack([row, row + 1, vel // 2, vel // 2]).astype(jnp.float32)
    node = ((node - (VXY - 1) / 2.0) * spacing).reshape(1, 4)

    extra = jnp.concatenate(
        [
            adjacency.astype(jnp.float32),
            normals.reshape(3 * FACES, CELLS),
            send_list[0].astype(jnp.float32),
            jnp.broadcast_to(block_counts.astype(jnp.float32), (GROUPS, CELLS)),
        ],
        axis=0,
    )
    block = jnp.concatenate(
        [distribution.reshape(GROUPS, NODES, CELLS), jnp.broadcast_to(extra, (GROUPS, *extra.shape))], axis=1
    )
    block = lax.all_to_all(block, "z", 0, 0, tiled=True)

    near, flux, sums = pl.pallas_call(
        first_kernel,
        out_shape=(
            shape(GROUPS, 8, LANES, dtype=jnp.int32),
            shape(GROUPS, NODES, CELLS),
            shape(TILES, 16, LANES),
        ),
        in_specs=[SMEM, VMEM],
        out_specs=(VMEM, VMEM, VMEM),
        scratch_shapes=[TERMS],
        compiler_params=PARAMS,
    )(node, block)

    mine = jnp.sum(lax.all_to_all(sums, ("z", "c"), 0, 0, tiled=True), axis=0)
    params = pl.pallas_call(
        fields_kernel,
        out_shape=shape(24, LANES),
        in_specs=[VMEM],
        out_specs=VMEM,
        scratch_shapes=TABLES,
        compiler_params=PARAMS,
    )(spread(mine, ("x", "y"), LEVELS))
    params = spread(params, ("z", "c"), TILES)

    value, sums = pl.pallas_call(
        second_kernel,
        out_shape=(shape(GROUPS, NODES, CELLS), shape(TILES, 8, LANES)),
        in_specs=[SMEM, VMEM, VMEM, VMEM, VMEM],
        out_specs=(VMEM, VMEM),
        scratch_shapes=[pltpu.VMEM((GROUPS, NODES, CELLS), jnp.float32), TERMS],
        compiler_params=PARAMS,
    )(node, block, near, flux, params)

    relaxed = lax.all_to_all(value, "z", 0, 0, tiled=True).reshape(GROUPS * NODES, CELLS)
    mine = jnp.sum(lax.all_to_all(sums, ("z", "c"), 0, 0, tiled=True), axis=0)
    fields = pl.pallas_call(
        final_kernel,
        out_shape=shape(16, LANES),
        in_specs=[VMEM],
        out_specs=VMEM,
        compiler_params=PARAMS,
    )(spread(mine, ("x", "y"), LEVELS))
    both = spread(fields, "c", 2)
    return relaxed, jnp.concatenate([both[0], both[1]], axis=1)[:13]


def solution(mesh):
    split = Mesh(mesh.devices.reshape(8, 4, 8, 2), ("z", "x", "y", "c"))
    vel = ("x", "y", "c")
    placed = (P(vel, "z"), P(None, None, "z"), P(None, "z"), P("z", None, None), P(None, "z"))
    return jax.shard_map(
        per_device,
        mesh=split,
        in_specs=placed,
        out_specs=(P(vel, "z"), P(None, "z")),
        check_vma=False,
    )
```

```python
import jax
import jax.numpy as jnp
from jax import lax
from jax.experimental import pallas as pl
from jax.experimental.pallas import tpu as pltpu
from jax.sharding import Mesh, PartitionSpec as P

VXY = 32
TILE = 128
CELLS = 256
GROUPS = 8
NODES = 64
LANES = 128
TILES = 16
LEVELS = 32
FACES = 4
TOTAL = 32768

spacing = 0.3
ellipsoid_mix = -0.25
prandtl = 0.8
visc_power = 0.26
time_step = 0.025

ROW_ADJ = NODES
ROW_NORMAL = ROW_ADJ + FACES
ROW_SEND = ROW_NORMAL + 3 * FACES
ROWS = ROW_SEND + GROUPS

HIGHEST = lax.Precision.HIGHEST
PARAMS = pltpu.CompilerParams(vmem_limit_bytes=48 * 1024 * 1024)


def level(i):
    return (i - (VXY - 1) / 2.0) * spacing


def take_lanes(values, lanes):
    return jnp.take_along_axis(values, lanes, axis=1, mode="promise_in_bounds")


def node_x(rows, lanes):
    row = lax.broadcasted_iota(jnp.int32, (rows, lanes), 0)
    return ((row & (VXY - 1)).astype(jnp.float32) - (VXY - 1) / 2.0) * spacing


def pack_kernel(value_ref, adjacency_ref, normal_ref, send_ref, count_ref, out_ref):
    adj = adjacency_ref[...]
    place = adj - CELLS
    counts = count_ref[...] * TILE
    end = jnp.zeros((1, 1), jnp.int32)
    source = jnp.zeros(adj.shape, jnp.int32)
    start = jnp.zeros(adj.shape, jnp.int32)
    for s in range(GROUPS - 1):
        end = end + counts[:, s : s + 1]
        past = end <= place
        source = source + jnp.where(past, 1, 0)
        start = jnp.where(past, end, start)
    slot = jnp.clip(place - start, 0, CELLS - 1)
    rows = [jnp.where(adj < CELLS, adj, CELLS + CELLS * source + slot).astype(jnp.float32)]
    rows += [normal_ref[d] for d in range(3)]
    rows = jnp.concatenate(rows + [send_ref[0].astype(jnp.float32)], axis=0)
    for g in range(GROUPS):
        out_ref[g, :NODES, :] = value_ref[g * NODES : (g + 1) * NODES, :]
        out_ref[g, NODES:, :] = rows


def neighbour_tiles(block_ref, g):
    adj = block_ref[g, ROW_ADJ : ROW_ADJ + FACES, :]
    adj = jnp.concatenate([adj[:, :LANES], adj[:, LANES:]], axis=0).astype(jnp.int32)
    place = jnp.maximum(adj - CELLS, 0)
    table = place >> 7
    lane = place & (LANES - 1)
    mine = lax.broadcasted_iota(jnp.int32, adj.shape, 0) == g
    listed = jnp.zeros(adj.shape, jnp.float32)
    for s in range(GROUPS):
        for half in range(2):
            rows = block_ref[s, ROW_SEND : ROW_SEND + GROUPS, half * LANES : (half + 1) * LANES]
            row = column_sum(jnp.where(mine, rows, 0.0))
            found = take_lanes(jnp.broadcast_to(row, adj.shape), lane)
            listed = jnp.where(table == s * 2 + half, found, listed)
    far = (place >> 8) * CELLS + listed.astype(jnp.int32)
    return jnp.where(adj < CELLS, adj + CELLS * g, far)


def split_terms(value_ref, terms_ref, g):
    value = value_ref[g, :NODES, :]
    high = value.astype(jnp.bfloat16)
    terms_ref[g, :NODES, :] = high
    terms_ref[g, NODES:, :] = (value - high.astype(jnp.float32)).astype(jnp.bfloat16)


def transport(value_ref, terms_ref, normal_ref, near, node_ref, g):
    own = value_ref[g, :NODES, :]
    x = node_x(NODES, CELLS)
    second = lax.broadcasted_iota(jnp.int32, (NODES, CELLS), 0) >= VXY
    place = lax.broadcasted_iota(jnp.int32, (CELLS, CELLS), 0)
    total = jnp.zeros((NODES, CELLS), jnp.float32)
    for face in range(FACES):
        row = jnp.concatenate([near[face : face + 1, :], near[FACES + face : FACES + face + 1, :]], axis=1)
        chosen = jnp.where(place == (row & (CELLS - 1)), 1.0, 0.0).astype(jnp.bfloat16)
        group = row >> 8
        found = None
        for s in range(GROUPS):
            both = jnp.dot(terms_ref[s], chosen, preferred_element_type=jnp.float32)
            got = both[:NODES] + both[NODES:]
            found = got if s == 0 else jnp.where(group == s, got, found)
        normal = [normal_ref[g, ROW_NORMAL + FACES * d + face : ROW_NORMAL + FACES * d + face + 1, :] for d in range(3)]
        fixed = [normal[1] * node_ref[0, y] + normal[2] * node_ref[0, 2] for y in range(2)]
        speed = normal[0] * x + jnp.where(second, fixed[1], fixed[0])
        total = total + speed * jnp.where(speed > 0.0, own, found)
    return total


def moment_table(node_ref, rows, cols):
    row = lax.broadcasted_iota(jnp.int32, (rows, cols), 0)
    col = lax.broadcasted_iota(jnp.int32, (rows, cols), 1)
    if rows > 8:
        row = jnp.where(col >= NODES, row - 6, jnp.where(row < 6, row, rows))
        col = col & (NODES - 1)
    x = ((col & (VXY - 1)).astype(jnp.float32) - (VXY - 1) / 2.0) * spacing
    y = jnp.where(col >= VXY, node_ref[0, 1], node_ref[0, 0])
    flat = x * x + y * y
    table = jnp.zeros((rows, cols), jnp.float32)
    picks = [jnp.ones_like(x), x, y, x * x, y * y, x * y]
    if rows == 8:
        picks += [x * flat, y * flat]
    for i, pick in enumerate(picks):
        table = jnp.where(row == i, pick, table)
    return table


def first_kernel(node_ref, block_ref, near_ref, flux_ref, sums_ref, terms_ref):
    table = moment_table(node_ref, 16, 2 * NODES)
    for g in range(GROUPS):
        split_terms(block_ref, terms_ref, g)

    def group(g, carry):
        near = neighbour_tiles(block_ref, g)
        near_ref[g] = near
        flux = transport(block_ref, terms_ref, block_ref, near, node_ref, g)
        flux_ref[g] = flux
        both = jnp.concatenate([block_ref[g, :NODES, :], flux], axis=0)
        sums = jnp.dot(table, both, precision=HIGHEST, preferred_element_type=jnp.float32)
        for half in range(2):
            for q in range(3):
                sums_ref[g * 2 + half, :, q * LANES : (q + 1) * LANES] = sums[
                    q * 4 : q * 4 + 4, half * LANES : (half + 1) * LANES
                ]
        return carry

    lax.fori_loop(0, GROUPS, group, 0)


def macroscopic(m):
    density = m[0]
    scale = 1.0 / density
    ux, uy, uz = m[1] * scale, m[2] * scale, m[3] * scale
    second = [m[4 + i] * scale for i in range(6)]
    txx = second[0] - ux * ux
    tyy = second[1] - uy * uy
    tzz = second[2] - uz * uz
    txy = second[3] - ux * uy
    txz = second[4] - ux * uz
    tyz = second[5] - uy * uz
    temper = (txx + tyy + tzz) / 3.0
    return density, (ux, uy, uz), second, (txx, tyy, tzz, txy, txz, tyz), temper


def coefficients(m):
    density, (ux, uy, uz), _, (txx, tyy, tzz, txy, txz, tyz), temper = macroscopic(m)
    iso = (1.0 - ellipsoid_mix) * temper
    lxx = iso + ellipsoid_mix * txx
    lyy = iso + ellipsoid_mix * tyy
    lzz = iso + ellipsoid_mix * tzz
    lxy = ellipsoid_mix * txy
    lxz = ellipsoid_mix * txz
    lyz = ellipsoid_mix * tyz
    cxx = lyy * lzz - lyz * lyz
    cxy = lyz * lxz - lxy * lzz
    cxz = lxy * lyz - lyy * lxz
    cyy = lxx * lzz - lxz * lxz
    cyz = lxy * lxz - lxx * lyz
    czz = lxx * lyy - lxy * lxy
    det = 1.0 / (lxx * cxx + lxy * cxy + lxz * cxz)
    inverse = (cxx * det, cyy * det, czz * det, cxy * det, cxz * det, cyz * det)
    collide = prandtl * density * jnp.exp(visc_power * jnp.log(temper))
    return density, (ux, uy, uz), inverse, collide


def factor_tables(mean, inverse, pair_ref, row_ref, col_ref):
    grid = level(lax.broadcasted_iota(jnp.int32, (VXY, LANES), 0).astype(jnp.float32))
    ixx, iyy, izz, ixy, ixz, iyz = inverse
    cx, cy, cz = grid - mean[0], grid - mean[1], grid - mean[2]
    own_x, own_y, own_z = -0.25 * ixx * cx * cx, -0.25 * iyy * cy * cy, -0.25 * izz * cz * cz
    cross_y = -ixy * cy
    cross_z = -ixz * cz
    cross_yz = -iyz * cy
    for i in range(VXY):
        x_own, x_c = own_x[i : i + 1, :], cx[i : i + 1, :]
        z_own, z_c = own_z[i : i + 1, :], cz[i : i + 1, :]
        pair_ref[i] = jnp.exp(x_own + own_y + x_c * cross_y)
        row_ref[i] = jnp.exp(x_own + own_z + x_c * cross_z)
        col_ref[i] = jnp.exp(z_own + own_y + z_c * cross_yz)


def column_sum(a):
    return jnp.sum(a, axis=0, keepdims=True)


def equilibrium_moments(mean, inverse, pair_ref, row_ref, col_ref):
    factor_tables(mean, inverse, pair_ref, row_ref, col_ref)
    zero = jnp.zeros((VXY, LANES), jnp.float32)

    def step(i, carry):
        s0, sx, sxx, s1, s1x, s2 = carry
        u0, u1, u2 = zero, zero, zero
        for k in range(VXY // 2):
            z = -level(k)
            low = row_ref[i, k : k + 1, :] * col_ref[k]
            high = row_ref[i, VXY - 1 - k : VXY - k, :] * col_ref[VXY - 1 - k]
            both = low + high
            u0 = u0 + both
            u1 = u1 + z * (high - low)
            u2 = u2 + (z * z) * both
        pair = pair_ref[i]
        x = level(lax.convert_element_type(i, jnp.float32))
        w0, w1 = pair * u0, pair * u1
        s0 = s0 + w0
        sx = sx + x * w0
        sxx = sxx + (x * x) * w0
        s1 = s1 + w1
        s1x = s1x + x * w1
        s2 = s2 + pair * u2
        return s0, sx, sxx, s1, s1x, s2

    s0, sx, sxx, s1, s1x, s2 = lax.fori_loop(0, VXY, step, (zero,) * 6)
    y = level(lax.broadcasted_iota(jnp.int32, (VXY, LANES), 0).astype(jnp.float32))
    return [
        column_sum(a)
        for a in (s0, sx, y * s0, s1, sxx, y * y * s0, s2, y * sx, s1x, y * s1)
    ]


def equilibrium_total(mean, inverse, pair_ref, row_ref, col_ref):
    factor_tables(mean, inverse, pair_ref, row_ref, col_ref)
    zero = jnp.zeros((VXY, LANES), jnp.float32)

    def step(i, total):
        u = zero
        for k in range(VXY):
            u = u + row_ref[i, k : k + 1, :] * col_ref[k]
        return total + pair_ref[i] * u

    return column_sum(lax.fori_loop(0, VXY, step, zero))


def put_rows(out_ref, base, mean, inverse, alpha, beta):
    ixx, iyy, izz, ixy, ixz, iyz = inverse
    lx = ixx * mean[0] + ixy * mean[1] + ixz * mean[2]
    ly = ixy * mean[0] + iyy * mean[1] + iyz * mean[2]
    lz = ixz * mean[0] + iyz * mean[1] + izz * mean[2]
    offset = mean[0] * lx + mean[1] * ly + mean[2] * lz
    rows = [ixx, iyy, izz, 2.0 * ixy, 2.0 * ixz, 2.0 * iyz, -2.0 * lx, -2.0 * ly, -2.0 * lz, offset, alpha, beta]
    for i, row in enumerate(rows):
        out_ref[base + i : base + i + 1, :] = row


def level_sums(parts_ref, orders):
    sums = [jnp.zeros(parts_ref.shape[1:], jnp.float32) for _ in range(orders)]
    for i in range(LEVELS):
        part = parts_ref[i]
        for order in range(orders):
            sums[order] = sums[order] + level(i) ** order * part
    return sums


def ten(row0, row1, row2):
    return [
        row0(0), row0(1), row0(2), row1(0), row0(3), row0(4), row2(0), row0(5), row1(1), row1(2),
    ]


def fields_kernel(parts_ref, out_ref, pair_ref, row_ref, col_ref):
    sums = level_sums(parts_ref, 3)

    def rows(base):
        def of(a):
            def row(i):
                i = base + i
                return a[i % 4 : i % 4 + 1, i // 4 * LANES : (i // 4 + 1) * LANES] / TOTAL

            return row

        return [of(a) for a in sums]

    now = ten(*rows(0))
    moved = ten(*rows(6))
    density, mean, inverse, collide = coefficients(now)
    gauss = equilibrium_moments(mean, inverse, pair_ref, row_ref, col_ref)
    beta = time_step * collide * density * TOTAL / gauss[0]
    alpha = 1.0 - time_step * collide
    put_rows(out_ref, 0, mean, inverse, alpha, beta)
    later = [alpha * a + beta * (e / TOTAL) - time_step * b for a, e, b in zip(now, gauss, moved)]
    density, mean, inverse, collide = coefficients(later)
    total = equilibrium_total(mean, inverse, pair_ref, row_ref, col_ref)
    beta = time_step * collide * density * TOTAL / total
    put_rows(out_ref, 12, mean, inverse, 1.0 - time_step * collide, beta)


def relaxed_tile(value, flux, params_ref, base, tile, node_ref):
    rows = [params_ref[tile, base + i : base + i + 1, :] for i in range(12)]
    ixx, iyy, izz, ixy, ixz, iyz, lx, ly, lz, offset, alpha, beta = rows
    vz = node_ref[0, 2]
    x = node_x(VXY, LANES)
    parts = []
    for y in range(2):
        vy = node_ref[0, y]
        slope = ixy * vy + ixz * vz + lx
        rest = (iyy * vy + iyz * vz + ly) * vy + (izz * vz + lz) * vz + offset
        energy = jnp.exp(-0.5 * ((ixx * x + slope) * x + rest))
        at = slice(y * VXY, (y + 1) * VXY)
        parts.append(alpha * value[at, :] + beta * energy - time_step * flux[at, :])
    return jnp.concatenate(parts, axis=0)


def second_kernel(node_ref, block_ref, near_ref, flux_ref, params_ref, out_ref, sums_ref, value_ref, terms_ref):
    table = moment_table(node_ref, 8, NODES)

    def first_step(g, carry):
        for half in range(2):
            at = slice(half * LANES, (half + 1) * LANES)
            value_ref[g, :, at] = relaxed_tile(
                block_ref[g, :NODES, at], flux_ref[g, :, at], params_ref, 0, g * 2 + half, node_ref
            )
        split_terms(value_ref, terms_ref, g)
        return carry

    lax.fori_loop(0, GROUPS, first_step, 0)

    def second_step(g, carry):
        flux = transport(value_ref, terms_ref, block_ref, near_ref[g], node_ref, g)
        for half in range(2):
            at = slice(half * LANES, (half + 1) * LANES)
            value = relaxed_tile(value_ref[g, :, at], flux[:, at], params_ref, 12, g * 2 + half, node_ref)
            out_ref[g, :, at] = value
            sums_ref[g * 2 + half] = jnp.dot(
                table, value, precision=HIGHEST, preferred_element_type=jnp.float32
            )
        return carry

    lax.fori_loop(0, GROUPS, second_step, 0)


def final_kernel(parts_ref, out_ref):
    def of(a):
        return lambda i: a[i : i + 1, :] / TOTAL

    row0, row1, row2, row3 = (of(a) for a in level_sums(parts_ref, 4))
    density, (ux, uy, uz), b, theta, _ = macroscopic(ten(row0, row1, row2))
    third = [row0(6) + row2(1), row0(7) + row2(2), row1(3) + row1(4) + row3(0)]
    trace = b[0] + b[1] + b[2]
    square = ux * ux + uy * uy + uz * uz
    stress = (
        b[0] * ux + b[3] * uy + b[4] * uz,
        b[3] * ux + b[1] * uy + b[5] * uz,
        b[4] * ux + b[5] * uy + b[2] * uz,
    )
    flux = [
        0.5 * (t / density - 2.0 * s - u * trace + 2.0 * u * square)
        for t, s, u in zip(third, stress, (ux, uy, uz))
    ]
    for i, value in enumerate((density, ux, uy, uz, *theta, *flux)):
        out_ref[i : i + 1, :] = value
    out_ref[13:16, :] = jnp.zeros((3, LANES), jnp.float32)


def shape(*dims, dtype=jnp.float32):
    return jax.ShapeDtypeStruct(dims, dtype)


VMEM = pl.BlockSpec(memory_space=pltpu.VMEM)
SMEM = pl.BlockSpec(memory_space=pltpu.SMEM)
TERMS = pltpu.VMEM((GROUPS, 2 * NODES, CELLS), jnp.bfloat16)
TABLES = [pltpu.VMEM((VXY, VXY, LANES), jnp.float32)] * 3


def spread(x, axes, count):
    copies = jnp.broadcast_to(x, (count, *x.shape))
    return lax.all_to_all(copies, axes, 0, 0, tiled=True)


def per_device(distribution, normals, adjacency, send_list, block_counts):
    z, x, y, c = (lax.axis_index(a) for a in ("z", "x", "y", "c"))
    vel = (x * 8 + y) * 2 + c
    row = (vel * 16 + z * 2) & (VXY - 1)
    node = jnp.stack([row, row + 1, vel // 2, vel // 2]).astype(jnp.float32)
    node = ((node - (VXY - 1) / 2.0) * spacing).reshape(1, 4)

    block = pl.pallas_call(
        pack_kernel,
        out_shape=shape(GROUPS, ROWS, CELLS),
        in_specs=[VMEM] * 5,
        out_specs=VMEM,
        compiler_params=PARAMS,
    )(distribution, adjacency, jnp.transpose(normals, (1, 0, 2)), send_list, block_counts.reshape(1, GROUPS))
    block = lax.all_to_all(block, "z", 0, 0, tiled=True)

    near, flux, sums = pl.pallas_call(
        first_kernel,
        out_shape=(
            shape(GROUPS, 8, LANES, dtype=jnp.int32),
            shape(GROUPS, NODES, CELLS),
            shape(TILES, 4, 3 * LANES),
        ),
        in_specs=[SMEM, VMEM],
        out_specs=(VMEM, VMEM, VMEM),
        scratch_shapes=[TERMS],
        compiler_params=PARAMS,
    )(node, block)

    mine = jnp.sum(lax.all_to_all(sums, ("z", "c"), 0, 0, tiled=True), axis=0)
    params = pl.pallas_call(
        fields_kernel,
        out_shape=shape(24, LANES),
        in_specs=[VMEM],
        out_specs=VMEM,
        scratch_shapes=TABLES,
        compiler_params=PARAMS,
    )(spread(mine, ("x", "y"), LEVELS))
    params = spread(params, ("z", "c"), TILES)

    value, sums = pl.pallas_call(
        second_kernel,
        out_shape=(shape(GROUPS, NODES, CELLS), shape(TILES, 8, LANES)),
        in_specs=[SMEM, VMEM, VMEM, VMEM, VMEM],
        out_specs=(VMEM, VMEM),
        scratch_shapes=[pltpu.VMEM((GROUPS, NODES, CELLS), jnp.float32), TERMS],
        compiler_params=PARAMS,
    )(node, block, near, flux, params)

    relaxed = lax.all_to_all(value, "z", 0, 0, tiled=True).reshape(GROUPS * NODES, CELLS)
    mine = jnp.sum(lax.all_to_all(sums, ("z", "c"), 0, 0, tiled=True), axis=0)
    fields = pl.pallas_call(
        final_kernel,
        out_shape=shape(16, LANES),
        in_specs=[VMEM],
        out_specs=VMEM,
        compiler_params=PARAMS,
    )(spread(mine, ("x", "y"), LEVELS))
    other = lax.ppermute(fields, "c", [(0, 1), (1, 0)])
    fields = jnp.where(
        c == 0, jnp.concatenate([fields, other], axis=1), jnp.concatenate([other, fields], axis=1)
    )
    return relaxed, fields[:13]


def solution(mesh):
    split = Mesh(mesh.devices.reshape(8, 4, 8, 2), ("z", "x", "y", "c"))
    vel = ("x", "y", "c")
    placed = (P(vel, "z"), P(None, None, "z"), P(None, "z"), P("z", None, None), P(None, "z"))
    return jax.shard_map(
        per_device,
        mesh=split,
        in_specs=placed,
        out_specs=(P(vel, "z"), P(None, "z")),
        check_vma=False,
    )
```

```python
import jax
import jax.numpy as jnp
from jax import lax
from jax.experimental import pallas as pl
from jax.experimental.pallas import tpu as pltpu
from jax.sharding import Mesh, PartitionSpec as P

VXY = 32
TILE = 128
CELLS = 256
GROUPS = 8
NODES = 64
LANES = 128
TILES = 16
LEVELS = 32
FACES = 4
TOTAL = 32768

spacing = 0.3
ellipsoid_mix = -0.25
prandtl = 0.8
visc_power = 0.26
time_step = 0.025

ROW_ADJ = NODES
ROW_NORMAL = ROW_ADJ + FACES
ROW_SEND = ROW_NORMAL + 3 * FACES
ROWS = ROW_SEND + GROUPS

PARAMS = pltpu.CompilerParams(vmem_limit_bytes=48 * 1024 * 1024)


def level(i):
    return (i - (VXY - 1) / 2.0) * spacing


def take_lanes(values, lanes):
    return jnp.take_along_axis(values, lanes, axis=1, mode="promise_in_bounds")


def node_x(rows, lanes):
    row = lax.broadcasted_iota(jnp.int32, (rows, lanes), 0)
    return ((row & (VXY - 1)).astype(jnp.float32) - (VXY - 1) / 2.0) * spacing


def pack_kernel(
    value_hbm, adjacency_hbm, normal_hbm, send_hbm, count_hbm, out_hbm,
    adjacency_ref, normal_ref, send_ref, count_ref, rows_ref, in_sem, value_sem, rows_sem,
):
    pairs = (
        (count_hbm, count_ref), (adjacency_hbm, adjacency_ref), (normal_hbm, normal_ref), (send_hbm, send_ref),
    )
    small = [pltpu.make_async_copy(a, b, in_sem.at[i]) for i, (a, b) in enumerate(pairs)]
    for copy in small:
        copy.start()
    large = [
        pltpu.make_async_copy(
            value_hbm.at[pl.ds(g * NODES, NODES), :], out_hbm.at[g, pl.ds(0, NODES), :], value_sem.at[g]
        )
        for g in range(GROUPS)
    ]
    for copy in large:
        copy.start()
    for copy in small:
        copy.wait()
    adj = adjacency_ref[...]
    place = adj - CELLS
    counts = count_ref[...] * TILE
    end = jnp.zeros((1, 1), jnp.int32)
    source = jnp.zeros(adj.shape, jnp.int32)
    start = jnp.zeros(adj.shape, jnp.int32)
    for s in range(GROUPS - 1):
        end = end + counts[:, s : s + 1]
        past = end <= place
        source = source + jnp.where(past, 1, 0)
        start = jnp.where(past, end, start)
    slot = jnp.clip(place - start, 0, CELLS - 1)
    rows = [jnp.where(adj < CELLS, adj, CELLS + CELLS * source + slot).astype(jnp.float32)]
    rows += [normal_ref[d] for d in range(3)]
    rows_ref[...] = jnp.concatenate(rows + [send_ref[0].astype(jnp.float32)], axis=0)
    shared = [
        pltpu.make_async_copy(rows_ref, out_hbm.at[g, pl.ds(NODES, ROWS - NODES), :], rows_sem.at[g])
        for g in range(GROUPS)
    ]
    for copy in shared:
        copy.start()
    for copy in large + shared:
        copy.wait()


def find_neighbours(block_ref, near_ref):
    base = CELLS * lax.broadcasted_iota(jnp.int32, (GROUPS, LANES), 0)
    for face in range(FACES):
        for half in range(2):
            at = slice(half * LANES, (half + 1) * LANES)
            adj = jnp.concatenate(
                [block_ref[g, ROW_ADJ + face : ROW_ADJ + face + 1, at] for g in range(GROUPS)], axis=0
            ).astype(jnp.int32)
            place = jnp.maximum(adj - CELLS, 0)
            table = place >> 7
            lane = place & (LANES - 1)
            listed = jnp.zeros(adj.shape, jnp.float32)
            for s in range(GROUPS):
                for part in range(2):
                    rows = block_ref[s, ROW_SEND : ROW_SEND + GROUPS, part * LANES : (part + 1) * LANES]
                    listed = jnp.where(table == s * 2 + part, take_lanes(rows, lane), listed)
            far = (place >> 8) * CELLS + listed.astype(jnp.int32)
            near = jnp.where(adj < CELLS, adj + base, far)
            for g in range(GROUPS):
                near_ref[g, face : face + 1, at] = near[g : g + 1, :]


def split_terms(value_ref, terms_ref, g):
    value = value_ref[g, :NODES, :]
    high = value.astype(jnp.bfloat16)
    terms_ref[g, :NODES, :] = high
    terms_ref[g, NODES:, :] = (value - high.astype(jnp.float32)).astype(jnp.bfloat16)


def transport(value_ref, terms_ref, normal_ref, near, node_ref, g):
    own = value_ref[g, :NODES, :]
    x = node_x(NODES, CELLS)
    second = lax.broadcasted_iota(jnp.int32, (NODES, CELLS), 0) >= VXY
    place = lax.broadcasted_iota(jnp.int32, (CELLS, CELLS), 0)
    total = jnp.zeros((NODES, CELLS), jnp.float32)
    for face in range(FACES):
        row = near[face : face + 1, :]
        chosen = jnp.where(place == (row & (CELLS - 1)), 1.0, 0.0).astype(jnp.bfloat16)
        group = row >> 8
        found = None
        for s in range(GROUPS):
            both = jnp.dot(terms_ref[s], chosen, preferred_element_type=jnp.float32)
            got = both[:NODES] + both[NODES:]
            found = got if s == 0 else jnp.where(group == s, got, found)
        normal = [normal_ref[g, ROW_NORMAL + FACES * d + face : ROW_NORMAL + FACES * d + face + 1, :] for d in range(3)]
        fixed = [normal[1] * node_ref[0, y] + normal[2] * node_ref[0, 2] for y in range(2)]
        speed = normal[0] * x + jnp.where(second, fixed[1], fixed[0])
        total = total + speed * jnp.where(speed > 0.0, own, found)
    return total


def plane_sums(value, node_ref, third):
    x = node_x(VXY, value.shape[1])
    sums = []
    for y in range(2):
        part = value[y * VXY : (y + 1) * VXY, :]
        powers = [part]
        for _ in range(3 if third else 2):
            powers.append(x * powers[-1])
        sums.append([column_sum(p) for p in powers])
    low, high = sums
    ya, yb = node_ref[0, 0], node_ref[0, 1]

    def over(i, order=0):
        return ya**order * low[i] + yb**order * high[i] if order else low[i] + high[i]

    rows = [over(0), over(1), over(0, 1), over(2), over(0, 2), over(1, 1)]
    if third:
        rows += [over(3) + over(1, 2), over(2, 1) + over(0, 3)]
    return rows


def first_kernel(node_ref, block_ref, near_ref, flux_ref, sums_ref, terms_ref):
    find_neighbours(block_ref, near_ref)
    for g in range(GROUPS):
        split_terms(block_ref, terms_ref, g)

    def group(g, carry):
        flux = transport(block_ref, terms_ref, block_ref, near_ref[g], node_ref, g)
        flux_ref[g] = flux
        rows = plane_sums(block_ref[g, :NODES, :], node_ref, False) + plane_sums(flux, node_ref, False)
        for i, row in enumerate(rows):
            for half in range(2):
                q = i // 4
                sums_ref[g * 2 + half, i % 4 : i % 4 + 1, q * LANES : (q + 1) * LANES] = row[
                    :, half * LANES : (half + 1) * LANES
                ]
        return carry

    lax.fori_loop(0, GROUPS, group, 0)


def macroscopic(m):
    density = m[0]
    scale = 1.0 / density
    ux, uy, uz = m[1] * scale, m[2] * scale, m[3] * scale
    second = [m[4 + i] * scale for i in range(6)]
    txx = second[0] - ux * ux
    tyy = second[1] - uy * uy
    tzz = second[2] - uz * uz
    txy = second[3] - ux * uy
    txz = second[4] - ux * uz
    tyz = second[5] - uy * uz
    temper = (txx + tyy + tzz) / 3.0
    return density, (ux, uy, uz), second, (txx, tyy, tzz, txy, txz, tyz), temper


def coefficients(m):
    density, (ux, uy, uz), _, (txx, tyy, tzz, txy, txz, tyz), temper = macroscopic(m)
    iso = (1.0 - ellipsoid_mix) * temper
    lxx = iso + ellipsoid_mix * txx
    lyy = iso + ellipsoid_mix * tyy
    lzz = iso + ellipsoid_mix * tzz
    lxy = ellipsoid_mix * txy
    lxz = ellipsoid_mix * txz
    lyz = ellipsoid_mix * tyz
    cxx = lyy * lzz - lyz * lyz
    cxy = lyz * lxz - lxy * lzz
    cxz = lxy * lyz - lyy * lxz
    cyy = lxx * lzz - lxz * lxz
    cyz = lxy * lxz - lxx * lyz
    czz = lxx * lyy - lxy * lxy
    det = 1.0 / (lxx * cxx + lxy * cxy + lxz * cxz)
    inverse = (cxx * det, cyy * det, czz * det, cxy * det, cxz * det, cyz * det)
    collide = prandtl * density * jnp.exp(visc_power * jnp.log(temper))
    return density, (ux, uy, uz), inverse, collide


def factor_tables(mean, inverse, pair_ref, row_ref, col_ref):
    grid = level(lax.broadcasted_iota(jnp.int32, (VXY, LANES), 0).astype(jnp.float32))
    ixx, iyy, izz, ixy, ixz, iyz = inverse
    cx, cy, cz = grid - mean[0], grid - mean[1], grid - mean[2]
    own_x, own_y, own_z = -0.25 * ixx * cx * cx, -0.25 * iyy * cy * cy, -0.25 * izz * cz * cz
    cross_y = -ixy * cy
    cross_z = -ixz * cz
    cross_yz = -iyz * cy
    for i in range(VXY):
        x_own, x_c = own_x[i : i + 1, :], cx[i : i + 1, :]
        z_own, z_c = own_z[i : i + 1, :], cz[i : i + 1, :]
        pair_ref[i] = jnp.exp(x_own + own_y + x_c * cross_y)
        row_ref[i] = jnp.exp(x_own + own_z + x_c * cross_z)
        col_ref[i] = jnp.exp(z_own + own_y + z_c * cross_yz)


def column_sum(a):
    return jnp.sum(a, axis=0, keepdims=True)


def equilibrium_moments(mean, inverse, pair_ref, row_ref, col_ref):
    factor_tables(mean, inverse, pair_ref, row_ref, col_ref)
    zero = jnp.zeros((VXY, LANES), jnp.float32)

    def step(i, carry):
        s0, sx, sxx, s1, s1x, s2 = carry
        u0, u1, u2 = zero, zero, zero
        for k in range(VXY // 2):
            z = -level(k)
            low = row_ref[i, k : k + 1, :] * col_ref[k]
            high = row_ref[i, VXY - 1 - k : VXY - k, :] * col_ref[VXY - 1 - k]
            both = low + high
            u0 = u0 + both
            u1 = u1 + z * (high - low)
            u2 = u2 + (z * z) * both
        pair = pair_ref[i]
        x = level(lax.convert_element_type(i, jnp.float32))
        w0, w1 = pair * u0, pair * u1
        s0 = s0 + w0
        sx = sx + x * w0
        sxx = sxx + (x * x) * w0
        s1 = s1 + w1
        s1x = s1x + x * w1
        s2 = s2 + pair * u2
        return s0, sx, sxx, s1, s1x, s2

    s0, sx, sxx, s1, s1x, s2 = lax.fori_loop(0, VXY, step, (zero,) * 6)
    y = level(lax.broadcasted_iota(jnp.int32, (VXY, LANES), 0).astype(jnp.float32))
    return [
        column_sum(a)
        for a in (s0, sx, y * s0, s1, sxx, y * y * s0, s2, y * sx, s1x, y * s1)
    ]


def equilibrium_total(mean, inverse, pair_ref, row_ref, col_ref):
    factor_tables(mean, inverse, pair_ref, row_ref, col_ref)
    zero = jnp.zeros((VXY, LANES), jnp.float32)

    def step(i, total):
        u = zero
        for k in range(VXY):
            u = u + row_ref[i, k : k + 1, :] * col_ref[k]
        return total + pair_ref[i] * u

    return column_sum(lax.fori_loop(0, VXY, step, zero))


def put_rows(out_ref, base, mean, inverse, alpha, beta):
    ixx, iyy, izz, ixy, ixz, iyz = inverse
    lx = ixx * mean[0] + ixy * mean[1] + ixz * mean[2]
    ly = ixy * mean[0] + iyy * mean[1] + iyz * mean[2]
    lz = ixz * mean[0] + iyz * mean[1] + izz * mean[2]
    offset = mean[0] * lx + mean[1] * ly + mean[2] * lz
    rows = [ixx, iyy, izz, 2.0 * ixy, 2.0 * ixz, 2.0 * iyz, -2.0 * lx, -2.0 * ly, -2.0 * lz, offset, alpha, beta]
    for i, row in enumerate(rows):
        out_ref[base + i : base + i + 1, :] = row


def level_sums(parts_ref, orders):
    sums = [jnp.zeros(parts_ref.shape[1:], jnp.float32) for _ in range(orders)]
    for i in range(LEVELS):
        part = parts_ref[i]
        for order in range(orders):
            sums[order] = sums[order] + level(i) ** order * part
    return sums


def ten(row0, row1, row2):
    return [
        row0(0), row0(1), row0(2), row1(0), row0(3), row0(4), row2(0), row0(5), row1(1), row1(2),
    ]


def fields_kernel(parts_ref, out_ref, pair_ref, row_ref, col_ref):
    sums = level_sums(parts_ref, 3)

    def rows(base):
        def of(a):
            def row(i):
                i = base + i
                return a[i % 4 : i % 4 + 1, i // 4 * LANES : (i // 4 + 1) * LANES] / TOTAL

            return row

        return [of(a) for a in sums]

    now = ten(*rows(0))
    moved = ten(*rows(6))
    density, mean, inverse, collide = coefficients(now)
    gauss = equilibrium_moments(mean, inverse, pair_ref, row_ref, col_ref)
    beta = time_step * collide * density * TOTAL / gauss[0]
    alpha = 1.0 - time_step * collide
    put_rows(out_ref, 0, mean, inverse, alpha, beta)
    later = [alpha * a + beta * (e / TOTAL) - time_step * b for a, e, b in zip(now, gauss, moved)]
    density, mean, inverse, collide = coefficients(later)
    total = equilibrium_total(mean, inverse, pair_ref, row_ref, col_ref)
    beta = time_step * collide * density * TOTAL / total
    put_rows(out_ref, 12, mean, inverse, 1.0 - time_step * collide, beta)


def relaxed_tile(value, flux, params_ref, base, tile, node_ref):
    rows = [params_ref[tile, base + i : base + i + 1, :] for i in range(12)]
    ixx, iyy, izz, ixy, ixz, iyz, lx, ly, lz, offset, alpha, beta = rows
    vz = node_ref[0, 2]
    x = node_x(VXY, LANES)
    parts = []
    for y in range(2):
        vy = node_ref[0, y]
        slope = ixy * vy + ixz * vz + lx
        rest = (iyy * vy + iyz * vz + ly) * vy + (izz * vz + lz) * vz + offset
        energy = jnp.exp(-0.5 * ((ixx * x + slope) * x + rest))
        at = slice(y * VXY, (y + 1) * VXY)
        parts.append(alpha * value[at, :] + beta * energy - time_step * flux[at, :])
    return jnp.concatenate(parts, axis=0)


def second_kernel(node_ref, block_ref, near_ref, flux_ref, params_ref, out_ref, sums_ref, value_ref, terms_ref):
    def first_step(g, carry):
        for half in range(2):
            at = slice(half * LANES, (half + 1) * LANES)
            value_ref[g, :, at] = relaxed_tile(
                block_ref[g, :NODES, at], flux_ref[g, :, at], params_ref, 0, g * 2 + half, node_ref
            )
        split_terms(value_ref, terms_ref, g)
        return carry

    lax.fori_loop(0, GROUPS, first_step, 0)

    def second_step(g, carry):
        flux = transport(value_ref, terms_ref, block_ref, near_ref[g], node_ref, g)
        for half in range(2):
            at = slice(half * LANES, (half + 1) * LANES)
            value = relaxed_tile(value_ref[g, :, at], flux[:, at], params_ref, 12, g * 2 + half, node_ref)
            out_ref[g, :, at] = value
            for i, row in enumerate(plane_sums(value, node_ref, True)):
                sums_ref[g * 2 + half, i : i + 1, :] = row
        return carry

    lax.fori_loop(0, GROUPS, second_step, 0)


def final_kernel(parts_ref, out_ref):
    def of(a):
        return lambda i: a[i : i + 1, :] / TOTAL

    row0, row1, row2, row3 = (of(a) for a in level_sums(parts_ref, 4))
    density, (ux, uy, uz), b, theta, _ = macroscopic(ten(row0, row1, row2))
    third = [row0(6) + row2(1), row0(7) + row2(2), row1(3) + row1(4) + row3(0)]
    trace = b[0] + b[1] + b[2]
    square = ux * ux + uy * uy + uz * uz
    stress = (
        b[0] * ux + b[3] * uy + b[4] * uz,
        b[3] * ux + b[1] * uy + b[5] * uz,
        b[4] * ux + b[5] * uy + b[2] * uz,
    )
    flux = [
        0.5 * (t / density - 2.0 * s - u * trace + 2.0 * u * square)
        for t, s, u in zip(third, stress, (ux, uy, uz))
    ]
    for i, value in enumerate((density, ux, uy, uz, *theta, *flux)):
        out_ref[i : i + 1, :] = value
    out_ref[13:16, :] = jnp.zeros((3, LANES), jnp.float32)


def shape(*dims, dtype=jnp.float32):
    return jax.ShapeDtypeStruct(dims, dtype)


VMEM = pl.BlockSpec(memory_space=pltpu.VMEM)
ANY = pl.BlockSpec(memory_space=pl.ANY)
SMEM = pl.BlockSpec(memory_space=pltpu.SMEM)
TERMS = pltpu.VMEM((GROUPS, 2 * NODES, CELLS), jnp.bfloat16)
TABLES = [pltpu.VMEM((VXY, VXY, LANES), jnp.float32)] * 3


def spread(x, axes, count):
    copies = jnp.broadcast_to(x, (count, *x.shape))
    return lax.all_to_all(copies, axes, 0, 0, tiled=True)


def per_device(distribution, normals, adjacency, send_list, block_counts):
    z, x, y, c = (lax.axis_index(a) for a in ("z", "x", "y", "c"))
    vel = (x * 8 + y) * 2 + c
    row = (vel * 16 + z * 2) & (VXY - 1)
    node = jnp.stack([row, row + 1, vel // 2, vel // 2]).astype(jnp.float32)
    node = ((node - (VXY - 1) / 2.0) * spacing).reshape(1, 4)

    block = pl.pallas_call(
        pack_kernel,
        out_shape=shape(GROUPS, ROWS, CELLS),
        in_specs=[ANY] * 5,
        out_specs=ANY,
        scratch_shapes=[
            pltpu.VMEM((FACES, CELLS), jnp.int32),
            pltpu.VMEM((3, FACES, CELLS), jnp.float32),
            pltpu.VMEM((1, GROUPS, CELLS), jnp.int32),
            pltpu.VMEM((1, GROUPS), jnp.int32),
            pltpu.VMEM((ROWS - NODES, CELLS), jnp.float32),
            pltpu.SemaphoreType.DMA((4,)),
            pltpu.SemaphoreType.DMA((GROUPS,)),
            pltpu.SemaphoreType.DMA((GROUPS,)),
        ],
        compiler_params=pltpu.CompilerParams(vmem_limit_bytes=60 * 1024 * 1024),
    )(distribution, adjacency, jnp.transpose(normals, (1, 0, 2)), send_list, block_counts.reshape(1, GROUPS))
    block = lax.all_to_all(block, "z", 0, 0, tiled=True)

    near, flux, sums = pl.pallas_call(
        first_kernel,
        out_shape=(
            shape(GROUPS, FACES, CELLS, dtype=jnp.int32),
            shape(GROUPS, NODES, CELLS),
            shape(TILES, 4, 3 * LANES),
        ),
        in_specs=[SMEM, VMEM],
        out_specs=(VMEM, VMEM, VMEM),
        scratch_shapes=[TERMS],
        compiler_params=PARAMS,
    )(node, block)

    mine = jnp.sum(lax.all_to_all(sums, ("z", "c"), 0, 0, tiled=True), axis=0)
    params = pl.pallas_call(
        fields_kernel,
        out_shape=shape(24, LANES),
        in_specs=[VMEM],
        out_specs=VMEM,
        scratch_shapes=TABLES,
        compiler_params=PARAMS,
    )(spread(mine, ("x", "y"), LEVELS))
    params = spread(params, ("z", "c"), TILES)

    value, sums = pl.pallas_call(
        second_kernel,
        out_shape=(shape(GROUPS, NODES, CELLS), shape(TILES, 8, LANES)),
        in_specs=[SMEM, VMEM, VMEM, VMEM, VMEM],
        out_specs=(VMEM, VMEM),
        scratch_shapes=[pltpu.VMEM((GROUPS, NODES, CELLS), jnp.float32), TERMS],
        compiler_params=PARAMS,
    )(node, block, near, flux, params)

    relaxed = lax.all_to_all(value, "z", 0, 0, tiled=True).reshape(GROUPS * NODES, CELLS)
    mine = jnp.sum(lax.all_to_all(sums, ("z", "c"), 0, 0, tiled=True), axis=0)
    fields = pl.pallas_call(
        final_kernel,
        out_shape=shape(16, LANES),
        in_specs=[VMEM],
        out_specs=VMEM,
        compiler_params=PARAMS,
    )(spread(mine, ("x", "y"), LEVELS))
    other = lax.ppermute(fields, "c", [(0, 1), (1, 0)])
    fields = jnp.where(
        c == 0, jnp.concatenate([fields, other], axis=1), jnp.concatenate([other, fields], axis=1)
    )
    return relaxed, fields[:13]


def solution(mesh):
    split = Mesh(mesh.devices.reshape(8, 4, 8, 2), ("z", "x", "y", "c"))
    vel = ("x", "y", "c")
    placed = (P(vel, "z"), P(None, None, "z"), P(None, "z"), P("z", None, None), P(None, "z"))
    return jax.shard_map(
        per_device,
        mesh=split,
        in_specs=placed,
        out_specs=(P(vel, "z"), P(None, "z")),
        check_vma=False,
    )
```

```python
import jax
import jax.numpy as jnp
from jax import lax
from jax.experimental import pallas as pl
from jax.experimental.pallas import tpu as pltpu
from jax.sharding import Mesh, PartitionSpec as P

VXY = 32
TILE = 128
CELLS = 256
GROUPS = 8
NODES = 64
LANES = 128
TILES = 16
LEVELS = 32
FACES = 4
TOTAL = 32768

spacing = 0.3
ellipsoid_mix = -0.25
prandtl = 0.8
visc_power = 0.26
time_step = 0.025

ROW_ADJ = NODES
ROW_NORMAL = ROW_ADJ + FACES
ROW_SEND = ROW_NORMAL + 3 * FACES
ROWS = ROW_SEND + GROUPS

PARAMS = pltpu.CompilerParams(vmem_limit_bytes=48 * 1024 * 1024)


def level(i):
    return (i - (VXY - 1) / 2.0) * spacing


def take_lanes(values, lanes):
    return jnp.take_along_axis(values, lanes, axis=1, mode="promise_in_bounds")


def node_x(rows, lanes):
    row = lax.broadcasted_iota(jnp.int32, (rows, lanes), 0)
    return ((row & (VXY - 1)).astype(jnp.float32) - (VXY - 1) / 2.0) * spacing


def pack_kernel(
    value_hbm, adjacency_hbm, normal_hbm, send_hbm, count_hbm, out_ref,
    adjacency_ref, normal_ref, send_ref, count_ref, in_sem, value_sem,
):
    pairs = (
        (count_hbm, count_ref), (adjacency_hbm, adjacency_ref), (normal_hbm, normal_ref), (send_hbm, send_ref),
    )
    small = [pltpu.make_async_copy(a, b, in_sem.at[i]) for i, (a, b) in enumerate(pairs)]
    for copy in small:
        copy.start()
    large = [
        pltpu.make_async_copy(
            value_hbm.at[pl.ds(g * NODES, NODES), :], out_ref.at[g, pl.ds(0, NODES), :], value_sem.at[g]
        )
        for g in range(GROUPS)
    ]
    for copy in large:
        copy.start()
    for copy in small:
        copy.wait()
    adj = adjacency_ref[...]
    place = adj - CELLS
    counts = count_ref[...] * TILE
    end = jnp.zeros((1, 1), jnp.int32)
    source = jnp.zeros(adj.shape, jnp.int32)
    start = jnp.zeros(adj.shape, jnp.int32)
    for s in range(GROUPS - 1):
        end = end + counts[:, s : s + 1]
        past = end <= place
        source = source + jnp.where(past, 1, 0)
        start = jnp.where(past, end, start)
    slot = jnp.clip(place - start, 0, CELLS - 1)
    rows = [jnp.where(adj < CELLS, adj, CELLS + CELLS * source + slot).astype(jnp.float32)]
    rows += [normal_ref[d] for d in range(3)]
    rows = jnp.concatenate(rows + [send_ref[0].astype(jnp.float32)], axis=0)
    for g in range(GROUPS):
        out_ref[g, NODES:, :] = rows
    for copy in large:
        copy.wait()


def find_neighbours(block_ref, near_ref):
    base = CELLS * lax.broadcasted_iota(jnp.int32, (GROUPS, LANES), 0)
    for face in range(FACES):
        for half in range(2):
            at = slice(half * LANES, (half + 1) * LANES)
            adj = jnp.concatenate(
                [block_ref[g, ROW_ADJ + face : ROW_ADJ + face + 1, at] for g in range(GROUPS)], axis=0
            ).astype(jnp.int32)
            place = jnp.maximum(adj - CELLS, 0)
            table = place >> 7
            lane = place & (LANES - 1)
            listed = jnp.zeros(adj.shape, jnp.float32)
            for s in range(GROUPS):
                for part in range(2):
                    rows = block_ref[s, ROW_SEND : ROW_SEND + GROUPS, part * LANES : (part + 1) * LANES]
                    listed = jnp.where(table == s * 2 + part, take_lanes(rows, lane), listed)
            far = (place >> 8) * CELLS + listed.astype(jnp.int32)
            near = jnp.where(adj < CELLS, adj + base, far)
            for g in range(GROUPS):
                near_ref[g, face : face + 1, at] = near[g : g + 1, :]


def split_terms(value_ref, terms_ref, g):
    value = value_ref[g, :NODES, :]
    high = value.astype(jnp.bfloat16)
    terms_ref[g, :NODES, :] = high
    terms_ref[g, NODES:, :] = (value - high.astype(jnp.float32)).astype(jnp.bfloat16)


def transport(value_ref, terms_ref, normal_ref, near, node_ref, g):
    own = value_ref[g, :NODES, :]
    x = node_x(NODES, CELLS)
    second = lax.broadcasted_iota(jnp.int32, (NODES, CELLS), 0) >= VXY
    place = lax.broadcasted_iota(jnp.int32, (CELLS, CELLS), 0)
    total = jnp.zeros((NODES, CELLS), jnp.float32)
    for face in range(FACES):
        row = near[face : face + 1, :]
        chosen = jnp.where(place == (row & (CELLS - 1)), 1.0, 0.0).astype(jnp.bfloat16)
        group = row >> 8
        found = None
        for s in range(GROUPS):
            both = jnp.dot(terms_ref[s], chosen, preferred_element_type=jnp.float32)
            got = both[:NODES] + both[NODES:]
            found = got if s == 0 else jnp.where(group == s, got, found)
        normal = [normal_ref[g, ROW_NORMAL + FACES * d + face : ROW_NORMAL + FACES * d + face + 1, :] for d in range(3)]
        fixed = [normal[1] * node_ref[0, y] + normal[2] * node_ref[0, 2] for y in range(2)]
        speed = normal[0] * x + jnp.where(second, fixed[1], fixed[0])
        total = total + speed * jnp.where(speed > 0.0, own, found)
    return total


def plane_sums(value, node_ref, third):
    x = node_x(VXY, value.shape[1])
    sums = []
    for y in range(2):
        part = value[y * VXY : (y + 1) * VXY, :]
        powers = [part]
        for _ in range(3 if third else 2):
            powers.append(x * powers[-1])
        sums.append([column_sum(p) for p in powers])
    low, high = sums
    ya, yb = node_ref[0, 0], node_ref[0, 1]

    def over(i, order=0):
        return ya**order * low[i] + yb**order * high[i] if order else low[i] + high[i]

    rows = [over(0), over(1), over(0, 1), over(2), over(0, 2), over(1, 1)]
    if third:
        rows += [over(3) + over(1, 2), over(2, 1) + over(0, 3)]
    return rows


def first_kernel(node_ref, block_ref, near_ref, flux_ref, sums_ref, terms_ref):
    find_neighbours(block_ref, near_ref)
    for g in range(GROUPS):
        split_terms(block_ref, terms_ref, g)

    def group(g, carry):
        flux = transport(block_ref, terms_ref, block_ref, near_ref[g], node_ref, g)
        flux_ref[g] = flux
        rows = plane_sums(block_ref[g, :NODES, :], node_ref, False) + plane_sums(flux, node_ref, False)
        for i, row in enumerate(rows):
            for half in range(2):
                q = i // 4
                sums_ref[g * 2 + half, i % 4 : i % 4 + 1, q * LANES : (q + 1) * LANES] = row[
                    :, half * LANES : (half + 1) * LANES
                ]
        return carry

    lax.fori_loop(0, GROUPS, group, 0)


def macroscopic(m):
    density = m[0]
    scale = 1.0 / density
    ux, uy, uz = m[1] * scale, m[2] * scale, m[3] * scale
    second = [m[4 + i] * scale for i in range(6)]
    txx = second[0] - ux * ux
    tyy = second[1] - uy * uy
    tzz = second[2] - uz * uz
    txy = second[3] - ux * uy
    txz = second[4] - ux * uz
    tyz = second[5] - uy * uz
    temper = (txx + tyy + tzz) / 3.0
    return density, (ux, uy, uz), second, (txx, tyy, tzz, txy, txz, tyz), temper


def coefficients(m):
    density, (ux, uy, uz), _, (txx, tyy, tzz, txy, txz, tyz), temper = macroscopic(m)
    iso = (1.0 - ellipsoid_mix) * temper
    lxx = iso + ellipsoid_mix * txx
    lyy = iso + ellipsoid_mix * tyy
    lzz = iso + ellipsoid_mix * tzz
    lxy = ellipsoid_mix * txy
    lxz = ellipsoid_mix * txz
    lyz = ellipsoid_mix * tyz
    cxx = lyy * lzz - lyz * lyz
    cxy = lyz * lxz - lxy * lzz
    cxz = lxy * lyz - lyy * lxz
    cyy = lxx * lzz - lxz * lxz
    cyz = lxy * lxz - lxx * lyz
    czz = lxx * lyy - lxy * lxy
    det = 1.0 / (lxx * cxx + lxy * cxy + lxz * cxz)
    inverse = (cxx * det, cyy * det, czz * det, cxy * det, cxz * det, cyz * det)
    collide = prandtl * density * jnp.exp(visc_power * jnp.log(temper))
    return density, (ux, uy, uz), inverse, collide


def factor_tables(mean, inverse, pair_ref, row_ref, col_ref):
    grid = level(lax.broadcasted_iota(jnp.int32, (VXY, LANES), 0).astype(jnp.float32))
    ixx, iyy, izz, ixy, ixz, iyz = inverse
    cx, cy, cz = grid - mean[0], grid - mean[1], grid - mean[2]
    own_x, own_y, own_z = -0.25 * ixx * cx * cx, -0.25 * iyy * cy * cy, -0.25 * izz * cz * cz
    cross_y = -ixy * cy
    cross_z = -ixz * cz
    cross_yz = -iyz * cy
    for i in range(VXY):
        x_own, x_c = own_x[i : i + 1, :], cx[i : i + 1, :]
        z_own, z_c = own_z[i : i + 1, :], cz[i : i + 1, :]
        pair_ref[i] = jnp.exp(x_own + own_y + x_c * cross_y)
        row_ref[i] = jnp.exp(x_own + own_z + x_c * cross_z)
        col_ref[i] = jnp.exp(z_own + own_y + z_c * cross_yz)


def column_sum(a):
    return jnp.sum(a, axis=0, keepdims=True)


def equilibrium_moments(mean, inverse, pair_ref, row_ref, col_ref):
    factor_tables(mean, inverse, pair_ref, row_ref, col_ref)
    zero = jnp.zeros((VXY, LANES), jnp.float32)

    def step(i, carry):
        s0, sx, sxx, s1, s1x, s2 = carry
        u0, u1, u2 = zero, zero, zero
        for k in range(VXY // 2):
            z = -level(k)
            low = row_ref[i, k : k + 1, :] * col_ref[k]
            high = row_ref[i, VXY - 1 - k : VXY - k, :] * col_ref[VXY - 1 - k]
            both = low + high
            u0 = u0 + both
            u1 = u1 + z * (high - low)
            u2 = u2 + (z * z) * both
        pair = pair_ref[i]
        x = level(lax.convert_element_type(i, jnp.float32))
        w0, w1 = pair * u0, pair * u1
        s0 = s0 + w0
        sx = sx + x * w0
        sxx = sxx + (x * x) * w0
        s1 = s1 + w1
        s1x = s1x + x * w1
        s2 = s2 + pair * u2
        return s0, sx, sxx, s1, s1x, s2

    s0, sx, sxx, s1, s1x, s2 = lax.fori_loop(0, VXY, step, (zero,) * 6)
    y = level(lax.broadcasted_iota(jnp.int32, (VXY, LANES), 0).astype(jnp.float32))
    return [
        column_sum(a)
        for a in (s0, sx, y * s0, s1, sxx, y * y * s0, s2, y * sx, s1x, y * s1)
    ]


def equilibrium_total(mean, inverse, pair_ref, row_ref, col_ref):
    factor_tables(mean, inverse, pair_ref, row_ref, col_ref)
    zero = jnp.zeros((VXY, LANES), jnp.float32)

    def step(i, total):
        u = zero
        for k in range(VXY):
            u = u + row_ref[i, k : k + 1, :] * col_ref[k]
        return total + pair_ref[i] * u

    return column_sum(lax.fori_loop(0, VXY, step, zero))


def put_rows(out_ref, base, mean, inverse, alpha, beta):
    ixx, iyy, izz, ixy, ixz, iyz = inverse
    lx = ixx * mean[0] + ixy * mean[1] + ixz * mean[2]
    ly = ixy * mean[0] + iyy * mean[1] + iyz * mean[2]
    lz = ixz * mean[0] + iyz * mean[1] + izz * mean[2]
    offset = mean[0] * lx + mean[1] * ly + mean[2] * lz
    rows = [ixx, iyy, izz, 2.0 * ixy, 2.0 * ixz, 2.0 * iyz, -2.0 * lx, -2.0 * ly, -2.0 * lz, offset, alpha, beta]
    for i, row in enumerate(rows):
        out_ref[base + i : base + i + 1, :] = row


def level_sums(parts_ref, orders):
    sums = [jnp.zeros(parts_ref.shape[1:], jnp.float32) for _ in range(orders)]
    for i in range(LEVELS):
        part = parts_ref[i]
        for order in range(orders):
            sums[order] = sums[order] + level(i) ** order * part
    return sums


def ten(row0, row1, row2):
    return [
        row0(0), row0(1), row0(2), row1(0), row0(3), row0(4), row2(0), row0(5), row1(1), row1(2),
    ]


def fields_kernel(parts_ref, out_ref, pair_ref, row_ref, col_ref):
    sums = level_sums(parts_ref, 3)

    def rows(base):
        def of(a):
            def row(i):
                i = base + i
                return a[i % 4 : i % 4 + 1, i // 4 * LANES : (i // 4 + 1) * LANES] / TOTAL

            return row

        return [of(a) for a in sums]

    now = ten(*rows(0))
    moved = ten(*rows(6))
    density, mean, inverse, collide = coefficients(now)
    gauss = equilibrium_moments(mean, inverse, pair_ref, row_ref, col_ref)
    beta = time_step * collide * density * TOTAL / gauss[0]
    alpha = 1.0 - time_step * collide
    put_rows(out_ref, 0, mean, inverse, alpha, beta)
    later = [alpha * a + beta * (e / TOTAL) - time_step * b for a, e, b in zip(now, gauss, moved)]
    density, mean, inverse, collide = coefficients(later)
    total = equilibrium_total(mean, inverse, pair_ref, row_ref, col_ref)
    beta = time_step * collide * density * TOTAL / total
    put_rows(out_ref, 12, mean, inverse, 1.0 - time_step * collide, beta)


def relaxed_tile(value, flux, params_ref, base, tile, node_ref):
    rows = [params_ref[tile, base + i : base + i + 1, :] for i in range(12)]
    ixx, iyy, izz, ixy, ixz, iyz, lx, ly, lz, offset, alpha, beta = rows
    vz = node_ref[0, 2]
    x = node_x(VXY, LANES)
    parts = []
    for y in range(2):
        vy = node_ref[0, y]
        slope = ixy * vy + ixz * vz + lx
        rest = (iyy * vy + iyz * vz + ly) * vy + (izz * vz + lz) * vz + offset
        energy = jnp.exp(-0.5 * ((ixx * x + slope) * x + rest))
        at = slice(y * VXY, (y + 1) * VXY)
        parts.append(alpha * value[at, :] + beta * energy - time_step * flux[at, :])
    return jnp.concatenate(parts, axis=0)


def second_kernel(node_ref, block_ref, near_ref, flux_ref, params_ref, out_ref, sums_ref, value_ref, terms_ref):
    def first_step(g, carry):
        for half in range(2):
            at = slice(half * LANES, (half + 1) * LANES)
            value_ref[g, :, at] = relaxed_tile(
                block_ref[g, :NODES, at], flux_ref[g, :, at], params_ref, 0, g * 2 + half, node_ref
            )
        split_terms(value_ref, terms_ref, g)
        return carry

    lax.fori_loop(0, GROUPS, first_step, 0)

    def second_step(g, carry):
        flux = transport(value_ref, terms_ref, block_ref, near_ref[g], node_ref, g)
        for half in range(2):
            at = slice(half * LANES, (half + 1) * LANES)
            value = relaxed_tile(value_ref[g, :, at], flux[:, at], params_ref, 12, g * 2 + half, node_ref)
            out_ref[g, :, at] = value
            for i, row in enumerate(plane_sums(value, node_ref, True)):
                sums_ref[g * 2 + half, i : i + 1, :] = row
        return carry

    lax.fori_loop(0, GROUPS, second_step, 0)


def final_kernel(parts_ref, out_ref):
    def of(a):
        return lambda i: a[i : i + 1, :] / TOTAL

    row0, row1, row2, row3 = (of(a) for a in level_sums(parts_ref, 4))
    density, (ux, uy, uz), b, theta, _ = macroscopic(ten(row0, row1, row2))
    third = [row0(6) + row2(1), row0(7) + row2(2), row1(3) + row1(4) + row3(0)]
    trace = b[0] + b[1] + b[2]
    square = ux * ux + uy * uy + uz * uz
    stress = (
        b[0] * ux + b[3] * uy + b[4] * uz,
        b[3] * ux + b[1] * uy + b[5] * uz,
        b[4] * ux + b[5] * uy + b[2] * uz,
    )
    flux = [
        0.5 * (t / density - 2.0 * s - u * trace + 2.0 * u * square)
        for t, s, u in zip(third, stress, (ux, uy, uz))
    ]
    for i, value in enumerate((density, ux, uy, uz, *theta, *flux)):
        out_ref[i : i + 1, :] = value
    out_ref[13:16, :] = jnp.zeros((3, LANES), jnp.float32)


def shape(*dims, dtype=jnp.float32):
    return jax.ShapeDtypeStruct(dims, dtype)


VMEM = pl.BlockSpec(memory_space=pltpu.VMEM)
ANY = pl.BlockSpec(memory_space=pl.ANY)
SMEM = pl.BlockSpec(memory_space=pltpu.SMEM)
TERMS = pltpu.VMEM((GROUPS, 2 * NODES, CELLS), jnp.bfloat16)
TABLES = [pltpu.VMEM((VXY, VXY, LANES), jnp.float32)] * 3


def spread(x, axes, count):
    copies = jnp.broadcast_to(x, (count, *x.shape))
    return lax.all_to_all(copies, axes, 0, 0, tiled=True)


def per_device(distribution, normals, adjacency, send_list, block_counts):
    z, x, y, c = (lax.axis_index(a) for a in ("z", "x", "y", "c"))
    vel = (x * 8 + y) * 2 + c
    row = (vel * 16 + z * 2) & (VXY - 1)
    node = jnp.stack([row, row + 1, vel // 2, vel // 2]).astype(jnp.float32)
    node = ((node - (VXY - 1) / 2.0) * spacing).reshape(1, 4)

    block = pl.pallas_call(
        pack_kernel,
        out_shape=shape(GROUPS, ROWS, CELLS),
        in_specs=[ANY] * 5,
        out_specs=VMEM,
        scratch_shapes=[
            pltpu.VMEM((FACES, CELLS), jnp.int32),
            pltpu.VMEM((3, FACES, CELLS), jnp.float32),
            pltpu.VMEM((1, GROUPS, CELLS), jnp.int32),
            pltpu.VMEM((1, GROUPS), jnp.int32),
            pltpu.SemaphoreType.DMA((4,)),
            pltpu.SemaphoreType.DMA((GROUPS,)),
        ],
        compiler_params=pltpu.CompilerParams(vmem_limit_bytes=60 * 1024 * 1024),
    )(distribution, adjacency, jnp.transpose(normals, (1, 0, 2)), send_list, block_counts.reshape(1, GROUPS))
    block = lax.all_to_all(block, "z", 0, 0, tiled=True)

    near, flux, sums = pl.pallas_call(
        first_kernel,
        out_shape=(
            shape(GROUPS, FACES, CELLS, dtype=jnp.int32),
            shape(GROUPS, NODES, CELLS),
            shape(TILES, 4, 3 * LANES),
        ),
        in_specs=[SMEM, VMEM],
        out_specs=(VMEM, VMEM, VMEM),
        scratch_shapes=[TERMS],
        compiler_params=PARAMS,
    )(node, block)

    mine = jnp.sum(lax.all_to_all(sums, ("z", "c"), 0, 0, tiled=True), axis=0)
    params = pl.pallas_call(
        fields_kernel,
        out_shape=shape(24, LANES),
        in_specs=[VMEM],
        out_specs=VMEM,
        scratch_shapes=TABLES,
        compiler_params=PARAMS,
    )(spread(mine, ("x", "y"), LEVELS))
    params = spread(params, ("z", "c"), TILES)

    value, sums = pl.pallas_call(
        second_kernel,
        out_shape=(shape(GROUPS, NODES, CELLS), shape(TILES, 8, LANES)),
        in_specs=[SMEM, VMEM, VMEM, VMEM, VMEM],
        out_specs=(VMEM, VMEM),
        scratch_shapes=[pltpu.VMEM((GROUPS, NODES, CELLS), jnp.float32), TERMS],
        compiler_params=PARAMS,
    )(node, block, near, flux, params)

    relaxed = lax.all_to_all(value, "z", 0, 0, tiled=True).reshape(GROUPS * NODES, CELLS)
    mine = jnp.sum(lax.all_to_all(sums, ("z", "c"), 0, 0, tiled=True), axis=0)
    fields = pl.pallas_call(
        final_kernel,
        out_shape=shape(16, LANES),
        in_specs=[VMEM],
        out_specs=VMEM,
        compiler_params=PARAMS,
    )(spread(mine, ("x", "y"), LEVELS))
    other = lax.ppermute(fields, "c", [(0, 1), (1, 0)])
    fields = jnp.where(
        c == 0, jnp.concatenate([fields, other], axis=1), jnp.concatenate([other, fields], axis=1)
    )
    return relaxed, fields[:13]


def solution(mesh):
    split = Mesh(mesh.devices.reshape(8, 4, 8, 2), ("z", "x", "y", "c"))
    vel = ("x", "y", "c")
    placed = (P(vel, "z"), P(None, None, "z"), P(None, "z"), P("z", None, None), P(None, "z"))
    return jax.shard_map(
        per_device,
        mesh=split,
        in_specs=placed,
        out_specs=(P(vel, "z"), P(None, "z")),
        check_vma=False,
    )
```

```python
import jax
import jax.numpy as jnp
from jax import lax
from jax.experimental import pallas as pl
from jax.experimental.pallas import tpu as pltpu
from jax.sharding import Mesh, PartitionSpec as P

VXY = 32
TILE = 128
CELLS = 256
GROUPS = 8
NODES = 64
LANES = 128
TILES = 16
LEVELS = 32
FACES = 4
TOTAL = 32768

spacing = 0.3
ellipsoid_mix = -0.25
prandtl = 0.8
visc_power = 0.26
time_step = 0.025

ROW_ADJ = NODES
ROW_NORMAL = ROW_ADJ + FACES
ROW_SEND = ROW_NORMAL + 3 * FACES
ROWS = ROW_SEND + GROUPS

PARAMS = pltpu.CompilerParams(vmem_limit_bytes=52 * 1024 * 1024)


def level(i):
    return (i - (VXY - 1) / 2.0) * spacing


def take_lanes(values, lanes):
    return jnp.take_along_axis(values, lanes, axis=1, mode="promise_in_bounds")


def node_x(rows, lanes):
    row = lax.broadcasted_iota(jnp.int32, (rows, lanes), 0)
    return ((row & (VXY - 1)).astype(jnp.float32) - (VXY - 1) / 2.0) * spacing


def pack_kernel(
    value_hbm, adjacency_hbm, normal_hbm, send_hbm, count_hbm, out_ref,
    adjacency_ref, normal_ref, send_ref, count_ref, in_sem, value_sem,
):
    pairs = (
        (count_hbm, count_ref), (adjacency_hbm, adjacency_ref), (normal_hbm, normal_ref), (send_hbm, send_ref),
    )
    small = [pltpu.make_async_copy(a, b, in_sem.at[i]) for i, (a, b) in enumerate(pairs)]
    for copy in small:
        copy.start()
    large = [
        pltpu.make_async_copy(
            value_hbm.at[pl.ds(g * NODES, NODES), :], out_ref.at[g, pl.ds(0, NODES), :], value_sem.at[g]
        )
        for g in range(GROUPS)
    ]
    for copy in large:
        copy.start()
    for copy in small:
        copy.wait()
    adj = adjacency_ref[...]
    place = adj - CELLS
    counts = count_ref[...] * TILE
    end = jnp.zeros((1, 1), jnp.int32)
    source = jnp.zeros(adj.shape, jnp.int32)
    start = jnp.zeros(adj.shape, jnp.int32)
    for s in range(GROUPS - 1):
        end = end + counts[:, s : s + 1]
        past = end <= place
        source = source + jnp.where(past, 1, 0)
        start = jnp.where(past, end, start)
    slot = jnp.clip(place - start, 0, CELLS - 1)
    rows = [jnp.where(adj < CELLS, adj, CELLS + CELLS * source + slot).astype(jnp.float32)]
    rows += [normal_ref[d] for d in range(3)]
    rows = jnp.concatenate(rows + [send_ref[0].astype(jnp.float32)], axis=0)
    for g in range(GROUPS):
        out_ref[g, NODES:, :] = rows
    for copy in large:
        copy.wait()


def find_neighbours(block_ref, kept_ref):
    base = CELLS * lax.broadcasted_iota(jnp.int32, (GROUPS, LANES), 0)
    for face in range(FACES):
        for half in range(2):
            at = slice(half * LANES, (half + 1) * LANES)
            adj = jnp.concatenate(
                [block_ref[g, ROW_ADJ + face : ROW_ADJ + face + 1, at] for g in range(GROUPS)], axis=0
            ).astype(jnp.int32)
            place = jnp.maximum(adj - CELLS, 0)
            table = place >> 7
            lane = place & (LANES - 1)
            listed = jnp.zeros(adj.shape, jnp.float32)
            for s in range(GROUPS):
                for part in range(2):
                    rows = block_ref[s, ROW_SEND : ROW_SEND + GROUPS, part * LANES : (part + 1) * LANES]
                    listed = jnp.where(table == s * 2 + part, take_lanes(rows, lane), listed)
            far = (place >> 8) * CELLS + listed.astype(jnp.int32)
            near = jnp.where(adj < CELLS, adj + base, far).astype(jnp.float32)
            for g in range(GROUPS):
                kept_ref[g, ROW_NEAR + face : ROW_NEAR + face + 1, at] = near[g : g + 1, :]


def split_terms(value_ref, terms_ref, g):
    value = value_ref[g, :NODES, :]
    high = value.astype(jnp.bfloat16)
    terms_ref[g, :NODES, :] = high
    terms_ref[g, NODES:, :] = (value - high.astype(jnp.float32)).astype(jnp.bfloat16)


def choice(row):
    place = lax.broadcasted_iota(jnp.int32, (CELLS, CELLS), 0)
    return jnp.where(place == (row & (CELLS - 1)), 1.0, 0.0).astype(jnp.bfloat16)


def look_up(terms_ref, row):
    chosen = choice(row)
    group = row >> 8
    found = None
    for s in range(GROUPS):
        both = jnp.dot(terms_ref[s], chosen, preferred_element_type=jnp.float32)
        got = both[:NODES] + both[NODES:]
        found = got if s == 0 else jnp.where(group == s, got, found)
    return found


def face_speeds(block_ref, node_ref, g, face):
    normal = [block_ref[g, ROW_NORMAL + FACES * d + face : ROW_NORMAL + FACES * d + face + 1, :] for d in range(3)]
    return normal[0], [normal[1] * node_ref[0, y] + normal[2] * node_ref[0, 2] for y in range(2)]


def transport(block_ref, terms_ref, near, node_ref, g, kept_ref):
    own = block_ref[g, :NODES, :]
    x = node_x(NODES, CELLS)
    second = lax.broadcasted_iota(jnp.int32, (NODES, CELLS), 0) >= VXY
    total = jnp.zeros((NODES, CELLS), jnp.float32)
    for face in range(FACES):
        found = look_up(terms_ref, near[face : face + 1, :])
        kept_ref[g, face * NODES : (face + 1) * NODES, :] = found
        slope, fixed = face_speeds(block_ref, node_ref, g, face)
        speed = slope * x + jnp.where(second, fixed[1], fixed[0])
        total = total + speed * jnp.where(speed > 0.0, own, found)
    return total


def plane_sums(value, node_ref, third):
    x = node_x(VXY, value.shape[1])
    sums = []
    for y in range(2):
        part = value[y * VXY : (y + 1) * VXY, :]
        powers = [part]
        for _ in range(3 if third else 2):
            powers.append(x * powers[-1])
        sums.append([column_sum(p) for p in powers])
    low, high = sums
    ya, yb = node_ref[0, 0], node_ref[0, 1]

    def over(i, order=0):
        return ya**order * low[i] + yb**order * high[i] if order else low[i] + high[i]

    rows = [over(0), over(1), over(0, 1), over(2), over(0, 2), over(1, 1)]
    if third:
        rows += [over(3) + over(1, 2), over(2, 1) + over(0, 3)]
    return rows


ROW_FLUX = FACES * NODES
ROW_NEAR = ROW_FLUX + NODES
KEPT = ROW_NEAR + 8


def near_rows(kept_ref, g):
    return kept_ref[g, ROW_NEAR : ROW_NEAR + FACES, :].astype(jnp.int32)


def first_kernel(node_ref, block_ref, kept_hbm, sums_ref, kept_ref, terms_ref, kept_sem):
    find_neighbours(block_ref, kept_ref)

    def out_copy(g):
        return pltpu.make_async_copy(kept_ref.at[g], kept_hbm.at[g], kept_sem.at[g])

    for g in range(GROUPS):
        split_terms(block_ref, terms_ref, g)

    def group(g, carry):
        flux = transport(block_ref, terms_ref, near_rows(kept_ref, g), node_ref, g, kept_ref)
        kept_ref[g, ROW_FLUX:ROW_NEAR, :] = flux
        out_copy(g).start()
        rows = plane_sums(block_ref[g, :NODES, :], node_ref, False) + plane_sums(flux, node_ref, False)
        for i, row in enumerate(rows):
            for half in range(2):
                q = i // 4
                sums_ref[g * 2 + half, i % 4 : i % 4 + 1, q * LANES : (q + 1) * LANES] = row[
                    :, half * LANES : (half + 1) * LANES
                ]
        return carry

    lax.fori_loop(0, GROUPS, group, 0)
    for g in range(GROUPS):
        out_copy(g).wait()


def between_kernel(kept_hbm, moved_hbm, flux_ref, moved_ref, terms_ref, flux_sem, moved_sem):
    def flux_in(g):
        rows = pl.ds(ROW_FLUX, KEPT - ROW_FLUX)
        return pltpu.make_async_copy(kept_hbm.at[g, rows, :], flux_ref.at[g], flux_sem.at[g])

    def out_copy(g):
        return pltpu.make_async_copy(moved_ref.at[g], moved_hbm.at[g], moved_sem.at[g])

    for g in range(GROUPS):
        flux_in(g).start()
    for g in range(GROUPS):
        flux_in(g).wait()
        split_terms(flux_ref, terms_ref, g)

    def group(g, carry):
        near = flux_ref[g, NODES : NODES + FACES, :].astype(jnp.int32)
        for face in range(FACES):
            moved_ref[g, face] = look_up(terms_ref, near[face : face + 1, :])
        out_copy(g).start()
        return carry

    lax.fori_loop(0, GROUPS, group, 0)
    for g in range(GROUPS):
        out_copy(g).wait()


def macroscopic(m):
    density = m[0]
    scale = 1.0 / density
    ux, uy, uz = m[1] * scale, m[2] * scale, m[3] * scale
    second = [m[4 + i] * scale for i in range(6)]
    txx = second[0] - ux * ux
    tyy = second[1] - uy * uy
    tzz = second[2] - uz * uz
    txy = second[3] - ux * uy
    txz = second[4] - ux * uz
    tyz = second[5] - uy * uz
    temper = (txx + tyy + tzz) / 3.0
    return density, (ux, uy, uz), second, (txx, tyy, tzz, txy, txz, tyz), temper


def coefficients(m):
    density, (ux, uy, uz), _, (txx, tyy, tzz, txy, txz, tyz), temper = macroscopic(m)
    iso = (1.0 - ellipsoid_mix) * temper
    lxx = iso + ellipsoid_mix * txx
    lyy = iso + ellipsoid_mix * tyy
    lzz = iso + ellipsoid_mix * tzz
    lxy = ellipsoid_mix * txy
    lxz = ellipsoid_mix * txz
    lyz = ellipsoid_mix * tyz
    cxx = lyy * lzz - lyz * lyz
    cxy = lyz * lxz - lxy * lzz
    cxz = lxy * lyz - lyy * lxz
    cyy = lxx * lzz - lxz * lxz
    cyz = lxy * lxz - lxx * lyz
    czz = lxx * lyy - lxy * lxy
    det = 1.0 / (lxx * cxx + lxy * cxy + lxz * cxz)
    inverse = (cxx * det, cyy * det, czz * det, cxy * det, cxz * det, cyz * det)
    collide = prandtl * density * jnp.exp(visc_power * jnp.log(temper))
    return density, (ux, uy, uz), inverse, collide


def factor_tables(mean, inverse, pair_ref, row_ref, col_ref):
    grid = level(lax.broadcasted_iota(jnp.int32, (VXY, LANES), 0).astype(jnp.float32))
    ixx, iyy, izz, ixy, ixz, iyz = inverse
    cx, cy, cz = grid - mean[0], grid - mean[1], grid - mean[2]
    own_x, own_y, own_z = -0.25 * ixx * cx * cx, -0.25 * iyy * cy * cy, -0.25 * izz * cz * cz
    cross_y = -ixy * cy
    cross_z = -ixz * cz
    cross_yz = -iyz * cy
    for i in range(VXY):
        x_own, x_c = own_x[i : i + 1, :], cx[i : i + 1, :]
        z_own, z_c = own_z[i : i + 1, :], cz[i : i + 1, :]
        pair_ref[i] = jnp.exp(x_own + own_y + x_c * cross_y)
        row_ref[i] = jnp.exp(x_own + own_z + x_c * cross_z)
        col_ref[i] = jnp.exp(z_own + own_y + z_c * cross_yz)


def column_sum(a):
    return jnp.sum(a, axis=0, keepdims=True)


def equilibrium_moments(mean, inverse, pair_ref, row_ref, col_ref):
    factor_tables(mean, inverse, pair_ref, row_ref, col_ref)
    zero = jnp.zeros((VXY, LANES), jnp.float32)

    def step(i, carry):
        s0, sx, sxx, s1, s1x, s2 = carry
        u0, u1, u2 = zero, zero, zero
        for k in range(VXY // 2):
            z = -level(k)
            low = row_ref[i, k : k + 1, :] * col_ref[k]
            high = row_ref[i, VXY - 1 - k : VXY - k, :] * col_ref[VXY - 1 - k]
            both = low + high
            u0 = u0 + both
            u1 = u1 + z * (high - low)
            u2 = u2 + (z * z) * both
        pair = pair_ref[i]
        x = level(lax.convert_element_type(i, jnp.float32))
        w0, w1 = pair * u0, pair * u1
        s0 = s0 + w0
        sx = sx + x * w0
        sxx = sxx + (x * x) * w0
        s1 = s1 + w1
        s1x = s1x + x * w1
        s2 = s2 + pair * u2
        return s0, sx, sxx, s1, s1x, s2

    s0, sx, sxx, s1, s1x, s2 = lax.fori_loop(0, VXY, step, (zero,) * 6)
    y = level(lax.broadcasted_iota(jnp.int32, (VXY, LANES), 0).astype(jnp.float32))
    return [
        column_sum(a)
        for a in (s0, sx, y * s0, s1, sxx, y * y * s0, s2, y * sx, s1x, y * s1)
    ]


def equilibrium_total(mean, inverse, pair_ref, row_ref, col_ref):
    factor_tables(mean, inverse, pair_ref, row_ref, col_ref)
    zero = jnp.zeros((VXY, LANES), jnp.float32)

    def step(i, total):
        u = zero
        for k in range(VXY):
            u = u + row_ref[i, k : k + 1, :] * col_ref[k]
        return total + pair_ref[i] * u

    return column_sum(lax.fori_loop(0, VXY, step, zero))


def put_rows(out_ref, base, mean, inverse, alpha, beta):
    ixx, iyy, izz, ixy, ixz, iyz = inverse
    lx = ixx * mean[0] + ixy * mean[1] + ixz * mean[2]
    ly = ixy * mean[0] + iyy * mean[1] + iyz * mean[2]
    lz = ixz * mean[0] + iyz * mean[1] + izz * mean[2]
    offset = mean[0] * lx + mean[1] * ly + mean[2] * lz
    rows = [ixx, iyy, izz, 2.0 * ixy, 2.0 * ixz, 2.0 * iyz, -2.0 * lx, -2.0 * ly, -2.0 * lz, offset, alpha, beta]
    for i, row in enumerate(rows):
        out_ref[base + i : base + i + 1, :] = row


def level_sums(parts_ref, orders):
    sums = [jnp.zeros(parts_ref.shape[1:], jnp.float32) for _ in range(orders)]
    for i in range(LEVELS):
        part = parts_ref[i]
        for order in range(orders):
            sums[order] = sums[order] + level(i) ** order * part
    return sums


def ten(row0, row1, row2):
    return [
        row0(0), row0(1), row0(2), row1(0), row0(3), row0(4), row2(0), row0(5), row1(1), row1(2),
    ]


def fields_kernel(parts_ref, out_ref, pair_ref, row_ref, col_ref):
    sums = level_sums(parts_ref, 3)

    def rows(base):
        def of(a):
            def row(i):
                i = base + i
                return a[i % 4 : i % 4 + 1, i // 4 * LANES : (i // 4 + 1) * LANES] / TOTAL

            return row

        return [of(a) for a in sums]

    now = ten(*rows(0))
    moved = ten(*rows(6))
    density, mean, inverse, collide = coefficients(now)
    gauss = equilibrium_moments(mean, inverse, pair_ref, row_ref, col_ref)
    beta = time_step * collide * density * TOTAL / gauss[0]
    alpha = 1.0 - time_step * collide
    put_rows(out_ref, 0, mean, inverse, alpha, beta)
    later = [alpha * a + beta * (e / TOTAL) - time_step * b for a, e, b in zip(now, gauss, moved)]
    density, mean, inverse, collide = coefficients(later)
    total = equilibrium_total(mean, inverse, pair_ref, row_ref, col_ref)
    beta = time_step * collide * density * TOTAL / total
    put_rows(out_ref, 12, mean, inverse, 1.0 - time_step * collide, beta)


def node_rows(params_ref, base, g, node_ref):
    rows = [
        jnp.concatenate([params_ref[g * 2 + half, base + i : base + i + 1, :] for half in range(2)], axis=1)
        for i in range(12)
    ]
    ixx, iyy, izz, ixy, ixz, iyz, lx, ly, lz, offset, alpha, beta = rows
    vz = node_ref[0, 2]
    out = [-0.5 * ixx]
    for y in range(2):
        vy = node_ref[0, y]
        out.append(-0.5 * (ixy * vy + ixz * vz + lx))
        out.append(-0.5 * ((iyy * vy + iyz * vz + ly) * vy + (izz * vz + lz) * vz + offset))
    return out + [alpha, beta]


def relaxed(value, flux, rows, x, y):
    energy = jnp.exp((rows[0] * x + rows[1 + 2 * y]) * x + rows[2 + 2 * y])
    return rows[5] * value + rows[6] * energy - time_step * flux


def second_kernel(
    node_ref, block_ref, kept_hbm, moved_hbm, params_ref, out_hbm, sums_ref,
    value_ref, terms_ref, kept_ref, moved_ref, out_ref, kept_sem, moved_sem, out_sem,
):
    x = node_x(VXY, CELLS)

    def kept_in(g):
        return pltpu.make_async_copy(kept_hbm.at[g], kept_ref.at[g], kept_sem.at[g])

    def moved_in(g):
        return pltpu.make_async_copy(moved_hbm.at[g], moved_ref.at[g], moved_sem.at[g])

    def out_copy(g):
        return pltpu.make_async_copy(out_ref.at[g], out_hbm.at[g], out_sem.at[g])

    for g in range(GROUPS):
        kept_in(g).start()
    for g in range(GROUPS):
        moved_in(g).start()

    def first_step(g, carry):
        kept_in(g).wait()
        rows = node_rows(params_ref, 0, g, node_ref)
        for y in range(2):
            at = slice(y * VXY, (y + 1) * VXY)
            flux = kept_ref[g, ROW_FLUX + y * VXY : ROW_FLUX + (y + 1) * VXY, :]
            value_ref[g, at, :] = relaxed(block_ref[g, at, :], flux, rows, x, y)
        rest = jnp.concatenate(rows + [jnp.zeros((1, CELLS), jnp.float32)], axis=0)
        parts = []
        for _ in range(3):
            part = rest.astype(jnp.bfloat16).astype(jnp.float32)
            parts.append(part)
            rest = rest - part
        parts.append(jnp.zeros((8, CELLS), jnp.float32))
        terms_ref[g] = jnp.concatenate(parts, axis=0).astype(jnp.bfloat16)
        return carry

    lax.fori_loop(0, GROUPS, first_step, 0)

    def second_step(g, carry):
        moved_in(g).wait()
        near = near_rows(kept_ref, g)
        total = [jnp.zeros((VXY, CELLS), jnp.float32)] * 2
        for face in range(FACES):
            row = near[face : face + 1, :]
            group = row >> 8
            terms = terms_ref[...].reshape(GROUPS * 32, CELLS)
            picked = jnp.dot(terms, choice(row), preferred_element_type=jnp.float32)
            there = None
            for s in range(GROUPS):
                got = picked[s * 32 : s * 32 + 8] + picked[s * 32 + 8 : s * 32 + 16] + picked[s * 32 + 16 : s * 32 + 24]
                there = got if s == 0 else jnp.where(group == s, got, there)
            rows = [there[i : i + 1, :] for i in range(7)]
            slope, fixed = face_speeds(block_ref, node_ref, g, face)
            for y in range(2):
                at = slice(y * VXY, (y + 1) * VXY)
                found = kept_ref[g, face * NODES + y * VXY : face * NODES + (y + 1) * VXY, :]
                far = relaxed(found, moved_ref[g, face, at, :], rows, x, y)
                speed = slope * x + fixed[y]
                total[y] = total[y] + speed * jnp.where(speed > 0.0, value_ref[g, at, :], far)
        rows = node_rows(params_ref, 12, g, node_ref)
        values = []
        for y in range(2):
            at = slice(y * VXY, (y + 1) * VXY)
            values.append(relaxed(value_ref[g, at, :], total[y], rows, x, y))
            out_ref[g, at, :] = values[y]
        out_copy(g).start()
        for i, row in enumerate(plane_sums(jnp.concatenate(values, axis=0), node_ref, True)):
            for half in range(2):
                sums_ref[g * 2 + half, i : i + 1, :] = row[:, half * LANES : (half + 1) * LANES]
        return carry

    lax.fori_loop(0, GROUPS, second_step, 0)
    for g in range(GROUPS):
        out_copy(g).wait()


def final_kernel(parts_ref, out_ref):
    def of(a):
        return lambda i: a[i : i + 1, :] / TOTAL

    row0, row1, row2, row3 = (of(a) for a in level_sums(parts_ref, 4))
    density, (ux, uy, uz), b, theta, _ = macroscopic(ten(row0, row1, row2))
    third = [row0(6) + row2(1), row0(7) + row2(2), row1(3) + row1(4) + row3(0)]
    trace = b[0] + b[1] + b[2]
    square = ux * ux + uy * uy + uz * uz
    stress = (
        b[0] * ux + b[3] * uy + b[4] * uz,
        b[3] * ux + b[1] * uy + b[5] * uz,
        b[4] * ux + b[5] * uy + b[2] * uz,
    )
    flux = [
        0.5 * (t / density - 2.0 * s - u * trace + 2.0 * u * square)
        for t, s, u in zip(third, stress, (ux, uy, uz))
    ]
    for i, value in enumerate((density, ux, uy, uz, *theta, *flux)):
        out_ref[i : i + 1, :] = value
    out_ref[13:16, :] = jnp.zeros((3, LANES), jnp.float32)


def shape(*dims, dtype=jnp.float32):
    return jax.ShapeDtypeStruct(dims, dtype)


VMEM = pl.BlockSpec(memory_space=pltpu.VMEM)
ANY = pl.BlockSpec(memory_space=pl.ANY)
HBM = pl.BlockSpec(memory_space=pltpu.HBM)
SMEM = pl.BlockSpec(memory_space=pltpu.SMEM)
MOVED = pltpu.VMEM((GROUPS, FACES, NODES, CELLS), jnp.float32)
KEEP = pltpu.VMEM((GROUPS, KEPT, CELLS), jnp.float32)
VALUES = pltpu.VMEM((GROUPS, NODES, CELLS), jnp.float32)
EACH = pltpu.SemaphoreType.DMA((GROUPS,))
TERMS = pltpu.VMEM((GROUPS, 2 * NODES, CELLS), jnp.bfloat16)
TABLES = [pltpu.VMEM((VXY, VXY, LANES), jnp.float32)] * 3


def spread(x, axes, count):
    copies = jnp.broadcast_to(x, (count, *x.shape))
    return lax.all_to_all(copies, axes, 0, 0, tiled=True)


def per_device(distribution, normals, adjacency, send_list, block_counts):
    z, x, y, c = (lax.axis_index(a) for a in ("z", "x", "y", "c"))
    vel = (x * 8 + y) * 2 + c
    row = (vel * 16 + z * 2) & (VXY - 1)
    node = jnp.stack([row, row + 1, vel // 2, vel // 2]).astype(jnp.float32)
    node = ((node - (VXY - 1) / 2.0) * spacing).reshape(1, 4)

    block = pl.pallas_call(
        pack_kernel,
        out_shape=shape(GROUPS, ROWS, CELLS),
        in_specs=[ANY] * 5,
        out_specs=VMEM,
        scratch_shapes=[
            pltpu.VMEM((FACES, CELLS), jnp.int32),
            pltpu.VMEM((3, FACES, CELLS), jnp.float32),
            pltpu.VMEM((1, GROUPS, CELLS), jnp.int32),
            pltpu.VMEM((1, GROUPS), jnp.int32),
            pltpu.SemaphoreType.DMA((4,)),
            pltpu.SemaphoreType.DMA((GROUPS,)),
        ],
        compiler_params=pltpu.CompilerParams(vmem_limit_bytes=60 * 1024 * 1024),
    )(distribution, adjacency, jnp.transpose(normals, (1, 0, 2)), send_list, block_counts.reshape(1, GROUPS))
    block = lax.all_to_all(block, "z", 0, 0, tiled=True)

    kept, sums = pl.pallas_call(
        first_kernel,
        out_shape=(
            shape(GROUPS, KEPT, CELLS),
            shape(TILES, 4, 3 * LANES),
        ),
        in_specs=[SMEM, VMEM],
        out_specs=(HBM, VMEM),
        scratch_shapes=[KEEP, TERMS, EACH],
        compiler_params=PARAMS,
    )(node, block)
    moved = pl.pallas_call(
        between_kernel,
        out_shape=shape(GROUPS, FACES, NODES, CELLS),
        in_specs=[HBM],
        out_specs=HBM,
        scratch_shapes=[
            pltpu.VMEM((GROUPS, KEPT - ROW_FLUX, CELLS), jnp.float32), MOVED, TERMS, EACH, EACH,
        ],
        compiler_params=PARAMS,
        cost_estimate=pl.CostEstimate(flops=4300000000, bytes_accessed=3000000, transcendentals=0),
    )(kept)

    mine = jnp.sum(lax.all_to_all(sums, ("z", "c"), 0, 0, tiled=True), axis=0)
    params = pl.pallas_call(
        fields_kernel,
        out_shape=shape(24, LANES),
        in_specs=[VMEM],
        out_specs=VMEM,
        scratch_shapes=TABLES,
        compiler_params=PARAMS,
    )(spread(mine, ("x", "y"), LEVELS))
    params = spread(params, ("z", "c"), TILES)

    value, sums = pl.pallas_call(
        second_kernel,
        out_shape=(shape(GROUPS, NODES, CELLS), shape(TILES, 8, LANES)),
        in_specs=[SMEM, VMEM, HBM, HBM, VMEM],
        out_specs=(HBM, VMEM),
        scratch_shapes=[
            VALUES, pltpu.VMEM((GROUPS, 32, CELLS), jnp.bfloat16), KEEP, MOVED, VALUES, EACH, EACH, EACH,
        ],
        compiler_params=PARAMS,
    )(node, block, kept, moved, params)

    result = lax.all_to_all(value, "z", 0, 0, tiled=True).reshape(GROUPS * NODES, CELLS)
    mine = jnp.sum(lax.all_to_all(sums, ("z", "c"), 0, 0, tiled=True), axis=0)
    fields = pl.pallas_call(
        final_kernel,
        out_shape=shape(16, LANES),
        in_specs=[VMEM],
        out_specs=VMEM,
        compiler_params=PARAMS,
    )(spread(mine, ("x", "y"), LEVELS))
    other = lax.ppermute(fields, "c", [(0, 1), (1, 0)])
    fields = jnp.where(
        c == 0, jnp.concatenate([fields, other], axis=1), jnp.concatenate([other, fields], axis=1)
    )
    return result, fields[:13]


def solution(mesh):
    split = Mesh(mesh.devices.reshape(8, 4, 8, 2), ("z", "x", "y", "c"))
    vel = ("x", "y", "c")
    placed = (P(vel, "z"), P(None, None, "z"), P(None, "z"), P("z", None, None), P(None, "z"))
    return jax.shard_map(
        per_device,
        mesh=split,
        in_specs=placed,
        out_specs=(P(vel, "z"), P(None, "z")),
        check_vma=False,
    )
```

```python
import jax
import jax.numpy as jnp
from jax import lax
from jax.experimental import pallas as pl
from jax.experimental.pallas import tpu as pltpu
from jax.sharding import Mesh, PartitionSpec as P

VXY = 32
TILE = 128
CELLS = 256
GROUPS = 8
NODES = 64
LANES = 128
TILES = 16
LEVELS = 32
FACES = 4
TOTAL = 32768

spacing = 0.3
ellipsoid_mix = -0.25
prandtl = 0.8
visc_power = 0.26
time_step = 0.025

ROW_ADJ = NODES
ROW_NORMAL = ROW_ADJ + FACES
ROW_SEND = ROW_NORMAL + 3 * FACES
ROWS = ROW_SEND + GROUPS

PARAMS = pltpu.CompilerParams(vmem_limit_bytes=48 * 1024 * 1024)


def level(i):
    return (i - (VXY - 1) / 2.0) * spacing


def take_lanes(values, lanes):
    return jnp.take_along_axis(values, lanes, axis=1, mode="promise_in_bounds")


def node_x(rows, lanes):
    row = lax.broadcasted_iota(jnp.int32, (rows, lanes), 0)
    return ((row & (VXY - 1)).astype(jnp.float32) - (VXY - 1) / 2.0) * spacing


def pack_kernel(
    value_hbm, adjacency_hbm, normal_hbm, send_hbm, count_hbm, out_ref,
    adjacency_ref, normal_ref, send_ref, count_ref, in_sem, value_sem,
):
    pairs = (
        (count_hbm, count_ref), (adjacency_hbm, adjacency_ref), (normal_hbm, normal_ref), (send_hbm, send_ref),
    )
    small = [pltpu.make_async_copy(a, b, in_sem.at[i]) for i, (a, b) in enumerate(pairs)]
    for copy in small:
        copy.start()
    large = [
        pltpu.make_async_copy(
            value_hbm.at[pl.ds(g * NODES, NODES), :], out_ref.at[g, pl.ds(0, NODES), :], value_sem.at[g]
        )
        for g in range(GROUPS)
    ]
    for copy in large:
        copy.start()
    for copy in small:
        copy.wait()
    adj = adjacency_ref[...]
    place = adj - CELLS
    counts = count_ref[...] * TILE
    end = jnp.zeros((1, 1), jnp.int32)
    source = jnp.zeros(adj.shape, jnp.int32)
    start = jnp.zeros(adj.shape, jnp.int32)
    for s in range(GROUPS - 1):
        end = end + counts[:, s : s + 1]
        past = end <= place
        source = source + jnp.where(past, 1, 0)
        start = jnp.where(past, end, start)
    slot = jnp.clip(place - start, 0, CELLS - 1)
    rows = [jnp.where(adj < CELLS, adj, CELLS + CELLS * source + slot).astype(jnp.float32)]
    rows += [normal_ref[d] for d in range(3)]
    rows = jnp.concatenate(rows + [send_ref[0].astype(jnp.float32)], axis=0)
    for g in range(GROUPS):
        out_ref[g, NODES:, :] = rows
    for copy in large:
        copy.wait()


def find_neighbours(block_ref, near_ref):
    base = CELLS * lax.broadcasted_iota(jnp.int32, (GROUPS, LANES), 0)
    for face in range(FACES):
        for half in range(2):
            at = slice(half * LANES, (half + 1) * LANES)
            adj = jnp.concatenate(
                [block_ref[g, ROW_ADJ + face : ROW_ADJ + face + 1, at] for g in range(GROUPS)], axis=0
            ).astype(jnp.int32)
            place = jnp.maximum(adj - CELLS, 0)
            table = place >> 7
            lane = place & (LANES - 1)
            listed = jnp.zeros(adj.shape, jnp.float32)
            for s in range(GROUPS):
                for part in range(2):
                    rows = block_ref[s, ROW_SEND : ROW_SEND + GROUPS, part * LANES : (part + 1) * LANES]
                    listed = jnp.where(table == s * 2 + part, take_lanes(rows, lane), listed)
            far = (place >> 8) * CELLS + listed.astype(jnp.int32)
            near = jnp.where(adj < CELLS, adj + base, far)
            for g in range(GROUPS):
                near_ref[g, face : face + 1, at] = near[g : g + 1, :]


def split_terms(value_ref, terms_ref, g):
    value = value_ref[g, :NODES, :]
    high = value.astype(jnp.bfloat16)
    terms_ref[g, :NODES, :] = high
    terms_ref[g, NODES:, :] = (value - high.astype(jnp.float32)).astype(jnp.bfloat16)


def look_up_lanes(value_ref, row):
    blocks = NODES // 8
    halves = []
    for half in range(2):
        near = jnp.broadcast_to(row[:, half * LANES : (half + 1) * LANES], (8, LANES))
        lane = near & (LANES - 1)
        tile = near >> 7
        found = [None] * blocks
        for t in range(TILES):
            hit = tile == t
            at = slice((t % 2) * LANES, (t % 2 + 1) * LANES)
            for b in range(blocks):
                got = take_lanes(value_ref[t // 2, b * 8 : b * 8 + 8, at], lane)
                found[b] = got if t == 0 else jnp.where(hit, got, found[b])
        halves.append(jnp.concatenate(found, axis=0))
    return jnp.concatenate(halves, axis=1)


def look_up(terms_ref, row):
    place = lax.broadcasted_iota(jnp.int32, (CELLS, CELLS), 0)
    chosen = jnp.where(place == (row & (CELLS - 1)), 1.0, 0.0).astype(jnp.bfloat16)
    group = row >> 8
    found = None
    for s in range(GROUPS):
        both = jnp.dot(terms_ref[s], chosen, preferred_element_type=jnp.float32)
        got = both[:NODES] + both[NODES:]
        found = got if s == 0 else jnp.where(group == s, got, found)
    return found


def transport(value_ref, terms_ref, normal_ref, near, node_ref, g):
    own = value_ref[g, :NODES, :]
    x = node_x(NODES, CELLS)
    second = lax.broadcasted_iota(jnp.int32, (NODES, CELLS), 0) >= VXY
    total = jnp.zeros((NODES, CELLS), jnp.float32)
    for face in range(FACES):
        row = near[face : face + 1, :]
        found = look_up(terms_ref, row) if face else look_up_lanes(value_ref, row)
        normal = [normal_ref[g, ROW_NORMAL + FACES * d + face : ROW_NORMAL + FACES * d + face + 1, :] for d in range(3)]
        fixed = [normal[1] * node_ref[0, y] + normal[2] * node_ref[0, 2] for y in range(2)]
        speed = normal[0] * x + jnp.where(second, fixed[1], fixed[0])
        total = total + speed * jnp.where(speed > 0.0, own, found)
    return total


def plane_sums(value, node_ref, third):
    x = node_x(VXY, value.shape[1])
    sums = []
    for y in range(2):
        part = value[y * VXY : (y + 1) * VXY, :]
        powers = [part]
        for _ in range(3 if third else 2):
            powers.append(x * powers[-1])
        sums.append([column_sum(p) for p in powers])
    low, high = sums
    ya, yb = node_ref[0, 0], node_ref[0, 1]

    def over(i, order=0):
        return ya**order * low[i] + yb**order * high[i] if order else low[i] + high[i]

    rows = [over(0), over(1), over(0, 1), over(2), over(0, 2), over(1, 1)]
    if third:
        rows += [over(3) + over(1, 2), over(2, 1) + over(0, 3)]
    return rows


def first_kernel(node_ref, block_ref, near_ref, flux_ref, sums_ref, terms_ref):
    find_neighbours(block_ref, near_ref)
    for g in range(GROUPS):
        split_terms(block_ref, terms_ref, g)

    def group(g, carry):
        flux = transport(block_ref, terms_ref, block_ref, near_ref[g], node_ref, g)
        flux_ref[g] = flux
        rows = plane_sums(block_ref[g, :NODES, :], node_ref, False) + plane_sums(flux, node_ref, False)
        for i, row in enumerate(rows):
            for half in range(2):
                q = i // 4
                sums_ref[half * GROUPS + g, i % 4 : i % 4 + 1, q * LANES : (q + 1) * LANES] = row[
                    :, half * LANES : (half + 1) * LANES
                ]
        return carry

    lax.fori_loop(0, GROUPS, group, 0)


def macroscopic(m):
    density = m[0]
    scale = 1.0 / density
    ux, uy, uz = m[1] * scale, m[2] * scale, m[3] * scale
    second = [m[4 + i] * scale for i in range(6)]
    txx = second[0] - ux * ux
    tyy = second[1] - uy * uy
    tzz = second[2] - uz * uz
    txy = second[3] - ux * uy
    txz = second[4] - ux * uz
    tyz = second[5] - uy * uz
    temper = (txx + tyy + tzz) / 3.0
    return density, (ux, uy, uz), second, (txx, tyy, tzz, txy, txz, tyz), temper


def coefficients(m):
    density, (ux, uy, uz), _, (txx, tyy, tzz, txy, txz, tyz), temper = macroscopic(m)
    iso = (1.0 - ellipsoid_mix) * temper
    lxx = iso + ellipsoid_mix * txx
    lyy = iso + ellipsoid_mix * tyy
    lzz = iso + ellipsoid_mix * tzz
    lxy = ellipsoid_mix * txy
    lxz = ellipsoid_mix * txz
    lyz = ellipsoid_mix * tyz
    cxx = lyy * lzz - lyz * lyz
    cxy = lyz * lxz - lxy * lzz
    cxz = lxy * lyz - lyy * lxz
    cyy = lxx * lzz - lxz * lxz
    cyz = lxy * lxz - lxx * lyz
    czz = lxx * lyy - lxy * lxy
    det = 1.0 / (lxx * cxx + lxy * cxy + lxz * cxz)
    inverse = (cxx * det, cyy * det, czz * det, cxy * det, cxz * det, cyz * det)
    collide = prandtl * density * jnp.exp(visc_power * jnp.log(temper))
    return density, (ux, uy, uz), inverse, collide


def factor_tables(mean, inverse, pair_ref, row_ref, col_ref):
    grid = level(lax.broadcasted_iota(jnp.int32, (VXY, LANES), 0).astype(jnp.float32))
    ixx, iyy, izz, ixy, ixz, iyz = inverse
    cx, cy, cz = grid - mean[0], grid - mean[1], grid - mean[2]
    own_x, own_y, own_z = -0.25 * ixx * cx * cx, -0.25 * iyy * cy * cy, -0.25 * izz * cz * cz
    cross_y = -ixy * cy
    cross_z = -ixz * cz
    cross_yz = -iyz * cy
    for i in range(VXY):
        x_own, x_c = own_x[i : i + 1, :], cx[i : i + 1, :]
        z_own, z_c = own_z[i : i + 1, :], cz[i : i + 1, :]
        pair_ref[i] = jnp.exp(x_own + own_y + x_c * cross_y)
        row_ref[i] = jnp.exp(x_own + own_z + x_c * cross_z)
        col_ref[i] = jnp.exp(z_own + own_y + z_c * cross_yz)


def column_sum(a):
    return jnp.sum(a, axis=0, keepdims=True)


def equilibrium_moments(mean, inverse, pair_ref, row_ref, col_ref):
    factor_tables(mean, inverse, pair_ref, row_ref, col_ref)
    zero = jnp.zeros((VXY, LANES), jnp.float32)

    def step(i, carry):
        s0, sx, sxx, s1, s1x, s2 = carry
        u0, u1, u2 = zero, zero, zero
        for k in range(VXY // 2):
            z = -level(k)
            low = row_ref[i, k : k + 1, :] * col_ref[k]
            high = row_ref[i, VXY - 1 - k : VXY - k, :] * col_ref[VXY - 1 - k]
            both = low + high
            u0 = u0 + both
            u1 = u1 + z * (high - low)
            u2 = u2 + (z * z) * both
        pair = pair_ref[i]
        x = level(lax.convert_element_type(i, jnp.float32))
        w0, w1 = pair * u0, pair * u1
        s0 = s0 + w0
        sx = sx + x * w0
        sxx = sxx + (x * x) * w0
        s1 = s1 + w1
        s1x = s1x + x * w1
        s2 = s2 + pair * u2
        return s0, sx, sxx, s1, s1x, s2

    s0, sx, sxx, s1, s1x, s2 = lax.fori_loop(0, VXY, step, (zero,) * 6)
    y = level(lax.broadcasted_iota(jnp.int32, (VXY, LANES), 0).astype(jnp.float32))
    return [
        column_sum(a)
        for a in (s0, sx, y * s0, s1, sxx, y * y * s0, s2, y * sx, s1x, y * s1)
    ]


def equilibrium_total(mean, inverse, pair_ref, row_ref, col_ref):
    factor_tables(mean, inverse, pair_ref, row_ref, col_ref)
    zero = jnp.zeros((VXY, LANES), jnp.float32)

    def step(i, total):
        u = zero
        for k in range(VXY):
            u = u + row_ref[i, k : k + 1, :] * col_ref[k]
        return total + pair_ref[i] * u

    return column_sum(lax.fori_loop(0, VXY, step, zero))


def put_rows(out_ref, base, mean, inverse, alpha, beta):
    ixx, iyy, izz, ixy, ixz, iyz = inverse
    lx = ixx * mean[0] + ixy * mean[1] + ixz * mean[2]
    ly = ixy * mean[0] + iyy * mean[1] + iyz * mean[2]
    lz = ixz * mean[0] + iyz * mean[1] + izz * mean[2]
    offset = mean[0] * lx + mean[1] * ly + mean[2] * lz
    rows = [ixx, iyy, izz, 2.0 * ixy, 2.0 * ixz, 2.0 * iyz, -2.0 * lx, -2.0 * ly, -2.0 * lz, offset, alpha, beta]
    for i, row in enumerate(rows):
        out_ref[base + i : base + i + 1, :] = row


def level_sums(parts_ref, orders):
    sums = [jnp.zeros(parts_ref.shape[1:], jnp.float32) for _ in range(orders)]
    for i in range(LEVELS):
        part = parts_ref[i]
        for order in range(orders):
            sums[order] = sums[order] + level(i) ** order * part
    return sums


def ten(row0, row1, row2):
    return [
        row0(0), row0(1), row0(2), row1(0), row0(3), row0(4), row2(0), row0(5), row1(1), row1(2),
    ]


def fields_kernel(parts_ref, out_ref, pair_ref, row_ref, col_ref):
    sums = level_sums(parts_ref, 3)

    def rows(base):
        def of(a):
            def row(i):
                i = base + i
                return a[i % 4 : i % 4 + 1, i // 4 * LANES : (i // 4 + 1) * LANES] / TOTAL

            return row

        return [of(a) for a in sums]

    now = ten(*rows(0))
    moved = ten(*rows(6))
    density, mean, inverse, collide = coefficients(now)
    gauss = equilibrium_moments(mean, inverse, pair_ref, row_ref, col_ref)
    beta = time_step * collide * density * TOTAL / gauss[0]
    alpha = 1.0 - time_step * collide
    put_rows(out_ref, 0, mean, inverse, alpha, beta)
    later = [alpha * a + beta * (e / TOTAL) - time_step * b for a, e, b in zip(now, gauss, moved)]
    density, mean, inverse, collide = coefficients(later)
    total = equilibrium_total(mean, inverse, pair_ref, row_ref, col_ref)
    beta = time_step * collide * density * TOTAL / total
    put_rows(out_ref, 12, mean, inverse, 1.0 - time_step * collide, beta)


def relaxed_tile(value, flux, params_ref, base, tile, node_ref):
    rows = [params_ref[tile, base + i : base + i + 1, :] for i in range(12)]
    ixx, iyy, izz, ixy, ixz, iyz, lx, ly, lz, offset, alpha, beta = rows
    vz = node_ref[0, 2]
    x = node_x(VXY, LANES)
    parts = []
    for y in range(2):
        vy = node_ref[0, y]
        slope = ixy * vy + ixz * vz + lx
        rest = (iyy * vy + iyz * vz + ly) * vy + (izz * vz + lz) * vz + offset
        energy = jnp.exp(-0.5 * ((ixx * x + slope) * x + rest))
        at = slice(y * VXY, (y + 1) * VXY)
        parts.append(alpha * value[at, :] + beta * energy - time_step * flux[at, :])
    return jnp.concatenate(parts, axis=0)


def second_kernel(node_ref, block_ref, near_ref, flux_ref, params_ref, out_ref, sums_ref, value_ref, terms_ref):
    def first_step(g, carry):
        for half in range(2):
            at = slice(half * LANES, (half + 1) * LANES)
            value_ref[g, :, at] = relaxed_tile(
                block_ref[g, :NODES, at], flux_ref[g, :, at], params_ref, 0, half * GROUPS + g, node_ref
            )
        split_terms(value_ref, terms_ref, g)
        return carry

    lax.fori_loop(0, GROUPS, first_step, 0)

    def second_step(g, carry):
        flux = transport(value_ref, terms_ref, block_ref, near_ref[g], node_ref, g)
        for half in range(2):
            at = slice(half * LANES, (half + 1) * LANES)
            value = relaxed_tile(value_ref[g, :, at], flux[:, at], params_ref, 12, half * GROUPS + g, node_ref)
            out_ref[g, :, at] = value
            for i, row in enumerate(plane_sums(value, node_ref, True)):
                sums_ref[half * GROUPS + g, i : i + 1, :] = row
        return carry

    lax.fori_loop(0, GROUPS, second_step, 0)


def final_kernel(parts_ref, out_ref):
    def of(a):
        return lambda i: a[i : i + 1, :] / TOTAL

    row0, row1, row2, row3 = (of(a) for a in level_sums(parts_ref, 4))
    density, (ux, uy, uz), b, theta, _ = macroscopic(ten(row0, row1, row2))
    third = [row0(6) + row2(1), row0(7) + row2(2), row1(3) + row1(4) + row3(0)]
    trace = b[0] + b[1] + b[2]
    square = ux * ux + uy * uy + uz * uz
    stress = (
        b[0] * ux + b[3] * uy + b[4] * uz,
        b[3] * ux + b[1] * uy + b[5] * uz,
        b[4] * ux + b[5] * uy + b[2] * uz,
    )
    flux = [
        0.5 * (t / density - 2.0 * s - u * trace + 2.0 * u * square)
        for t, s, u in zip(third, stress, (ux, uy, uz))
    ]
    for i, value in enumerate((density, ux, uy, uz, *theta, *flux)):
        out_ref[i : i + 1, :] = value
    out_ref[13:16, :] = jnp.zeros((3, LANES), jnp.float32)


def shape(*dims, dtype=jnp.float32):
    return jax.ShapeDtypeStruct(dims, dtype)


VMEM = pl.BlockSpec(memory_space=pltpu.VMEM)
ANY = pl.BlockSpec(memory_space=pl.ANY)
SMEM = pl.BlockSpec(memory_space=pltpu.SMEM)
TERMS = pltpu.VMEM((GROUPS, 2 * NODES, CELLS), jnp.bfloat16)
TABLES = [pltpu.VMEM((VXY, VXY, LANES), jnp.float32)] * 3


def spread(x, axes, count):
    copies = jnp.broadcast_to(x, (count, *x.shape))
    return lax.all_to_all(copies, axes, 0, 0, tiled=True)


def per_device(distribution, normals, adjacency, send_list, block_counts):
    z, x, y, c = (lax.axis_index(a) for a in ("z", "x", "y", "c"))
    vel = (x * 8 + y) * 2 + c
    row = (vel * 16 + z * 2) & (VXY - 1)
    node = jnp.stack([row, row + 1, vel // 2, vel // 2]).astype(jnp.float32)
    node = ((node - (VXY - 1) / 2.0) * spacing).reshape(1, 4)

    block = pl.pallas_call(
        pack_kernel,
        out_shape=shape(GROUPS, ROWS, CELLS),
        in_specs=[ANY] * 5,
        out_specs=VMEM,
        scratch_shapes=[
            pltpu.VMEM((FACES, CELLS), jnp.int32),
            pltpu.VMEM((3, FACES, CELLS), jnp.float32),
            pltpu.VMEM((1, GROUPS, CELLS), jnp.int32),
            pltpu.VMEM((1, GROUPS), jnp.int32),
            pltpu.SemaphoreType.DMA((4,)),
            pltpu.SemaphoreType.DMA((GROUPS,)),
        ],
        compiler_params=pltpu.CompilerParams(vmem_limit_bytes=60 * 1024 * 1024),
    )(distribution, adjacency, jnp.transpose(normals, (1, 0, 2)), send_list, block_counts.reshape(1, GROUPS))
    block = lax.all_to_all(block, "z", 0, 0, tiled=True)

    near, flux, sums = pl.pallas_call(
        first_kernel,
        out_shape=(
            shape(GROUPS, FACES, CELLS, dtype=jnp.int32),
            shape(GROUPS, NODES, CELLS),
            shape(TILES, 4, 3 * LANES),
        ),
        in_specs=[SMEM, VMEM],
        out_specs=(VMEM, VMEM, VMEM),
        scratch_shapes=[TERMS],
        compiler_params=PARAMS,
    )(node, block)

    mine = jnp.sum(lax.all_to_all(sums, ("c", "z"), 0, 0, tiled=True), axis=0)
    params = pl.pallas_call(
        fields_kernel,
        out_shape=shape(24, LANES),
        in_specs=[VMEM],
        out_specs=VMEM,
        scratch_shapes=TABLES,
        compiler_params=PARAMS,
    )(spread(mine, ("x", "y"), LEVELS))
    params = spread(params, ("c", "z"), TILES)

    value, sums = pl.pallas_call(
        second_kernel,
        out_shape=(shape(GROUPS, NODES, CELLS), shape(TILES, 8, LANES)),
        in_specs=[SMEM, VMEM, VMEM, VMEM, VMEM],
        out_specs=(VMEM, VMEM),
        scratch_shapes=[pltpu.VMEM((GROUPS, NODES, CELLS), jnp.float32), TERMS],
        compiler_params=PARAMS,
    )(node, block, near, flux, params)

    relaxed = lax.all_to_all(value, "z", 0, 0, tiled=True).reshape(GROUPS * NODES, CELLS)
    mine = jnp.sum(lax.all_to_all(sums, ("c", "z"), 0, 0, tiled=True), axis=0)
    fields = pl.pallas_call(
        final_kernel,
        out_shape=shape(16, LANES),
        in_specs=[VMEM],
        out_specs=VMEM,
        compiler_params=PARAMS,
    )(spread(mine, ("x", "y"), LEVELS))
    other = lax.ppermute(fields, "c", [(0, 1), (1, 0)])
    fields = jnp.where(
        c == 0, jnp.concatenate([fields, other], axis=1), jnp.concatenate([other, fields], axis=1)
    )
    return relaxed, fields[:13]


def solution(mesh):
    split = Mesh(mesh.devices.reshape(8, 4, 8, 2), ("z", "x", "y", "c"))
    vel = ("x", "y", "c")
    placed = (P(vel, "z"), P(None, None, "z"), P(None, "z"), P("z", None, None), P(None, "z"))
    return jax.shard_map(
        per_device,
        mesh=split,
        in_specs=placed,
        out_specs=(P(vel, "z"), P(None, "z")),
        check_vma=False,
    )
```

```python
import jax
import jax.numpy as jnp
from jax import lax
from jax.experimental import pallas as pl
from jax.experimental.pallas import tpu as pltpu
from jax.sharding import Mesh, PartitionSpec as P

VXY = 32
TILE = 128
CELLS = 256
GROUPS = 8
NODES = 64
LANES = 128
TILES = 16
LEVELS = 32
FACES = 4
TOTAL = 32768

spacing = 0.3
ellipsoid_mix = -0.25
prandtl = 0.8
visc_power = 0.26
time_step = 0.025

ROW_ADJ = NODES
ROW_NORMAL = ROW_ADJ + FACES
ROW_SEND = ROW_NORMAL + 3 * FACES
ROWS = ROW_SEND + GROUPS

PARAMS = pltpu.CompilerParams(vmem_limit_bytes=48 * 1024 * 1024)


def level(i):
    return (i - (VXY - 1) / 2.0) * spacing


def take_lanes(values, lanes):
    return jnp.take_along_axis(values, lanes, axis=1, mode="promise_in_bounds")


def node_x(rows, lanes):
    row = lax.broadcasted_iota(jnp.int32, (rows, lanes), 0)
    return ((row & (VXY - 1)).astype(jnp.float32) - (VXY - 1) / 2.0) * spacing


def pack_kernel(
    value_hbm, adjacency_hbm, normal_hbm, send_hbm, count_hbm, out_ref,
    adjacency_ref, normal_ref, send_ref, count_ref, in_sem, value_sem,
):
    pairs = (
        (count_hbm, count_ref), (adjacency_hbm, adjacency_ref), (normal_hbm, normal_ref), (send_hbm, send_ref),
    )
    small = [pltpu.make_async_copy(a, b, in_sem.at[i]) for i, (a, b) in enumerate(pairs)]
    for copy in small:
        copy.start()
    large = [
        pltpu.make_async_copy(
            value_hbm.at[pl.ds(g * NODES, NODES), :], out_ref.at[g, pl.ds(0, NODES), :], value_sem.at[g]
        )
        for g in range(GROUPS)
    ]
    for copy in large:
        copy.start()
    for copy in small:
        copy.wait()
    adj = adjacency_ref[...]
    place = adj - CELLS
    counts = count_ref[...] * TILE
    end = jnp.zeros((1, 1), jnp.int32)
    source = jnp.zeros(adj.shape, jnp.int32)
    start = jnp.zeros(adj.shape, jnp.int32)
    for s in range(GROUPS - 1):
        end = end + counts[:, s : s + 1]
        past = end <= place
        source = source + jnp.where(past, 1, 0)
        start = jnp.where(past, end, start)
    slot = jnp.clip(place - start, 0, CELLS - 1)
    rows = [jnp.where(adj < CELLS, adj, CELLS + CELLS * source + slot).astype(jnp.float32)]
    rows += [normal_ref[d] for d in range(3)]
    rows = jnp.concatenate(rows + [send_ref[0].astype(jnp.float32)], axis=0)
    for g in range(GROUPS):
        out_ref[g, NODES:, :] = rows
    for copy in large:
        copy.wait()


def find_neighbours(block_ref, near_ref):
    base = CELLS * lax.broadcasted_iota(jnp.int32, (GROUPS, LANES), 0)
    for face in range(FACES):
        for half in range(2):
            at = slice(half * LANES, (half + 1) * LANES)
            adj = jnp.concatenate(
                [block_ref[g, ROW_ADJ + face : ROW_ADJ + face + 1, at] for g in range(GROUPS)], axis=0
            ).astype(jnp.int32)
            place = jnp.maximum(adj - CELLS, 0)
            table = place >> 7
            lane = place & (LANES - 1)
            listed = jnp.zeros(adj.shape, jnp.float32)
            for s in range(GROUPS):
                for part in range(2):
                    rows = block_ref[s, ROW_SEND : ROW_SEND + GROUPS, part * LANES : (part + 1) * LANES]
                    listed = jnp.where(table == s * 2 + part, take_lanes(rows, lane), listed)
            far = (place >> 8) * CELLS + listed.astype(jnp.int32)
            near = jnp.where(adj < CELLS, adj + base, far)
            for g in range(GROUPS):
                near_ref[g, face : face + 1, at] = near[g : g + 1, :]


def split_terms(value_ref, terms_ref, g):
    value = value_ref[g, :NODES, :]
    high = value.astype(jnp.bfloat16)
    terms_ref[g, :NODES, :] = high
    terms_ref[g, NODES:, :] = (value - high.astype(jnp.float32)).astype(jnp.bfloat16)


def look_up_lanes(value_ref, row):
    blocks = NODES // 8
    halves = []
    for half in range(2):
        near = jnp.broadcast_to(row[:, half * LANES : (half + 1) * LANES], (8, LANES))
        lane = near & (LANES - 1)
        tile = near >> 7
        found = [None] * blocks
        for t in range(TILES):
            hit = tile == t
            at = slice((t % 2) * LANES, (t % 2 + 1) * LANES)
            for b in range(blocks):
                got = take_lanes(value_ref[t // 2, b * 8 : b * 8 + 8, at], lane)
                found[b] = got if t == 0 else jnp.where(hit, got, found[b])
        halves.append(jnp.concatenate(found, axis=0))
    return jnp.concatenate(halves, axis=1)


def look_up(terms_ref, row):
    place = lax.broadcasted_iota(jnp.int32, (CELLS, CELLS), 0)
    chosen = jnp.where(place == (row & (CELLS - 1)), 1.0, 0.0).astype(jnp.bfloat16)
    group = row >> 8
    found = None
    for s in range(GROUPS):
        both = jnp.dot(terms_ref[s], chosen, preferred_element_type=jnp.float32)
        got = both[:NODES] + both[NODES:]
        found = got if s == 0 else jnp.where(group == s, got, found)
    return found


def transport(value_ref, terms_ref, normal_ref, near, node_ref, g):
    own = value_ref[g, :NODES, :]
    x = node_x(NODES, CELLS)
    second = lax.broadcasted_iota(jnp.int32, (NODES, CELLS), 0) >= VXY
    total = jnp.zeros((NODES, CELLS), jnp.float32)
    for face in range(FACES):
        row = near[face : face + 1, :]
        found = look_up(terms_ref, row) if face else look_up_lanes(value_ref, row)
        normal = [normal_ref[g, ROW_NORMAL + FACES * d + face : ROW_NORMAL + FACES * d + face + 1, :] for d in range(3)]
        fixed = [normal[1] * node_ref[0, y] + normal[2] * node_ref[0, 2] for y in range(2)]
        speed = normal[0] * x + jnp.where(second, fixed[1], fixed[0])
        total = total + speed * jnp.where(speed > 0.0, own, found)
    return total


def plane_sums(value, node_ref, third):
    x = node_x(VXY, value.shape[1])
    sums = []
    for y in range(2):
        part = value[y * VXY : (y + 1) * VXY, :]
        powers = [part]
        for _ in range(3 if third else 2):
            powers.append(x * powers[-1])
        sums.append([column_sum(p) for p in powers])
    low, high = sums
    ya, yb = node_ref[0, 0], node_ref[0, 1]

    def over(i, order=0):
        return ya**order * low[i] + yb**order * high[i] if order else low[i] + high[i]

    rows = [over(0), over(1), over(0, 1), over(2), over(0, 2), over(1, 1)]
    if third:
        rows += [over(3) + over(1, 2), over(2, 1) + over(0, 3)]
    return rows


def first_kernel(node_ref, block_ref, near_ref, flux_ref, sums_ref, terms_ref):
    find_neighbours(block_ref, near_ref)
    for g in range(GROUPS):
        split_terms(block_ref, terms_ref, g)

    def group(g, carry):
        flux = transport(block_ref, terms_ref, block_ref, near_ref[g], node_ref, g)
        flux_ref[g] = flux
        rows = plane_sums(block_ref[g, :NODES, :], node_ref, False) + plane_sums(flux, node_ref, False)
        for i, row in enumerate(rows):
            for half in range(2):
                q = i // 4
                sums_ref[half * GROUPS + g, i % 4 : i % 4 + 1, q * LANES : (q + 1) * LANES] = row[
                    :, half * LANES : (half + 1) * LANES
                ]
        return carry

    lax.fori_loop(0, GROUPS, group, 0)


def macroscopic(m):
    density = m[0]
    scale = 1.0 / density
    ux, uy, uz = m[1] * scale, m[2] * scale, m[3] * scale
    second = [m[4 + i] * scale for i in range(6)]
    txx = second[0] - ux * ux
    tyy = second[1] - uy * uy
    tzz = second[2] - uz * uz
    txy = second[3] - ux * uy
    txz = second[4] - ux * uz
    tyz = second[5] - uy * uz
    temper = (txx + tyy + tzz) / 3.0
    return density, (ux, uy, uz), second, (txx, tyy, tzz, txy, txz, tyz), temper


def coefficients(m):
    density, (ux, uy, uz), _, (txx, tyy, tzz, txy, txz, tyz), temper = macroscopic(m)
    iso = (1.0 - ellipsoid_mix) * temper
    lxx = iso + ellipsoid_mix * txx
    lyy = iso + ellipsoid_mix * tyy
    lzz = iso + ellipsoid_mix * tzz
    lxy = ellipsoid_mix * txy
    lxz = ellipsoid_mix * txz
    lyz = ellipsoid_mix * tyz
    cxx = lyy * lzz - lyz * lyz
    cxy = lyz * lxz - lxy * lzz
    cxz = lxy * lyz - lyy * lxz
    cyy = lxx * lzz - lxz * lxz
    cyz = lxy * lxz - lxx * lyz
    czz = lxx * lyy - lxy * lxy
    det = 1.0 / (lxx * cxx + lxy * cxy + lxz * cxz)
    inverse = (cxx * det, cyy * det, czz * det, cxy * det, cxz * det, cyz * det)
    collide = prandtl * density * jnp.exp(visc_power * jnp.log(temper))
    return density, (ux, uy, uz), inverse, collide


def factor_tables(mean, inverse, pair_ref, row_ref, col_ref):
    grid = level(lax.broadcasted_iota(jnp.int32, (VXY, LANES), 0).astype(jnp.float32))
    ixx, iyy, izz, ixy, ixz, iyz = inverse
    cx, cy, cz = grid - mean[0], grid - mean[1], grid - mean[2]
    own_x, own_y, own_z = -0.25 * ixx * cx * cx, -0.25 * iyy * cy * cy, -0.25 * izz * cz * cz
    cross_y = -ixy * cy
    cross_z = -ixz * cz
    cross_yz = -iyz * cy
    for i in range(VXY):
        x_own, x_c = own_x[i : i + 1, :], cx[i : i + 1, :]
        z_own, z_c = own_z[i : i + 1, :], cz[i : i + 1, :]
        pair_ref[i] = jnp.exp(x_own + own_y + x_c * cross_y)
        row_ref[i] = jnp.exp(x_own + own_z + x_c * cross_z)
        col_ref[i] = jnp.exp(z_own + own_y + z_c * cross_yz)


def column_sum(a):
    return jnp.sum(a, axis=0, keepdims=True)


def equilibrium_moments(mean, inverse, pair_ref, row_ref, col_ref):
    factor_tables(mean, inverse, pair_ref, row_ref, col_ref)
    zero = jnp.zeros((VXY, LANES), jnp.float32)

    def step(i, carry):
        s0, sx, sxx, s1, s1x, s2 = carry
        u0, u1, u2 = zero, zero, zero
        for k in range(VXY // 2):
            z = -level(k)
            low = row_ref[i, k : k + 1, :] * col_ref[k]
            high = row_ref[i, VXY - 1 - k : VXY - k, :] * col_ref[VXY - 1 - k]
            both = low + high
            u0 = u0 + both
            u1 = u1 + z * (high - low)
            u2 = u2 + (z * z) * both
        pair = pair_ref[i]
        x = level(lax.convert_element_type(i, jnp.float32))
        w0, w1 = pair * u0, pair * u1
        s0 = s0 + w0
        sx = sx + x * w0
        sxx = sxx + (x * x) * w0
        s1 = s1 + w1
        s1x = s1x + x * w1
        s2 = s2 + pair * u2
        return s0, sx, sxx, s1, s1x, s2

    s0, sx, sxx, s1, s1x, s2 = lax.fori_loop(0, VXY, step, (zero,) * 6)
    y = level(lax.broadcasted_iota(jnp.int32, (VXY, LANES), 0).astype(jnp.float32))
    return [
        column_sum(a)
        for a in (s0, sx, y * s0, s1, sxx, y * y * s0, s2, y * sx, s1x, y * s1)
    ]


def equilibrium_total(mean, inverse, pair_ref, row_ref, col_ref):
    factor_tables(mean, inverse, pair_ref, row_ref, col_ref)
    zero = jnp.zeros((VXY, LANES), jnp.float32)

    def step(i, total):
        u = zero
        for k in range(VXY):
            u = u + row_ref[i, k : k + 1, :] * col_ref[k]
        return total + pair_ref[i] * u

    return column_sum(lax.fori_loop(0, VXY, step, zero))


def put_rows(out_ref, base, mean, inverse, alpha, beta):
    ixx, iyy, izz, ixy, ixz, iyz = inverse
    lx = ixx * mean[0] + ixy * mean[1] + ixz * mean[2]
    ly = ixy * mean[0] + iyy * mean[1] + iyz * mean[2]
    lz = ixz * mean[0] + iyz * mean[1] + izz * mean[2]
    offset = mean[0] * lx + mean[1] * ly + mean[2] * lz
    rows = [ixx, iyy, izz, 2.0 * ixy, 2.0 * ixz, 2.0 * iyz, -2.0 * lx, -2.0 * ly, -2.0 * lz, offset, alpha, beta]
    for i, row in enumerate(rows):
        out_ref[base + i : base + i + 1, :] = row


def level_sums(parts_ref, orders):
    sums = [jnp.zeros(parts_ref.shape[1:], jnp.float32) for _ in range(orders)]
    for i in range(LEVELS):
        part = parts_ref[i]
        for order in range(orders):
            sums[order] = sums[order] + level(i) ** order * part
    return sums


def ten(row0, row1, row2):
    return [
        row0(0), row0(1), row0(2), row1(0), row0(3), row0(4), row2(0), row0(5), row1(1), row1(2),
    ]


def fields_kernel(parts_ref, out_ref, pair_ref, row_ref, col_ref):
    sums = level_sums(parts_ref, 3)

    def rows(base):
        def of(a):
            def row(i):
                i = base + i
                return a[i % 4 : i % 4 + 1, i // 4 * LANES : (i // 4 + 1) * LANES] / TOTAL

            return row

        return [of(a) for a in sums]

    now = ten(*rows(0))
    moved = ten(*rows(6))
    density, mean, inverse, collide = coefficients(now)
    gauss = equilibrium_moments(mean, inverse, pair_ref, row_ref, col_ref)
    beta = time_step * collide * density * TOTAL / gauss[0]
    alpha = 1.0 - time_step * collide
    put_rows(out_ref, 0, mean, inverse, alpha, beta)
    later = [alpha * a + beta * (e / TOTAL) - time_step * b for a, e, b in zip(now, gauss, moved)]
    density, mean, inverse, collide = coefficients(later)
    total = equilibrium_total(mean, inverse, pair_ref, row_ref, col_ref)
    beta = time_step * collide * density * TOTAL / total
    put_rows(out_ref, 12, mean, inverse, 1.0 - time_step * collide, beta)


def relaxed_tile(value, flux, params_ref, base, tile, node_ref):
    rows = [params_ref[tile, base + i : base + i + 1, :] for i in range(12)]
    ixx, iyy, izz, ixy, ixz, iyz, lx, ly, lz, offset, alpha, beta = rows
    vz = node_ref[0, 2]
    x = node_x(VXY, LANES)
    parts = []
    for y in range(2):
        vy = node_ref[0, y]
        slope = ixy * vy + ixz * vz + lx
        rest = (iyy * vy + iyz * vz + ly) * vy + (izz * vz + lz) * vz + offset
        energy = jnp.exp(-0.5 * ((ixx * x + slope) * x + rest))
        at = slice(y * VXY, (y + 1) * VXY)
        parts.append(alpha * value[at, :] + beta * energy - time_step * flux[at, :])
    return jnp.concatenate(parts, axis=0)


def second_kernel(node_ref, block_ref, near_ref, flux_ref, params_ref, out_ref, sums_ref, value_ref, terms_ref):
    def first_step(g, carry):
        for half in range(2):
            at = slice(half * LANES, (half + 1) * LANES)
            value_ref[g, :, at] = relaxed_tile(
                block_ref[g, :NODES, at], flux_ref[g, :, at], params_ref, 0, half * GROUPS + g, node_ref
            )
        split_terms(value_ref, terms_ref, g)
        return carry

    lax.fori_loop(0, GROUPS, first_step, 0)

    def second_step(g, carry):
        flux = transport(value_ref, terms_ref, block_ref, near_ref[g], node_ref, g)
        for half in range(2):
            at = slice(half * LANES, (half + 1) * LANES)
            value = relaxed_tile(value_ref[g, :, at], flux[:, at], params_ref, 12, half * GROUPS + g, node_ref)
            out_ref[g, :, at] = value
            for i, row in enumerate(plane_sums(value, node_ref, True)):
                sums_ref[half * GROUPS + g, i : i + 1, :] = row
        return carry

    lax.fori_loop(0, GROUPS, second_step, 0)


def partial_kernel(node_ref, parts_ref, out_ref):
    sums = [jnp.zeros((8, LANES), jnp.float32) for _ in range(4)]
    for i in range(parts_ref.shape[0]):
        part = parts_ref[i]
        z = node_ref[0, 3] + i * spacing
        for order in range(4):
            sums[order] = sums[order] + part
            part = z * part

    def of(a):
        return lambda i: a[i : i + 1, :] / TOTAL

    row0, row1, row2, row3 = (of(a) for a in sums)
    rows = ten(row0, row1, row2)
    rows += [row0(6) + row2(1), row0(7) + row2(2), row1(3) + row1(4) + row3(0)]
    for i, row in enumerate(rows):
        out_ref[i : i + 1, :] = row
    out_ref[13:16, :] = jnp.zeros((3, LANES), jnp.float32)


def final_kernel(moments_ref, out_ref):
    rows = [moments_ref[i : i + 1, :] for i in range(13)]
    density, (ux, uy, uz), b, theta, _ = macroscopic(rows[:10])
    third = rows[10:]
    trace = b[0] + b[1] + b[2]
    square = ux * ux + uy * uy + uz * uz
    stress = (
        b[0] * ux + b[3] * uy + b[4] * uz,
        b[3] * ux + b[1] * uy + b[5] * uz,
        b[4] * ux + b[5] * uy + b[2] * uz,
    )
    flux = [
        0.5 * (t / density - 2.0 * s - u * trace + 2.0 * u * square)
        for t, s, u in zip(third, stress, (ux, uy, uz))
    ]
    for i, value in enumerate((density, ux, uy, uz, *theta, *flux)):
        out_ref[i : i + 1, :] = value
    out_ref[13:16, :] = jnp.zeros((3, LANES), jnp.float32)


def shape(*dims, dtype=jnp.float32):
    return jax.ShapeDtypeStruct(dims, dtype)


VMEM = pl.BlockSpec(memory_space=pltpu.VMEM)
ANY = pl.BlockSpec(memory_space=pl.ANY)
SMEM = pl.BlockSpec(memory_space=pltpu.SMEM)
TERMS = pltpu.VMEM((GROUPS, 2 * NODES, CELLS), jnp.bfloat16)
TABLES = [pltpu.VMEM((VXY, VXY, LANES), jnp.float32)] * 3


def spread(x, axes, count):
    copies = jnp.broadcast_to(x, (count, *x.shape))
    return lax.all_to_all(copies, axes, 0, 0, tiled=True)


def per_device(distribution, normals, adjacency, send_list, block_counts):
    z, x, y, c = (lax.axis_index(a) for a in ("z", "x", "y", "c"))
    vel = (x * 8 + y) * 2 + c
    row = (vel * 16 + z * 2) & (VXY - 1)
    node = jnp.stack([row, row + 1, vel // 2, x * 8]).astype(jnp.float32)
    node = ((node - (VXY - 1) / 2.0) * spacing).reshape(1, 4)

    block = pl.pallas_call(
        pack_kernel,
        out_shape=shape(GROUPS, ROWS, CELLS),
        in_specs=[ANY] * 5,
        out_specs=VMEM,
        scratch_shapes=[
            pltpu.VMEM((FACES, CELLS), jnp.int32),
            pltpu.VMEM((3, FACES, CELLS), jnp.float32),
            pltpu.VMEM((1, GROUPS, CELLS), jnp.int32),
            pltpu.VMEM((1, GROUPS), jnp.int32),
            pltpu.SemaphoreType.DMA((4,)),
            pltpu.SemaphoreType.DMA((GROUPS,)),
        ],
        compiler_params=pltpu.CompilerParams(vmem_limit_bytes=60 * 1024 * 1024),
    )(distribution, adjacency, jnp.transpose(normals, (1, 0, 2)), send_list, block_counts.reshape(1, GROUPS))
    block = lax.all_to_all(block, "z", 0, 0, tiled=True)

    near, flux, sums = pl.pallas_call(
        first_kernel,
        out_shape=(
            shape(GROUPS, FACES, CELLS, dtype=jnp.int32),
            shape(GROUPS, NODES, CELLS),
            shape(TILES, 4, 3 * LANES),
        ),
        in_specs=[SMEM, VMEM],
        out_specs=(VMEM, VMEM, VMEM),
        scratch_shapes=[TERMS],
        compiler_params=PARAMS,
    )(node, block)

    mine = jnp.sum(lax.all_to_all(sums, ("c", "z"), 0, 0, tiled=True), axis=0)
    params = pl.pallas_call(
        fields_kernel,
        out_shape=shape(24, LANES),
        in_specs=[VMEM],
        out_specs=VMEM,
        scratch_shapes=TABLES,
        compiler_params=PARAMS,
    )(spread(mine, ("x", "y"), LEVELS))
    params = spread(params, ("c", "z"), TILES)

    value, sums = pl.pallas_call(
        second_kernel,
        out_shape=(shape(GROUPS, NODES, CELLS), shape(TILES, 8, LANES)),
        in_specs=[SMEM, VMEM, VMEM, VMEM, VMEM],
        out_specs=(VMEM, VMEM),
        scratch_shapes=[pltpu.VMEM((GROUPS, NODES, CELLS), jnp.float32), TERMS],
        compiler_params=PARAMS,
    )(node, block, near, flux, params)

    relaxed = lax.all_to_all(value, "z", 0, 0, tiled=True).reshape(GROUPS * NODES, CELLS)
    mine = jnp.sum(lax.all_to_all(sums, ("c", "z"), 0, 0, tiled=True), axis=0)
    moments = pl.pallas_call(
        partial_kernel,
        out_shape=shape(16, LANES),
        in_specs=[SMEM, VMEM],
        out_specs=VMEM,
        compiler_params=PARAMS,
    )(node, spread(mine, "y", 8))
    for step in (1, 2):
        moments = moments + lax.ppermute(moments, "x", [(i, i ^ step) for i in range(4)])
    fields = pl.pallas_call(
        final_kernel,
        out_shape=shape(16, LANES),
        in_specs=[VMEM],
        out_specs=VMEM,
        compiler_params=PARAMS,
    )(moments)
    other = lax.ppermute(fields, "c", [(0, 1), (1, 0)])
    fields = jnp.where(
        c == 0, jnp.concatenate([fields, other], axis=1), jnp.concatenate([other, fields], axis=1)
    )
    return relaxed, fields[:13]


def solution(mesh):
    split = Mesh(mesh.devices.reshape(8, 4, 8, 2), ("z", "x", "y", "c"))
    vel = ("x", "y", "c")
    placed = (P(vel, "z"), P(None, None, "z"), P(None, "z"), P("z", None, None), P(None, "z"))
    return jax.shard_map(
        per_device,
        mesh=split,
        in_specs=placed,
        out_specs=(P(vel, "z"), P(None, "z")),
        check_vma=False,
    )
```

```python
import jax
import jax.numpy as jnp
from jax import lax
from jax.experimental import pallas as pl
from jax.experimental.pallas import tpu as pltpu
from jax.sharding import Mesh, PartitionSpec as P

VXY = 32
TILE = 128
CELLS = 256
GROUPS = 8
NODES = 64
LANES = 128
TILES = 16
LEVELS = 32
FACES = 4
TOTAL = 32768

spacing = 0.3
ellipsoid_mix = -0.25
prandtl = 0.8
visc_power = 0.26
time_step = 0.025

ROW_ADJ = NODES
ROW_NORMAL = ROW_ADJ + FACES
ROW_SEND = ROW_NORMAL + 3 * FACES
ROWS = ROW_SEND + GROUPS

PARAMS = pltpu.CompilerParams(vmem_limit_bytes=48 * 1024 * 1024)


def level(i):
    return (i - (VXY - 1) / 2.0) * spacing


def take_lanes(values, lanes):
    return jnp.take_along_axis(values, lanes, axis=1, mode="promise_in_bounds")


def node_x(rows, lanes):
    row = lax.broadcasted_iota(jnp.int32, (rows, lanes), 0)
    return ((row & (VXY - 1)).astype(jnp.float32) - (VXY - 1) / 2.0) * spacing


def pack_kernel(
    value_hbm, adjacency_hbm, normal_hbm, send_hbm, count_hbm, out_ref,
    adjacency_ref, normal_ref, send_ref, count_ref, in_sem, value_sem,
):
    pairs = (
        (count_hbm, count_ref), (adjacency_hbm, adjacency_ref), (normal_hbm, normal_ref), (send_hbm, send_ref),
    )
    small = [pltpu.make_async_copy(a, b, in_sem.at[i]) for i, (a, b) in enumerate(pairs)]
    for copy in small:
        copy.start()
    large = [
        pltpu.make_async_copy(
            value_hbm.at[pl.ds(g * NODES, NODES), :], out_ref.at[g, pl.ds(0, NODES), :], value_sem.at[g]
        )
        for g in range(GROUPS)
    ]
    for copy in large:
        copy.start()
    for copy in small:
        copy.wait()
    adj = adjacency_ref[...]
    place = adj - CELLS
    counts = count_ref[...] * TILE
    end = jnp.zeros((1, 1), jnp.int32)
    source = jnp.zeros(adj.shape, jnp.int32)
    start = jnp.zeros(adj.shape, jnp.int32)
    for s in range(GROUPS - 1):
        end = end + counts[:, s : s + 1]
        past = end <= place
        source = source + jnp.where(past, 1, 0)
        start = jnp.where(past, end, start)
    slot = jnp.clip(place - start, 0, CELLS - 1)
    rows = [jnp.where(adj < CELLS, adj, CELLS + CELLS * source + slot).astype(jnp.float32)]
    rows += [normal_ref[d] for d in range(3)]
    rows = jnp.concatenate(rows + [send_ref[0].astype(jnp.float32)], axis=0)
    for g in range(GROUPS):
        out_ref[g, NODES:, :] = rows
    for copy in large:
        copy.wait()


def find_neighbours(block_ref, near_ref):
    base = CELLS * lax.broadcasted_iota(jnp.int32, (GROUPS, LANES), 0)
    for face in range(FACES):
        for half in range(2):
            at = slice(half * LANES, (half + 1) * LANES)
            adj = jnp.concatenate(
                [block_ref[g, ROW_ADJ + face : ROW_ADJ + face + 1, at] for g in range(GROUPS)], axis=0
            ).astype(jnp.int32)
            place = jnp.maximum(adj - CELLS, 0)
            table = place >> 7
            lane = place & (LANES - 1)
            listed = jnp.zeros(adj.shape, jnp.float32)
            for s in range(GROUPS):
                for part in range(2):
                    rows = block_ref[s, ROW_SEND : ROW_SEND + GROUPS, part * LANES : (part + 1) * LANES]
                    listed = jnp.where(table == s * 2 + part, take_lanes(rows, lane), listed)
            far = (place >> 8) * CELLS + listed.astype(jnp.int32)
            near = jnp.where(adj < CELLS, adj + base, far)
            for g in range(GROUPS):
                near_ref[g, face : face + 1, at] = near[g : g + 1, :]


def split_terms(value_ref, terms_ref, g):
    value = value_ref[g, :NODES, :]
    high = value.astype(jnp.bfloat16)
    terms_ref[g, :NODES, :] = high
    terms_ref[g, NODES:, :] = (value - high.astype(jnp.float32)).astype(jnp.bfloat16)


def look_up_lanes(value_ref, row):
    blocks = NODES // 8
    halves = []
    for half in range(2):
        near = jnp.broadcast_to(row[:, half * LANES : (half + 1) * LANES], (8, LANES))
        lane = near & (LANES - 1)
        tile = near >> 7
        found = [None] * blocks
        for t in range(TILES):
            hit = tile == t
            at = slice((t % 2) * LANES, (t % 2 + 1) * LANES)
            for b in range(blocks):
                got = take_lanes(value_ref[t // 2, b * 8 : b * 8 + 8, at], lane)
                found[b] = got if t == 0 else jnp.where(hit, got, found[b])
        halves.append(jnp.concatenate(found, axis=0))
    return jnp.concatenate(halves, axis=1)


def look_up(terms_ref, row):
    place = lax.broadcasted_iota(jnp.int32, (CELLS, CELLS), 0)
    chosen = jnp.where(place == (row & (CELLS - 1)), 1.0, 0.0).astype(jnp.bfloat16)
    group = row >> 8
    found = None
    for s in range(GROUPS):
        both = jnp.dot(terms_ref[s], chosen, preferred_element_type=jnp.float32)
        got = both[:NODES] + both[NODES:]
        found = got if s == 0 else jnp.where(group == s, got, found)
    return found


def transport(value_ref, terms_ref, normal_ref, near, node_ref, g):
    own = value_ref[g, :NODES, :]
    x = node_x(NODES, CELLS)
    second = lax.broadcasted_iota(jnp.int32, (NODES, CELLS), 0) >= VXY
    total = jnp.zeros((NODES, CELLS), jnp.float32)
    for face in range(FACES):
        row = near[face : face + 1, :]
        found = look_up(terms_ref, row) if face else look_up_lanes(value_ref, row)
        normal = [normal_ref[g, ROW_NORMAL + FACES * d + face : ROW_NORMAL + FACES * d + face + 1, :] for d in range(3)]
        fixed = [normal[1] * node_ref[0, y] + normal[2] * node_ref[0, 2] for y in range(2)]
        speed = normal[0] * x + jnp.where(second, fixed[1], fixed[0])
        total = total + speed * jnp.where(speed > 0.0, own, found)
    return total


def plane_sums(value, node_ref, third):
    x = node_x(VXY, value.shape[1])
    sums = []
    for y in range(2):
        part = value[y * VXY : (y + 1) * VXY, :]
        powers = [part]
        for _ in range(3 if third else 2):
            powers.append(x * powers[-1])
        sums.append([column_sum(p) for p in powers])
    low, high = sums
    ya, yb = node_ref[0, 0], node_ref[0, 1]

    def over(i, order=0):
        return ya**order * low[i] + yb**order * high[i] if order else low[i] + high[i]

    rows = [over(0), over(1), over(0, 1), over(2), over(0, 2), over(1, 1)]
    if third:
        rows += [over(3) + over(1, 2), over(2, 1) + over(0, 3)]
    return rows


def first_kernel(node_ref, block_ref, near_ref, flux_ref, sums_ref, terms_ref):
    find_neighbours(block_ref, near_ref)
    for g in range(GROUPS):
        split_terms(block_ref, terms_ref, g)

    def group(g, carry):
        flux = transport(block_ref, terms_ref, block_ref, near_ref[g], node_ref, g)
        flux_ref[g] = flux
        rows = plane_sums(block_ref[g, :NODES, :], node_ref, False) + plane_sums(flux, node_ref, False)
        for i, row in enumerate(rows):
            for half in range(2):
                q = i // 4
                sums_ref[half * GROUPS + g, i % 4 : i % 4 + 1, q * LANES : (q + 1) * LANES] = row[
                    :, half * LANES : (half + 1) * LANES
                ]
        return carry

    lax.fori_loop(0, GROUPS, group, 0)


def macroscopic(m):
    density = m[0]
    scale = 1.0 / density
    ux, uy, uz = m[1] * scale, m[2] * scale, m[3] * scale
    second = [m[4 + i] * scale for i in range(6)]
    txx = second[0] - ux * ux
    tyy = second[1] - uy * uy
    tzz = second[2] - uz * uz
    txy = second[3] - ux * uy
    txz = second[4] - ux * uz
    tyz = second[5] - uy * uz
    temper = (txx + tyy + tzz) / 3.0
    return density, (ux, uy, uz), second, (txx, tyy, tzz, txy, txz, tyz), temper


def coefficients(m):
    density, (ux, uy, uz), _, (txx, tyy, tzz, txy, txz, tyz), temper = macroscopic(m)
    iso = (1.0 - ellipsoid_mix) * temper
    lxx = iso + ellipsoid_mix * txx
    lyy = iso + ellipsoid_mix * tyy
    lzz = iso + ellipsoid_mix * tzz
    lxy = ellipsoid_mix * txy
    lxz = ellipsoid_mix * txz
    lyz = ellipsoid_mix * tyz
    cxx = lyy * lzz - lyz * lyz
    cxy = lyz * lxz - lxy * lzz
    cxz = lxy * lyz - lyy * lxz
    cyy = lxx * lzz - lxz * lxz
    cyz = lxy * lxz - lxx * lyz
    czz = lxx * lyy - lxy * lxy
    det = 1.0 / (lxx * cxx + lxy * cxy + lxz * cxz)
    inverse = (cxx * det, cyy * det, czz * det, cxy * det, cxz * det, cyz * det)
    collide = prandtl * density * jnp.exp(visc_power * jnp.log(temper))
    return density, (ux, uy, uz), inverse, collide


def factor_tables(mean, inverse, pair_ref, row_ref, col_ref):
    grid = level(lax.broadcasted_iota(jnp.int32, (VXY, LANES), 0).astype(jnp.float32))
    ixx, iyy, izz, ixy, ixz, iyz = inverse
    cx, cy, cz = grid - mean[0], grid - mean[1], grid - mean[2]
    own_x, own_y, own_z = -0.25 * ixx * cx * cx, -0.25 * iyy * cy * cy, -0.25 * izz * cz * cz
    cross_y = -ixy * cy
    cross_z = -ixz * cz
    cross_yz = -iyz * cy
    for i in range(VXY):
        x_own, x_c = own_x[i : i + 1, :], cx[i : i + 1, :]
        z_own, z_c = own_z[i : i + 1, :], cz[i : i + 1, :]
        pair_ref[i] = jnp.exp(x_own + own_y + x_c * cross_y)
        row_ref[i] = jnp.exp(x_own + own_z + x_c * cross_z)
        col_ref[i] = jnp.exp(z_own + own_y + z_c * cross_yz)


def column_sum(a):
    return jnp.sum(a, axis=0, keepdims=True)


def equilibrium_moments(mean, inverse, pair_ref, row_ref, col_ref):
    factor_tables(mean, inverse, pair_ref, row_ref, col_ref)
    zero = jnp.zeros((VXY, LANES), jnp.float32)

    def step(i, carry):
        s0, sx, sxx, s1, s1x, s2 = carry
        u0, u1, u2 = zero, zero, zero
        for k in range(VXY // 2):
            z = -level(k)
            low = row_ref[i, k : k + 1, :] * col_ref[k]
            high = row_ref[i, VXY - 1 - k : VXY - k, :] * col_ref[VXY - 1 - k]
            both = low + high
            u0 = u0 + both
            u1 = u1 + z * (high - low)
            u2 = u2 + (z * z) * both
        pair = pair_ref[i]
        x = level(lax.convert_element_type(i, jnp.float32))
        w0, w1 = pair * u0, pair * u1
        s0 = s0 + w0
        sx = sx + x * w0
        sxx = sxx + (x * x) * w0
        s1 = s1 + w1
        s1x = s1x + x * w1
        s2 = s2 + pair * u2
        return s0, sx, sxx, s1, s1x, s2

    s0, sx, sxx, s1, s1x, s2 = lax.fori_loop(0, VXY, step, (zero,) * 6)
    y = level(lax.broadcasted_iota(jnp.int32, (VXY, LANES), 0).astype(jnp.float32))
    return [
        column_sum(a)
        for a in (s0, sx, y * s0, s1, sxx, y * y * s0, s2, y * sx, s1x, y * s1)
    ]


def equilibrium_total(mean, inverse, pair_ref, row_ref, col_ref):
    factor_tables(mean, inverse, pair_ref, row_ref, col_ref)
    zero = jnp.zeros((VXY, LANES), jnp.float32)

    def step(i, total):
        u = zero
        for k in range(VXY):
            u = u + row_ref[i, k : k + 1, :] * col_ref[k]
        return total + pair_ref[i] * u

    return column_sum(lax.fori_loop(0, VXY, step, zero))


def put_rows(out_ref, base, mean, inverse, alpha, beta):
    ixx, iyy, izz, ixy, ixz, iyz = inverse
    lx = ixx * mean[0] + ixy * mean[1] + ixz * mean[2]
    ly = ixy * mean[0] + iyy * mean[1] + iyz * mean[2]
    lz = ixz * mean[0] + iyz * mean[1] + izz * mean[2]
    offset = mean[0] * lx + mean[1] * ly + mean[2] * lz
    rows = [ixx, iyy, izz, 2.0 * ixy, 2.0 * ixz, 2.0 * iyz, -2.0 * lx, -2.0 * ly, -2.0 * lz, offset, alpha, beta]
    for i, row in enumerate(rows):
        out_ref[base + i : base + i + 1, :] = row


def level_sums(parts_ref, orders):
    sums = [jnp.zeros(parts_ref.shape[1:], jnp.float32) for _ in range(orders)]
    for i in range(LEVELS):
        part = parts_ref[i]
        for order in range(orders):
            sums[order] = sums[order] + level(i) ** order * part
    return sums


def ten(row0, row1, row2):
    return [
        row0(0), row0(1), row0(2), row1(0), row0(3), row0(4), row2(0), row0(5), row1(1), row1(2),
    ]


def fields_kernel(parts_ref, out_ref, pair_ref, row_ref, col_ref):
    sums = level_sums(parts_ref, 3)

    def rows(base):
        def of(a):
            def row(i):
                i = base + i
                return a[i % 4 : i % 4 + 1, i // 4 * LANES : (i // 4 + 1) * LANES] / TOTAL

            return row

        return [of(a) for a in sums]

    now = ten(*rows(0))
    moved = ten(*rows(6))
    density, mean, inverse, collide = coefficients(now)
    gauss = equilibrium_moments(mean, inverse, pair_ref, row_ref, col_ref)
    beta = time_step * collide * density * TOTAL / gauss[0]
    alpha = 1.0 - time_step * collide
    put_rows(out_ref, 0, mean, inverse, alpha, beta)
    later = [alpha * a + beta * (e / TOTAL) - time_step * b for a, e, b in zip(now, gauss, moved)]
    density, mean, inverse, collide = coefficients(later)
    total = equilibrium_total(mean, inverse, pair_ref, row_ref, col_ref)
    beta = time_step * collide * density * TOTAL / total
    put_rows(out_ref, 12, mean, inverse, 1.0 - time_step * collide, beta)


def relaxed_tile(value, flux, params_ref, base, tile, node_ref):
    rows = [params_ref[tile, base + i : base + i + 1, :] for i in range(12)]
    ixx, iyy, izz, ixy, ixz, iyz, lx, ly, lz, offset, alpha, beta = rows
    vz = node_ref[0, 2]
    x = node_x(VXY, LANES)
    parts = []
    for y in range(2):
        vy = node_ref[0, y]
        slope = ixy * vy + ixz * vz + lx
        rest = (iyy * vy + iyz * vz + ly) * vy + (izz * vz + lz) * vz + offset
        energy = jnp.exp(-0.5 * ((ixx * x + slope) * x + rest))
        at = slice(y * VXY, (y + 1) * VXY)
        parts.append(alpha * value[at, :] + beta * energy - time_step * flux[at, :])
    return jnp.concatenate(parts, axis=0)


def second_kernel(node_ref, block_ref, near_ref, flux_ref, params_ref, out_ref, sums_ref, value_ref, terms_ref):
    def first_step(g, carry):
        for half in range(2):
            at = slice(half * LANES, (half + 1) * LANES)
            value_ref[g, :, at] = relaxed_tile(
                block_ref[g, :NODES, at], flux_ref[g, :, at], params_ref, 0, half * GROUPS + g, node_ref
            )
        split_terms(value_ref, terms_ref, g)
        return carry

    lax.fori_loop(0, GROUPS, first_step, 0)

    def second_step(g, carry):
        flux = transport(value_ref, terms_ref, block_ref, near_ref[g], node_ref, g)
        for half in range(2):
            at = slice(half * LANES, (half + 1) * LANES)
            value = relaxed_tile(value_ref[g, :, at], flux[:, at], params_ref, 12, half * GROUPS + g, node_ref)
            out_ref[g, :, at] = value
            for i, row in enumerate(plane_sums(value, node_ref, True)):
                sums_ref[half * GROUPS + g, i : i + 1, :] = row
        return carry

    lax.fori_loop(0, GROUPS, second_step, 0)


def partial_kernel(node_ref, parts_ref, out_ref):
    sums = [jnp.zeros((8, LANES), jnp.float32) for _ in range(4)]
    for i in range(parts_ref.shape[0]):
        part = parts_ref[i]
        z = node_ref[0, 3] + (i // 8 * 16 + i % 8) * spacing
        for order in range(4):
            sums[order] = sums[order] + part
            part = z * part

    def of(a):
        return lambda i: a[i : i + 1, :] / TOTAL

    row0, row1, row2, row3 = (of(a) for a in sums)
    rows = ten(row0, row1, row2)
    rows += [row0(6) + row2(1), row0(7) + row2(2), row1(3) + row1(4) + row3(0)]
    for i, row in enumerate(rows):
        out_ref[i : i + 1, :] = row
    out_ref[13:16, :] = jnp.zeros((3, LANES), jnp.float32)


def final_kernel(moments_ref, out_ref):
    rows = [moments_ref[i : i + 1, :] for i in range(13)]
    density, (ux, uy, uz), b, theta, _ = macroscopic(rows[:10])
    third = rows[10:]
    trace = b[0] + b[1] + b[2]
    square = ux * ux + uy * uy + uz * uz
    stress = (
        b[0] * ux + b[3] * uy + b[4] * uz,
        b[3] * ux + b[1] * uy + b[5] * uz,
        b[4] * ux + b[5] * uy + b[2] * uz,
    )
    flux = [
        0.5 * (t / density - 2.0 * s - u * trace + 2.0 * u * square)
        for t, s, u in zip(third, stress, (ux, uy, uz))
    ]
    for i, value in enumerate((density, ux, uy, uz, *theta, *flux)):
        out_ref[i : i + 1, :] = value
    out_ref[13:16, :] = jnp.zeros((3, LANES), jnp.float32)


def shape(*dims, dtype=jnp.float32):
    return jax.ShapeDtypeStruct(dims, dtype)


VMEM = pl.BlockSpec(memory_space=pltpu.VMEM)
ANY = pl.BlockSpec(memory_space=pl.ANY)
SMEM = pl.BlockSpec(memory_space=pltpu.SMEM)
TERMS = pltpu.VMEM((GROUPS, 2 * NODES, CELLS), jnp.bfloat16)
TABLES = [pltpu.VMEM((VXY, VXY, LANES), jnp.float32)] * 3


def spread(x, axes, count):
    copies = jnp.broadcast_to(x, (count, *x.shape))
    return lax.all_to_all(copies, axes, 0, 0, tiled=True)


def per_device(distribution, normals, adjacency, send_list, block_counts):
    z, x, w, y, c = (lax.axis_index(a) for a in ("z", "x", "w", "y", "c"))
    vel = ((x * 2 + w) * 8 + y) * 2 + c
    row = (vel * 16 + z * 2) & (VXY - 1)
    node = jnp.stack([row, row + 1, vel // 2, w * 8]).astype(jnp.float32)
    node = ((node - (VXY - 1) / 2.0) * spacing).reshape(1, 4)

    block = pl.pallas_call(
        pack_kernel,
        out_shape=shape(GROUPS, ROWS, CELLS),
        in_specs=[ANY] * 5,
        out_specs=VMEM,
        scratch_shapes=[
            pltpu.VMEM((FACES, CELLS), jnp.int32),
            pltpu.VMEM((3, FACES, CELLS), jnp.float32),
            pltpu.VMEM((1, GROUPS, CELLS), jnp.int32),
            pltpu.VMEM((1, GROUPS), jnp.int32),
            pltpu.SemaphoreType.DMA((4,)),
            pltpu.SemaphoreType.DMA((GROUPS,)),
        ],
        compiler_params=pltpu.CompilerParams(vmem_limit_bytes=60 * 1024 * 1024),
    )(distribution, adjacency, jnp.transpose(normals, (1, 0, 2)), send_list, block_counts.reshape(1, GROUPS))
    block = lax.all_to_all(block, "z", 0, 0, tiled=True)

    near, flux, sums = pl.pallas_call(
        first_kernel,
        out_shape=(
            shape(GROUPS, FACES, CELLS, dtype=jnp.int32),
            shape(GROUPS, NODES, CELLS),
            shape(TILES, 4, 3 * LANES),
        ),
        in_specs=[SMEM, VMEM],
        out_specs=(VMEM, VMEM, VMEM),
        scratch_shapes=[TERMS],
        compiler_params=PARAMS,
    )(node, block)

    mine = jnp.sum(lax.all_to_all(sums, ("c", "z"), 0, 0, tiled=True), axis=0)
    params = pl.pallas_call(
        fields_kernel,
        out_shape=shape(24, LANES),
        in_specs=[VMEM],
        out_specs=VMEM,
        scratch_shapes=TABLES,
        compiler_params=PARAMS,
    )(spread(mine, ("x", "w", "y"), LEVELS))
    params = spread(params, ("c", "z"), TILES)

    value, sums = pl.pallas_call(
        second_kernel,
        out_shape=(shape(GROUPS, NODES, CELLS), shape(TILES, 8, LANES)),
        in_specs=[SMEM, VMEM, VMEM, VMEM, VMEM],
        out_specs=(VMEM, VMEM),
        scratch_shapes=[pltpu.VMEM((GROUPS, NODES, CELLS), jnp.float32), TERMS],
        compiler_params=PARAMS,
    )(node, block, near, flux, params)

    relaxed = lax.all_to_all(value, "z", 0, 0, tiled=True).reshape(GROUPS * NODES, CELLS)
    mine = jnp.sum(lax.all_to_all(sums, ("c", "z"), 0, 0, tiled=True), axis=0)
    moments = pl.pallas_call(
        partial_kernel,
        out_shape=shape(16, LANES),
        in_specs=[SMEM, VMEM],
        out_specs=VMEM,
        compiler_params=PARAMS,
    )(node, spread(mine, ("x", "y"), 16))
    moments = moments + lax.ppermute(moments, "w", [(0, 1), (1, 0)])
    fields = pl.pallas_call(
        final_kernel,
        out_shape=shape(16, LANES),
        in_specs=[VMEM],
        out_specs=VMEM,
        compiler_params=PARAMS,
    )(moments)
    other = lax.ppermute(fields, "c", [(0, 1), (1, 0)])
    fields = jnp.where(
        c == 0, jnp.concatenate([fields, other], axis=1), jnp.concatenate([other, fields], axis=1)
    )
    return relaxed, fields[:13]


def solution(mesh):
    split = Mesh(mesh.devices.reshape(8, 2, 2, 8, 2), ("z", "x", "w", "y", "c"))
    vel = ("x", "w", "y", "c")
    placed = (P(vel, "z"), P(None, None, "z"), P(None, "z"), P("z", None, None), P(None, "z"))
    return jax.shard_map(
        per_device,
        mesh=split,
        in_specs=placed,
        out_specs=(P(vel, "z"), P(None, "z")),
        check_vma=False,
    )
```
